32 devices in a mesh: rows: 8 (over z, y), hid: 4 (over x, core).
Axes of the slice: x: 2, y: 2, z: 4, core: 2. Of those that a mesh axis runs over, the one named last changes fastest.
Arguments:
- tokens: bfloat16 [768, 4096], P('hid', 'rows'), may hold values from -6 to 6
- w_qkv: bfloat16 [3, 768, 768], P(None, 'hid'), may hold values from -0.3125 to 0.3125
- b_qv: float32 [2, 768], P(None, 'hid'), may hold values from -3 to 3
- w_out: bfloat16 [768, 768], P('hid'), may hold values from -1.25 to 1.25
- b_out: float32 [768], P('hid'), may hold values from -2 to 2
- w_in: bfloat16 [768, 3072], P(None, 'hid'), may hold values from -0.21875 to 0.21875
- b_in: float32 [3072], P('hid'), may hold values from -2 to 2
- w_back: bfloat16 [768, 3072], P('hid'), may hold values from -0.15625 to 0.15625
- b_back: float32 [768], P('hid'), may hold values from -2 to 2
- norm_gain: float32 [2, 768], P(None, 'hid'), may hold values from 0.5 to 1.5
- norm_bias: float32 [2, 768], P(None, 'hid'), may hold values from -2 to 2
- head_gate: float32 [12], P('hid'), may hold values from 0.3 to 1
- inter_gate: float32 [3072], P('hid'), may hold values from 0.3 to 1
- branch_gate: float32 [2], replicated, may hold values from 0.6 to 1.4
- hidden_gate: float32 [768], P('hid'), may hold values from 0.5 to 1.2
- hidden_mask: int32 [768], P('hid'), may hold values 0 or 1
- doc_lengths: int32 [8, 4], P('rows'), may hold values from 1 to 256, 512 in all within a row
- cotangent: bfloat16 [768, 4096], P('hid', 'rows'), may hold values from -6 to 6
Outputs:
- output: bfloat16 [768, 4096], P('hid', 'rows')
- grad_tokens: bfloat16 [768, 4096], P('hid', 'rows')
- grad_w_qkv: float32 [3, 768, 768], P(None, 'hid')
- grad_b_qv: float32 [2, 768], P(None, 'hid')
- grad_w_out: float32 [768, 768], P('hid')
- grad_b_out: float32 [768], P('hid')
- grad_w_in: float32 [768, 3072], P(None, 'hid')
- grad_b_in: float32 [3072], P('hid')
- grad_w_back: float32 [768, 3072], P('hid')
- grad_b_back: float32 [768], P('hid')
- grad_norm_gain: float32 [2, 768], P(None, 'hid')
- grad_norm_bias: float32 [2, 768], P(None, 'hid')
- grad_head_gate: float32 [12], P('hid')
- grad_inter_gate: float32 [3072], P('hid')
- grad_branch_gate: float32 [2], replicated
- grad_hidden_gate: float32 [768], P('hid')
The draws below stay inside these ranges and needn't reach their ends.
Inputs may be any that keep to these rules, and one draw needn't show every extreme that they name: `doc_lengths`: in each packed row the 4 lengths add up to 512.
All inputs are finite; a program needn't handle non-finite values. No bound on the sum of `hidden_mask` on one device may be relied on, other than what follows from the above.
Results may differ from the reference program's by a relative error of at most 0.0128.
The reference program's roundings to bfloat16 on the way count: a program that leaves them out, or rounds other values in their place, can miss the bound.
Values may be sent and summed in bfloat16 or wider, within the bound.
No kernel may reach another device: no remote copies, remote signals or barrier semaphores. Data moves between devices by JAX's collectives and lax.ppermute only.
A program may use at most 64 MiB of HBM per device.

```python
import math
import jax
import jax.numpy as jnp
import numpy as np
from jax import lax

D = 768
HEADS = 12
HEAD_DIM = 64
FF = 3072
LEN = 512
DOCS = 4
ROWS = 8
TOKENS = 4096


def place_ends(array, stream_key, least, high):
    longest = array.shape.index(max(array.shape))
    spots = []
    for shift in (0, 1):
        where = [jax.random.randint(jax.random.fold_in(stream_key, axis), (), 0, length) for axis, length in enumerate(array.shape)]
        where[longest] = (where[longest] + shift) % array.shape[longest]
        spots.append(tuple(where))
    return array.at[spots[0]].set(least).at[spots[1]].set(high)


def levels(rng, shape, shards, smallest, high):
    factor_of, own = 1.0, jax.random.fold_in(rng, 6)
    for dim, shards_of in shards:
        heights = jnp.exp(jax.random.uniform(jax.random.fold_in(own, dim), (shards_of,), jnp.float32, smallest / len(shards), high / len(shards)))
        factor_of = factor_of * jnp.repeat(heights, shape[dim] // shards_of).reshape([-1 if axis == dim else 1 for axis in range(len(shape))])
    return factor_of


def length_profile(number_of, total, most, slope):
    portions = [(1 << 20) // math.isqrt(grade ** slope) + 1 for grade in range(2, number_of + 1)]
    rest, given = total - most - (number_of - 1), [1] * (number_of - 1)
    while rest > 0:
        movable = [i for i in range(number_of - 1) if given[i] < most]
        pool, remaining = sum([portions[i] for i in movable]), rest
        for i in movable:
            extra = min(most - given[i], max(1, remaining * portions[i] // pool), rest)
            given[i] = given[i] + extra
            rest = rest - extra
    return np.array([most] + given)


def uneven_parts(key, number_of, total, limit, lean):
    if number_of == 2:
        one = jax.random.randint(key, (), max(1, total - limit), min(limit, total - 1) + 1)
        return jnp.stack([one, total - one])
    tallies = jnp.asarray(length_profile(number_of, total, limit, lean), jnp.int32)
    couples = (number_of - 1) // 2
    source_of, taker = tallies[1:1 + 2 * couples:2], tallies[2:2 + 2 * couples:2]
    slack = jnp.minimum(source_of - 1, limit - taker)
    shifted = jax.random.randint(jax.random.fold_in(key, 1), (couples,), 0, 1 << 20) % (slack + 1)
    tallies = tallies.at[1:1 + 2 * couples:2].set(source_of - shifted).at[2:2 + 2 * couples:2].set(taker + shifted)
    return tallies[jax.random.permutation(jax.random.fold_in(key, 2), number_of)]


def bell_draw(own_key, extent, deviation, limit, pieces=(), kind=jnp.bfloat16):
    values = deviation * jax.random.normal(own_key, extent, jnp.float32)
    if pieces:
        values = values * levels(own_key, extent, pieces, -0.22, 0.18)
    return jnp.clip(values, -limit, limit).astype(kind)


def setup_inputs(seed: int = 0) -> dict:
    keys = jax.random.split(jax.random.key(seed), 19)
    tokens = bell_draw(keys[0], (D, TOKENS), 1.0, 6.0, ((0, 4), (1, 8)))
    w_qkv = bell_draw(keys[1], (3, D, D), (D // 2) ** -0.5, 0.3125, ((1, 4),))
    b_qv = bell_draw(keys[2], (2, D), 0.5, 3.0, ((1, 4),), jnp.float32)
    w_out = bell_draw(keys[3], (D, D), (D // 32) ** -0.5, 1.25, ((0, 4),))
    b_out = bell_draw(keys[4], (D,), 0.3, 2.0, ((0, 4),), jnp.float32)
    w_in = bell_draw(keys[5], (D, FF), D ** -0.5, 0.21875, ((1, 4),))
    b_in = bell_draw(keys[6], (FF,), 0.3, 2.0, ((0, 4),), jnp.float32)
    w_back = bell_draw(keys[7], (D, FF), (FF // 2) ** -0.5, 0.15625, ((0, 4),))
    b_back = bell_draw(keys[8], (D,), 0.3, 2.0, ((0, 4),), jnp.float32)
    norm_gain = jnp.clip(1.0 + 0.1 * jax.random.normal(keys[9], (2, D), jnp.float32), 0.5, 1.5)
    norm_bias = bell_draw(keys[10], (2, D), 0.3, 2.0, ((1, 4),), jnp.float32)
    head_gate = jnp.clip(0.3 + 0.7 * jax.random.uniform(keys[11], (HEADS,), jnp.float32) ** levels(keys[11], (HEADS,), ((0, 4),), -0.2, 0.2), 0.3, 1.0)
    inter_gate = jnp.clip(0.3 + 0.7 * jax.random.uniform(keys[12], (FF,), jnp.float32) ** levels(keys[12], (FF,), ((0, 4),), -0.2, 0.2), 0.3, 1.0)
    branch_gate = jnp.clip(jax.random.uniform(keys[13], (2,), jnp.float32, 0.6, 1.4), 0.6, 1.4)
    hidden_gate = jnp.clip(0.5 + 0.70000005 * jax.random.uniform(keys[14], (D,), jnp.float32) ** levels(keys[14], (D,), ((0, 4),), -0.2, 0.2), 0.5, 1.2)
    hidden_mask = place_ends((jax.random.randint(keys[15], (D,), 0, 4) < 3).astype(jnp.int32), jax.random.fold_in(keys[15], 1), 0, 1)
    doc_lengths = jax.vmap(lambda own: uneven_parts(own, DOCS, LEN, LEN // 2, 2))(jax.random.split(keys[16], ROWS)).reshape((ROWS, DOCS)).astype(jnp.int32)
    cotangent = bell_draw(keys[17], (D, TOKENS), 1.0, 6.0, ((0, 4), (1, 8)))
    return {"tokens": tokens, "w_qkv": w_qkv, "b_qv": b_qv, "w_out": w_out, "b_out": b_out, "w_in": w_in, "b_in": b_in, "w_back": w_back, "b_back": b_back, "norm_gain": norm_gain, "norm_bias": norm_bias, "head_gate": head_gate, "inter_gate": inter_gate, "branch_gate": branch_gate, "hidden_gate": hidden_gate, "hidden_mask": hidden_mask, "doc_lengths": doc_lengths, "cotangent": cotangent}


@jax.custom_vjp
def low(v):
    return lax.optimization_barrier(v.astype(jnp.bfloat16)).astype(jnp.float32)

@jax.custom_vjp
def low_back(v):
    return v

def low_keep(v):
    return (low(v), None)

def low_pass(kept, grad):
    return (grad,)

def back_keep(v):
    return (v, None)

def back_low(kept, grad):
    return (low(grad),)
low.defvjp(low_keep, low_pass)
low_back.defvjp(back_keep, back_low)
norm_eps = 1e-06
masked_score = -1e+30

def high_dot(left_mat, right_mat):
    return jnp.dot(left_mat, right_mat, precision=lax.Precision.HIGHEST)

def doc_table(lengths):
    doc_ends = jnp.cumsum(lengths, axis=1)
    position = jnp.arange(LEN, dtype=jnp.int32)
    return lax.optimization_barrier(jnp.sum((position[None, :, None] >= doc_ends[:, None, :]).astype(jnp.int32), axis=2))

def layer_norm(residual, gain_row, bias_row):
    row_mean = lax.optimization_barrier(jnp.mean(residual, axis=-1, keepdims=True))
    centered = residual - row_mean
    spread = lax.optimization_barrier(jnp.mean(centered * centered, axis=-1, keepdims=True))
    return centered * lax.rsqrt(spread + norm_eps) * gain_row + bias_row

def row_attention(query_rows, key_rows, value_rows, segments):
    q_heads = query_rows.reshape(LEN, HEADS, HEAD_DIM)
    k_heads = key_rows.reshape(LEN, HEADS, HEAD_DIM)
    v_heads = value_rows.reshape(LEN, HEADS, HEAD_DIM)
    raw_scores = jnp.einsum('qhd,khd->hqk', q_heads, k_heads, precision=lax.Precision.HIGHEST) * HEAD_DIM ** (-0.5)
    raw_scores = low_back(raw_scores)
    same_doc = segments[:, None] == segments[None, :]
    logits = jnp.where(same_doc[None], raw_scores, masked_score)
    row_peak = lax.optimization_barrier(jnp.max(logits, axis=-1, keepdims=True))
    exponent = jnp.exp(logits - row_peak)
    probs = exponent / lax.optimization_barrier(jnp.sum(exponent, axis=-1, keepdims=True))
    context = jnp.einsum('hqk,khd->qhd', low(probs), v_heads, precision=lax.Precision.HIGHEST)
    return context.reshape(LEN, D)

def forward(params, tokens, segments, kept_units):
    w_qkv, b_qv, w_out, b_out, w_in, b_in, w_back, b_back, norm_gain, norm_bias, head_gate, inter_gate, branch_gate, hidden_gate = params
    row_count = segments.shape[0]
    hidden_cols = hidden_gate * kept_units
    query_rows = low(low_back(high_dot(tokens, w_qkv[0].T) + b_qv[0]))
    key_rows = low(low_back(high_dot(tokens, w_qkv[1].T)))
    value_rows = low(low_back(high_dot(tokens, w_qkv[2].T) + b_qv[1]))

    def one_row(block_item):
        return row_attention(block_item[0], block_item[1], block_item[2], block_item[3])
    context = lax.map(jax.checkpoint(one_row), (query_rows.reshape(row_count, LEN, D), key_rows.reshape(row_count, LEN, D), value_rows.reshape(row_count, LEN, D), segments))
    context = low_back(context.reshape(row_count * LEN, D))
    gated_ctx = low(context * jnp.repeat(head_gate, HEAD_DIM))
    attn_pre = low_back(high_dot(gated_ctx, w_out.T) + b_out)
    residual = tokens + branch_gate[0] * attn_pre * hidden_cols
    normed = layer_norm(residual, norm_gain[0], norm_bias[0])
    pre_act = low_back(high_dot(low(normed), w_in) + b_in)
    inter_out = low(jax.nn.gelu(pre_act, approximate=False) * inter_gate)
    ffn_pre = low_back(high_dot(inter_out, w_back.T) + b_back)
    return layer_norm(normed + branch_gate[1] * ffn_pre * hidden_cols, norm_gain[1], norm_bias[1])

def reference(tokens, w_qkv, b_qv, w_out, b_out, w_in, b_in, w_back, b_back, norm_gain, norm_bias, head_gate, inter_gate, branch_gate, hidden_gate, hidden_mask, doc_lengths, cotangent):
    params = (w_qkv.astype(jnp.float32), b_qv.astype(jnp.float32), w_out.astype(jnp.float32), b_out.astype(jnp.float32), w_in.astype(jnp.float32), b_in.astype(jnp.float32), w_back.astype(jnp.float32), b_back.astype(jnp.float32), norm_gain.astype(jnp.float32), norm_bias.astype(jnp.float32), head_gate.astype(jnp.float32), inter_gate.astype(jnp.float32), branch_gate.astype(jnp.float32), hidden_gate.astype(jnp.float32))
    kept_units = hidden_mask.astype(jnp.float32)
    segments = doc_table(doc_lengths)
    group_rows = 8 if ROWS % 8 == 0 else ROWS
    blocks = ROWS // group_rows
    token_blocks = tokens.astype(jnp.float32).T.reshape(blocks, group_rows * LEN, D)
    cot_blocks = cotangent.astype(jnp.float32).T.reshape(blocks, group_rows * LEN, D)
    seg_blocks = segments.reshape(blocks, group_rows, LEN)

    def step(running, block_item):
        block_tokens, block_cot, block_seg = block_item

        def run_layer(layer_params, layer_tokens):
            return forward(layer_params, layer_tokens, block_seg, kept_units)
        block_out, pull_back = jax.vjp(run_layer, params, block_tokens)
        grad_params, grad_input = pull_back(block_cot)
        running = jax.tree.map(jnp.add, running, grad_params)
        return (running, (block_out.astype(jnp.bfloat16), grad_input.astype(jnp.bfloat16)))
    start = jax.tree.map(jnp.zeros_like, params)
    grad_sums, (outputs, grad_inputs) = lax.scan(step, start, (token_blocks, cot_blocks, seg_blocks))
    return (outputs.reshape(TOKENS, D).T, grad_inputs.reshape(TOKENS, D).T, grad_sums[0], grad_sums[1], grad_sums[2], grad_sums[3], grad_sums[4], grad_sums[5], grad_sums[6], grad_sums[7], grad_sums[8], grad_sums[9], grad_sums[10], grad_sums[11], grad_sums[12], grad_sums[13])
```

```python
import functools

import jax
import jax.numpy as jnp
from jax import lax
from jax.experimental import pallas as pl
from jax.experimental.pallas import tpu as pltpu
from jax.sharding import PartitionSpec as P

HEAD_DIM = 64
norm_eps = 1e-06
masked_score = -1e30
bf16 = jnp.bfloat16
f32 = jnp.float32
MIB = 1 << 20

VMEM = pl.BlockSpec(memory_space=pltpu.VMEM)
SMEM = pl.BlockSpec(memory_space=pltpu.SMEM)
ANY = pl.BlockSpec(memory_space=pl.ANY)


def swap(block, axis, bit):
    return lax.ppermute(block, axis, [(i, i ^ bit) for i in range(lax.axis_size(axis))])


def sds(shape, dtype):
    return jax.ShapeDtypeStruct(shape, dtype)


def local_kernel(body, name, args, specs, outs, scratch=(), flops=0, vmem=40):
    nbytes = sum(a.size * a.dtype.itemsize for a in args)
    nbytes += sum(o.size * o.dtype.itemsize for o in outs)
    return pl.pallas_call(
        body,
        name=name,
        out_shape=outs,
        in_specs=specs,
        out_specs=[VMEM] * len(outs),
        scratch_shapes=list(scratch),
        compiler_params=pltpu.CompilerParams(vmem_limit_bytes=vmem * MIB),
        cost_estimate=pl.CostEstimate(flops=flops, bytes_accessed=nbytes, transcendentals=0),
    )(*args)


def dot(left, right):
    return jnp.dot(left, right, preferred_element_type=f32)


def dot_nt(left, right):
    return lax.dot_general(left, right, (((1,), (1,)), ((), ())), preferred_element_type=f32)


def dot_tn(left, right):
    return lax.dot_general(left, right, (((0,), (0,)), ((), ())), preferred_element_type=f32)


def at(index, size):
    return pl.ds(pl.multiple_of(index * size, size), size)


def doc_bounds(lengths, query):
    start = jnp.zeros_like(query)
    stop = jnp.zeros_like(query)
    end = jnp.int32(0)
    for j in range(lengths.shape[1]):
        begin, end = end, end + lengths[0, j]
        inside = (query >= begin) & (query < end)
        start = jnp.where(inside, begin, start)
        stop = jnp.where(inside, end, stop)
    return start, stop


def attn_forward(
    where, lengths, gate, bias, x0, x1, x2, x3, w_qkv,
    x_all, qkv, logsum, mine, mine_x, send, x_block, gated,
):
    me = where[0]
    feats, toks = x0.shape
    block = toks // 4
    for k, piece in enumerate((x0, x1, x2, x3)):
        x_all[at(me ^ k, feats), :] = piece[...]
    x_block[...] = x_all[:, at(me, block)]
    cols = jnp.transpose(bias[...])
    for c in range(3):
        rows = dot(w_qkv[c], x_all[...])
        if c != 1:
            rows = rows + cols[:feats, c // 2 : c // 2 + 1]
        rows = rows.astype(bf16)
        if c == 0:
            rows = rows * jnp.asarray(HEAD_DIM ** (-0.5), bf16)
        qkv[c] = rows
    heads = feats // HEAD_DIM
    for head in range(heads):
        span = slice(head * HEAD_DIM, (head + 1) * HEAD_DIM)
        keys = jnp.transpose(qkv[1, span, :])
        values = qkv[2, span, :]
        for j in range(4):
            chunk = slice(j * block, (j + 1) * block)
            scores = dot(keys, qkv[0, span, chunk])
            query = lax.broadcasted_iota(jnp.int32, (1, block), 1) + j * block
            start, stop = doc_bounds(lengths, query)
            position = lax.broadcasted_iota(jnp.int32, scores.shape, 0)
            scores = jnp.where((position >= start) & (position < stop), scores, masked_score)
            peak = jnp.max(scores, axis=0, keepdims=True)
            expo = jnp.exp(scores - peak)
            total = jnp.sum(expo, axis=0, keepdims=True)
            probs = (expo * (1.0 / total)).astype(bf16)
            logsum[head : head + 1, chunk] = peak + jnp.log(total)
            gated[span, chunk] = (dot(values, probs) * gate[head]).astype(bf16)
    mine[...] = gated[:, at(me, block)]
    mine_x[...] = gated[:, at(me ^ 2, block)]
    send[:feats, :] = gated[:, at(me ^ 1, block)]
    send[feats:, :] = gated[:, at(me ^ 3, block)]


def attn_backward(
    where, lengths, qkv, logsum, mine, from_x, from_core, grads, head_sums, bias_sums, up
):
    me = where[0]
    feats, block = mine.shape
    up[:, at(me, block)] = mine[...]
    up[:, at(me ^ 1, block)] = from_core[:feats, :]
    up[:, at(me ^ 2, block)] = from_x[:feats, :]
    up[:, at(me ^ 3, block)] = from_core[feats:, :]
    heads = feats // HEAD_DIM
    head_sums[...] = jnp.zeros_like(head_sums)
    for head in range(heads):
        span = slice(head * HEAD_DIM, (head + 1) * HEAD_DIM)
        queries, keys_t, values_t = (qkv[c, span, :] for c in range(3))
        keys = jnp.transpose(keys_t)
        values = jnp.transpose(values_t)
        upstream = up[span, :]
        grad_k = jnp.zeros((HEAD_DIM, 4 * block), f32)
        grad_v = jnp.zeros((HEAD_DIM, 4 * block), f32)
        inner_sum = jnp.zeros((1, block), f32)
        for j in range(4):
            chunk = slice(j * block, (j + 1) * block)
            scores = dot(keys, queries[:, chunk])
            query = lax.broadcasted_iota(jnp.int32, (1, block), 1) + j * block
            start, stop = doc_bounds(lengths, query)
            position = lax.broadcasted_iota(jnp.int32, scores.shape, 0)
            scores = jnp.where((position >= start) & (position < stop), scores, masked_score)
            probs = jnp.exp(scores - logsum[head : head + 1, chunk])
            grad_p = dot(values, upstream[:, chunk])
            weighted = probs * grad_p
            inner = jnp.sum(weighted, axis=0, keepdims=True)
            inner_sum = inner_sum + inner
            grad_s = (weighted - probs * inner).astype(bf16)
            grad_v = grad_v + dot_nt(upstream[:, chunk], probs.astype(bf16))
            grad_k = grad_k + dot_nt(queries[:, chunk], grad_s)
            grads[span, chunk] = (dot(keys_t, grad_s) * HEAD_DIM ** (-0.5)).astype(bf16)
        grads[feats + head * HEAD_DIM : feats + (head + 1) * HEAD_DIM, :] = grad_k.astype(bf16)
        grads[2 * feats + head * HEAD_DIM : 2 * feats + (head + 1) * HEAD_DIM, :] = grad_v.astype(
            bf16
        )
        head_sums[head : head + 1, :] = inner_sum
    ones = jnp.ones((8, 4 * block), bf16)
    bias_sums[...] = dot_nt(ones, grads[...])


def qkv_weight_grad(grads, x_all, grad_w):
    for k in range(3):
        rows = slice(k * 192, (k + 1) * 192)
        grad_w[rows, :] = dot_nt(grads[rows, :], x_all[...])


def qkv_input_grad(where, grads, w_qkv, dres, mine, mine_x, send, full):
    me = where[0]
    feats = mine.shape[0]
    block = dres.shape[0]
    total = None
    for c in range(3):
        part = dot(jnp.transpose(w_qkv[c]), grads[c * feats : (c + 1) * feats, :])
        total = part if total is None else total + part
    full[...] = total
    full[:, at(me, block)] += jnp.transpose(dres[...])
    mine[...] = full[at(me, feats), :]
    mine_x[...] = full[at(me ^ 2, feats), :]
    send[:feats, :] = full[at(me ^ 1, feats), :].astype(bf16)
    send[feats:, :] = full[at(me ^ 3, feats), :].astype(bf16)


def load_rows(where, own, from_x, from_core, whole, sems):
    me = where[0]
    n = own.shape[0]
    copies = [
        pltpu.make_async_copy(own, whole.at[at(me, n), :], sems.at[0]),
        pltpu.make_async_copy(from_core.at[:n, :], whole.at[at(me ^ 1, n), :], sems.at[1]),
        pltpu.make_async_copy(from_x, whole.at[at(me ^ 2, n), :], sems.at[2]),
        pltpu.make_async_copy(from_core.at[n:, :], whole.at[at(me ^ 3, n), :], sems.at[3]),
    ]
    for copy in copies:
        copy.start()
    return copies


def row_norm(values):
    mean = jnp.mean(values, axis=1, keepdims=True)
    centered = values - mean
    spread = jnp.mean(centered * centered, axis=1, keepdims=True)
    inv = lax.rsqrt(spread + norm_eps)
    return centered * inv, inv


def attn_out(
    where, branch, g0, g1, g2, x_block, vecs, wo_own, wo_x, wo_core,
    normed, normed_low, hat, inv_out, pre, gated_rows, wo, heads_all, sems,
):
    me = where[0]
    copies = load_rows(where, wo_own, wo_x, wo_core, wo, sems)
    feats = g0.shape[0]
    heads_all[at(me, feats), :] = g0[...]
    heads_all[at(me ^ 1, feats), :] = g1[:feats, :]
    heads_all[at(me ^ 2, feats), :] = g2[:feats, :]
    heads_all[at(me ^ 3, feats), :] = g2[feats:, :]
    gated = jnp.transpose(heads_all[...])
    gated_rows[...] = gated
    tokens = jnp.transpose(x_block[...].astype(f32))
    for copy in copies:
        copy.wait()
    attn = dot_nt(gated, wo[...]) + vecs[0:1, :]
    pre[...] = attn
    resid = tokens + branch[0] * attn * vecs[3:4, :]
    x_hat, inv = row_norm(resid)
    value = x_hat * vecs[1:2, :] + vecs[2:3, :]
    hat[...] = x_hat
    inv_out[...] = jnp.broadcast_to(inv, inv_out.shape)
    normed[...] = value
    normed_low[...] = value.astype(bf16)


def attn_out_back(
    where, branch, part, recv, dres2, hat, inv, pre, vecs, wo_own, wo_x, wo_core,
    dres, grad_attn, sums, up_mine, up_core, up_x, wo, ups, sems,
):
    me = where[0]
    copies = load_rows(where, wo_own, wo_x, wo_core, wo, sems)
    feats = up_mine.shape[0]
    grad = part[...] + recv[...].astype(f32) + dres2[...]
    x_hat = hat[...]
    scaled = grad * vecs[1:2, :]
    mean_plain = jnp.mean(scaled, axis=1, keepdims=True)
    mean_along = jnp.mean(scaled * x_hat, axis=1, keepdims=True)
    grad_resid = inv[:, 0:1] * (scaled - mean_plain - x_hat * mean_along)
    dres[...] = grad_resid
    low = (grad_resid * (branch[0] * vecs[3:4, :])).astype(bf16)
    grad_attn[...] = low
    for copy in copies:
        copy.wait()
    grad_gated = dot(low, wo[...])
    upstream = (grad_gated * vecs[7:8, :]).astype(bf16)
    ups[...] = jnp.transpose(upstream)
    up_mine[...] = ups[at(me, feats), :]
    up_core[...] = ups[at(me ^ 1, feats), :]
    up_x[:feats, :] = ups[at(me ^ 2, feats), :]
    up_x[feats:, :] = ups[at(me ^ 3, feats), :]
    sums[0:1, :] = jnp.sum(grad * x_hat, axis=0, keepdims=True)
    sums[1:2, :] = jnp.sum(grad, axis=0, keepdims=True)
    sums[2:3, :] = jnp.sum(low.astype(f32), axis=0, keepdims=True)
    sums[3:4, :] = jnp.sum(grad_resid * pre[...], axis=0, keepdims=True)


def out_weight_grad(where, grad_attn, gated_rows, mine, mine_x, send, full):
    me = where[0]
    feats = mine.shape[0]
    full[...] = dot_tn(grad_attn[...], gated_rows[...])
    mine[...] = full[at(me, feats), :]
    mine_x[...] = full[at(me ^ 2, feats), :]
    send[:feats, :] = full[at(me ^ 1, feats), :].astype(bf16)
    send[feats:, :] = full[at(me ^ 3, feats), :].astype(bf16)


def load_units(where, wi_own, wi_core, wi, sems, k):
    core = where[0] & 1
    n = wi_own.shape[1]
    copies = [
        pltpu.make_async_copy(wi_own, wi.at[:, at(core, n)], sems.at[k]),
        pltpu.make_async_copy(wi_core, wi.at[:, at(core ^ 1, n)], sems.at[k + 1]),
    ]
    for copy in copies:
        copy.start()
    return copies


def load_back(where, wb_own, wb_x, wb_core, wb, sems, k):
    me = where[0]
    n = wb_own.shape[0]
    units = wb_x.shape[1]
    copies = [
        pltpu.make_async_copy(
            wb_own.at[:, at(me // 2, units)], wb.at[at(me, n), :], sems.at[k]
        ),
        pltpu.make_async_copy(wb_core.at[:n, :], wb.at[at(me ^ 1, n), :], sems.at[k + 1]),
        pltpu.make_async_copy(wb_x, wb.at[at(me ^ 2, n), :], sems.at[k + 2]),
        pltpu.make_async_copy(wb_core.at[n:, :], wb.at[at(me ^ 3, n), :], sems.at[k + 3]),
    ]
    for copy in copies:
        copy.start()
    return copies


def ffn_forward(
    where, normed, unit_rows, wi_own, wi_core, wb_own, wb_x, wb_core,
    act, slope, inter_mine, inter_core, part, wi, wb, inter, sems,
):
    core = where[0] & 1
    first = load_units(where, wi_own, wi_core, wi, sems, 0)
    second = load_back(where, wb_own, wb_x, wb_core, wb, sems, 2)
    for copy in first:
        copy.wait()
    units = wi.shape[1]
    step = 256
    for j in range(units // step):
        cut = slice(j * step, (j + 1) * step)
        u = dot(normed[...], wi[:, cut]) + unit_rows[0:1, cut]
        cdf = 0.5 * (1.0 + lax.erf(u * 0.7071067811865476))
        value = u * cdf
        act[:, cut] = value
        slope[:, cut] = cdf + u * (jnp.exp(-0.5 * u * u) * 0.3989422804014327)
        inter[:, cut] = (value * unit_rows[1:2, cut]).astype(bf16)
    inter_mine[...] = inter[:, at(core, units // 2)]
    inter_core[...] = inter[:, at(core ^ 1, units // 2)]
    for copy in second:
        copy.wait()
    part[...] = dot_nt(inter[...], wb[...]).astype(part.dtype)


def ffn_backward(
    where, grad_ffn, act, slope, unit_rows, wi_own, wi_core, wb_own, wb_x, wb_core,
    gpre_mine, gpre_core, part, sums, wi, wb, gpre, sems,
):
    core = where[0] & 1
    first = load_back(where, wb_own, wb_x, wb_core, wb, sems, 2)
    second = load_units(where, wi_own, wi_core, wi, sems, 0)
    for copy in first:
        copy.wait()
    units = wi.shape[1]
    step = 256
    for j in range(units // step):
        cut = slice(j * step, (j + 1) * step)
        ginter = dot(grad_ffn[...], wb[:, cut])
        sums[:, cut] = jnp.broadcast_to(
            jnp.sum(ginter * act[:, cut], axis=0, keepdims=True), (8, step)
        )
        gpre[:, cut] = (ginter * unit_rows[1:2, cut] * slope[:, cut]).astype(bf16)
    gpre_mine[...] = gpre[:, at(core, units // 2)]
    gpre_core[...] = gpre[:, at(core ^ 1, units // 2)]
    for copy in second:
        copy.wait()
    part[...] = dot_nt(gpre[...], wi[...]).astype(part.dtype)


def ffn_weight_grads(
    where, n0, n1, n2, n3, e0, e1, e2, e3, p0, p1, p2, p3, f0, f1, f2, f3,
    in_keep, in_send, back_keep, back_send, bias_sums, left, right, full,
):
    parity = where[1] & 1
    toks = n0.shape[0]
    half = full.shape[0] // 2

    def fill(ref, pieces):
        for k, piece in enumerate(pieces):
            ref[k * toks : (k + 1) * toks, :] = piece[...]

    fill(left, (n0, n1, n2, n3))
    fill(right, (p0, p1, p2, p3))
    full[...] = dot_tn(left[...], right[...])
    in_keep[...] = full[at(parity, half), :]
    in_send[...] = full[at(parity ^ 1, half), :].astype(bf16)
    bias_sums[...] = jnp.broadcast_to(
        jnp.sum(right[...].astype(f32), axis=0, keepdims=True), bias_sums.shape
    )
    fill(left, (f0, f1, f2, f3))
    fill(right, (e0, e1, e2, e3))
    full[...] = dot_tn(left[...], right[...])
    owners, subs = 4, 8
    rows = full.shape[0] // (owners * subs)
    for q in range(subs // 2):
        for h in range(owners):
            to = slice((q * owners + h) * rows, (q * owners + h + 1) * rows)
            base = h * subs * rows + q * rows
            kept = base + parity * (subs // 2) * rows
            sent = base + (parity ^ 1) * (subs // 2) * rows
            back_keep[to, :] = full[pl.ds(pl.multiple_of(kept, rows), rows), :]
            left_rows = full[pl.ds(pl.multiple_of(sent, rows), rows), :]
            back_send[to, :] = left_rows.astype(bf16)


def second_norm(
    where, branch, part, recv, normed, cot_own, cot_x, cot_core, vecs,
    out_mine, out_x, out_send, dres, grad_low, sums, cots, outs,
):
    me = where[0]
    feats = cot_own.shape[0]
    block = cot_core.shape[1]
    cots[at(me, feats), :] = cot_own[:, at(me, block)]
    cots[at(me ^ 1, feats), :] = cot_core[:feats, :]
    cots[at(me ^ 2, feats), :] = cot_x[:, at(me & 1, block)]
    cots[at(me ^ 3, feats), :] = cot_core[feats:, :]
    grad_out = jnp.transpose(cots[...].astype(f32))
    ffn = part[...] + recv[...].astype(f32) + vecs[4:5, :]
    resid = normed[...] + branch[1] * ffn * vecs[3:4, :]
    x_hat, inv = row_norm(resid)
    value = x_hat * vecs[5:6, :] + vecs[6:7, :]
    scaled = grad_out * vecs[5:6, :]
    mean_plain = jnp.mean(scaled, axis=1, keepdims=True)
    mean_along = jnp.mean(scaled * x_hat, axis=1, keepdims=True)
    grad_resid = inv * (scaled - mean_plain - x_hat * mean_along)
    dres[...] = grad_resid
    low = (grad_resid * (branch[1] * vecs[3:4, :])).astype(bf16)
    grad_low[...] = low
    sums[0:1, :] = jnp.sum(grad_out * x_hat, axis=0, keepdims=True)
    sums[1:2, :] = jnp.sum(grad_out, axis=0, keepdims=True)
    sums[2:3, :] = jnp.sum(low.astype(f32), axis=0, keepdims=True)
    sums[3:4, :] = jnp.sum(grad_resid * ffn, axis=0, keepdims=True)
    outs[...] = jnp.transpose(value).astype(bf16)
    out_mine[...] = outs[at(me, feats), :]
    out_x[...] = outs[at(me ^ 2, feats), :]
    out_send[:feats, :] = outs[at(me ^ 1, feats), :]
    out_send[feats:, :] = outs[at(me ^ 3, feats), :]


def ordered(bit, mine, other, axis=0):
    return jnp.where(
        bit == 0,
        jnp.concatenate([mine, other], axis=axis),
        jnp.concatenate([other, mine], axis=axis),
    )


def cut_half(full, bit):
    half = full.shape[0] // 2
    keep = lax.dynamic_slice_in_dim(full, bit * half, half, 0)
    send = lax.dynamic_slice_in_dim(full, (1 - bit) * half, half, 0)
    return keep, send.astype(bf16)


def far_rows_sum(chunk):
    count = lax.axis_size("rows")
    if count == 8:
        return chunk
    groups = [[i + 8 * j for j in range(count // 8)] for i in range(8)]
    return lax.psum(chunk, "rows", axis_index_groups=groups)


def scatter_rows(keep, send, row):
    total = keep + swap(send, "rows", 1).astype(f32)
    for k in (1, 2):
        keep, send = cut_half(total, (row >> k) & 1)
        total = keep + swap(send, "rows", 1 << k).astype(f32)
    return far_rows_sum(total)


def gather_rows(chunk, row):
    for k in (2, 1, 0):
        chunk = ordered((row >> k) & 1, chunk, swap(chunk, "rows", 1 << k))
    return chunk.astype(f32)


def shards(
    tokens, w_qkv, b_qv, w_out, b_out, w_in, b_in, w_back, b_back, norm_gain, norm_bias,
    head_gate, inter_gate, branch_gate, hidden_gate, hidden_mask, doc_lengths, cotangent,
):
    feats, toks = tokens.shape
    width = 4 * feats
    units = w_in.shape[1]
    block = toks // 4
    hid = lax.axis_index("hid")
    row = lax.axis_index("rows")
    core, chip = hid & 1, hid >> 1
    where = jnp.stack([hid, row]).astype(jnp.int32)

    tokens_core = swap(tokens, "hid", 1)
    tokens_x = swap(tokens, "hid", 2)
    tokens_far = swap(tokens_x, "hid", 1)

    kept = hidden_mask.astype(f32)
    own_vecs = jnp.stack(
        [
            b_out, norm_gain[0], norm_bias[0], hidden_gate * kept, b_back,
            norm_gain[1], norm_bias[1], jnp.repeat(head_gate, HEAD_DIM),
        ]
    )
    pair_vecs = ordered(core, own_vecs, swap(own_vecs, "hid", 1), axis=1)
    vecs = ordered(chip, pair_vecs, swap(pair_vecs, "hid", 2), axis=1)
    own_units = jnp.stack([b_in, inter_gate])
    unit_rows = ordered(core, own_units, swap(own_units, "hid", 1), axis=1)

    wo_x = swap(w_out, "hid", 2)
    wo_core = swap(jnp.concatenate([w_out, wo_x], 0), "hid", 1)
    wb_chip = lax.dynamic_slice_in_dim(w_back, chip * 2 * units, 2 * units, 1)
    wb_x = swap(lax.dynamic_slice_in_dim(w_back, (1 - chip) * 2 * units, 2 * units, 1), "hid", 2)
    wb_core = swap(jnp.concatenate([wb_chip, wb_x], 0), "hid", 1)
    wi_core = swap(w_in, "hid", 1)
    cot_x = swap(
        lax.dynamic_slice_in_dim(cotangent, (1 - chip) * 2 * block, 2 * block, 1), "hid", 2
    )
    cot_core = swap(
        jnp.concatenate(
            [
                lax.dynamic_slice_in_dim(cotangent, (hid ^ 1) * block, block, 1),
                lax.dynamic_slice_in_dim(cot_x, (1 - core) * block, block, 1),
            ],
            0,
        ),
        "hid",
        1,
    )

    bias = jnp.pad(b_qv, ((0, 6), (0, -feats % 128)))
    x_all, qkv, logsum, ctx, ctx_x, ctx_send, x_block = local_kernel(
        attn_forward,
        "attn_forward",
        (where, doc_lengths, head_gate, bias, tokens, tokens_core, tokens_x, tokens_far, w_qkv),
        [SMEM, SMEM, SMEM] + [VMEM] * 6,
        [
            sds((width, toks), bf16),
            sds((3, feats, toks), bf16),
            sds((8, toks), f32),
            sds((feats, block), bf16),
            sds((feats, block), bf16),
            sds((2 * feats, block), bf16),
            sds((width, block), bf16),
        ],
        [pltpu.VMEM((feats, toks), bf16)],
        flops=2 * toks * feats * (3 * width + 2 * toks),
    )
    ctx_core = swap(ctx_send, "hid", 1)
    ctx_far = swap(jnp.concatenate([ctx_x, ctx_core[feats:]], 0), "hid", 2)

    normed, normed_low, hat, inv, attn_pre, gated_rows = local_kernel(
        attn_out,
        "attn_out",
        (where, branch_gate, ctx, ctx_core, ctx_far, x_block, vecs, w_out, wo_x, wo_core),
        [SMEM, SMEM] + [VMEM] * 5 + [ANY] * 3,
        [
            sds((block, width), f32),
            sds((block, width), bf16),
            sds((block, width), f32),
            sds((block, 128), f32),
            sds((block, width), f32),
            sds((block, width), bf16),
        ],
        [
            pltpu.VMEM((width, width), bf16),
            pltpu.VMEM((width, block), bf16),
            pltpu.SemaphoreType.DMA((4,)),
        ],
        flops=2 * block * width * width,
    )

    def forward_part(rows, part_type):
        return local_kernel(
            ffn_forward,
            "ffn_forward",
            (where, rows, unit_rows, w_in, wi_core, w_back, wb_x, wb_core),
            [SMEM, VMEM, VMEM] + [ANY] * 5,
            [
                sds((block, 2 * units), f32),
                sds((block, 2 * units), f32),
                sds((block, units), bf16),
                sds((block, units), bf16),
                sds((block, width), part_type),
            ],
            [
                pltpu.VMEM((width, 2 * units), bf16),
                pltpu.VMEM((width, 2 * units), bf16),
                pltpu.VMEM((block, 2 * units), bf16),
                pltpu.SemaphoreType.DMA((6,)),
            ],
            flops=8 * block * width * units,
        )

    normed_x = swap(normed_low, "hid", 2)
    act, slope, inter, inter_send, ffn_part = forward_part(normed_low, f32)
    act_x, slope_x, inter_x, inter_x_send, ffn_send = forward_part(normed_x, bf16)
    ffn_recv = swap(ffn_send, "hid", 2)

    out_mine, out_x, out_send, dres2, gffn, sums2 = local_kernel(
        second_norm,
        "second_norm",
        (where, branch_gate, ffn_part, ffn_recv, normed, cotangent, cot_x, cot_core, vecs),
        [SMEM, SMEM] + [VMEM] * 7,
        [
            sds((feats, block), bf16),
            sds((feats, block), bf16),
            sds((2 * feats, block), bf16),
            sds((block, width), f32),
            sds((block, width), bf16),
            sds((4, width), f32),
        ],
        [pltpu.VMEM((width, block), bf16), pltpu.VMEM((width, block), bf16)],
    )

    def backward_part(rows, act, slope, part_type):
        return local_kernel(
            ffn_backward,
            "ffn_backward",
            (where, rows, act, slope, unit_rows, w_in, wi_core, w_back, wb_x, wb_core),
            [SMEM] + [VMEM] * 4 + [ANY] * 5,
            [
                sds((block, units), bf16),
                sds((block, units), bf16),
                sds((block, width), part_type),
                sds((8, 2 * units), f32),
            ],
            [
                pltpu.VMEM((width, 2 * units), bf16),
                pltpu.VMEM((width, 2 * units), bf16),
                pltpu.VMEM((block, 2 * units), bf16),
                pltpu.SemaphoreType.DMA((6,)),
            ],
            flops=8 * block * width * units,
        )

    gffn_x = swap(gffn, "hid", 2)
    gpre, gpre_send, gn_part, ig_sum = backward_part(gffn, act, slope, f32)
    gpre_x, gpre_x_send, gn_send, ig_sum_x = backward_part(gffn_x, act_x, slope_x, bf16)
    gn_recv = swap(gn_send, "hid", 2)

    to_core = [
        swap(a, "hid", 1)
        for a in (
            normed_low, normed_x, inter_send, inter_x_send, gpre_send, gpre_x_send, gffn, gffn_x,
        )
    ]
    in_keep, in_send, back_keep, back_send, bin_sum = local_kernel(
        ffn_weight_grads,
        "ffn_weight_grads",
        (
            where,
            normed_low, normed_x, to_core[0], to_core[1],
            inter, inter_x, to_core[2], to_core[3],
            gpre, gpre_x, to_core[4], to_core[5],
            gffn, gffn_x, to_core[6], to_core[7],
        ),
        [SMEM] + [VMEM] * 16,
        [
            sds((width // 2, units), f32),
            sds((width // 2, units), bf16),
            sds((width // 2, units), f32),
            sds((width // 2, units), bf16),
            sds((8, units), f32),
        ],
        [
            pltpu.VMEM((toks, width), bf16),
            pltpu.VMEM((toks, units), bf16),
            pltpu.VMEM((width, units), f32),
        ],
        flops=4 * toks * width * units,
    )

    dres1, gattn, sums1, up_mine, up_core, up_x = local_kernel(
        attn_out_back,
        "attn_out_back",
        (
            where, branch_gate, gn_part, gn_recv, dres2, hat, inv, attn_pre, vecs,
            w_out, wo_x, wo_core,
        ),
        [SMEM, SMEM] + [VMEM] * 7 + [ANY] * 3,
        [
            sds((block, width), f32),
            sds((block, width), bf16),
            sds((4, width), f32),
            sds((feats, block), bf16),
            sds((feats, block), bf16),
            sds((2 * feats, block), bf16),
        ],
        [
            pltpu.VMEM((width, width), bf16),
            pltpu.VMEM((width, block), bf16),
            pltpu.SemaphoreType.DMA((4,)),
        ],
        flops=2 * block * width * width,
    )
    up_far = swap(up_x, "hid", 2)
    up_recv = swap(jnp.concatenate([up_core, up_far[feats:]], 0), "hid", 1)

    grads, head_sums, bias_sums = local_kernel(
        attn_backward,
        "attn_backward",
        (where, doc_lengths, qkv, logsum, up_mine, up_far, up_recv),
        [SMEM, SMEM] + [VMEM] * 5,
        [
            sds((3 * feats, toks), bf16),
            sds((8, block), f32),
            sds((8, 3 * feats), f32),
        ],
        [pltpu.VMEM((feats, toks), bf16)],
        flops=2 * toks * toks * feats * 5,
    )

    (grad_w_qkv,) = local_kernel(
        qkv_weight_grad,
        "qkv_weight_grad",
        (grads, x_all),
        [VMEM, VMEM],
        [sds((3 * feats, width), f32)],
        flops=6 * toks * feats * width,
    )
    gx_mine, gx_x, gx_send = local_kernel(
        qkv_input_grad,
        "qkv_input_grad",
        (where, grads, w_qkv, dres1),
        [SMEM] + [VMEM] * 3,
        [
            sds((feats, toks), f32),
            sds((feats, toks), f32),
            sds((2 * feats, toks), bf16),
        ],
        [pltpu.VMEM((width, toks), f32)],
        flops=6 * toks * feats * width,
    )
    gx_core = swap(gx_send, "hid", 1).astype(f32)
    gx_far = swap((gx_x + gx_core[feats:]).astype(bf16), "hid", 2)
    grad_tokens = (gx_mine + gx_core[:feats] + gx_far.astype(f32)).astype(bf16)

    out_core = swap(out_send, "hid", 1)
    out_far = swap(jnp.concatenate([out_x, out_core[feats:]], 0), "hid", 2)
    output = ordered(
        chip,
        ordered(core, out_mine, out_core[:feats], axis=1),
        ordered(core, out_far[:feats], out_far[feats:], axis=1),
        axis=1,
    )

    back = scatter_rows(back_keep, back_send, row).reshape(4, -1, units)
    sub = back.shape[1]

    def pick(full, k):
        return lax.dynamic_slice_in_dim(full, hid ^ k, 1, 0)[0]

    back_core = swap(jnp.concatenate([pick(back, 1), pick(back, 3)], 0), "hid", 1)
    back_far = swap(jnp.concatenate([pick(back, 2), back_core[sub:]], 0), "hid", 2)
    back_chunk = ordered(
        chip,
        ordered(core, pick(back, 0), back_core[:sub]),
        ordered(core, back_far[:sub], back_far[sub:]),
    )
    grad_w_back = gather_rows(back_chunk.astype(bf16), row)
    grad_w_back = grad_w_back.reshape(8, 4, sub, units).transpose(0, 2, 1, 3)
    grad_w_back = grad_w_back.reshape(feats, 4 * units)

    grad_w_in = gather_rows(scatter_rows(in_keep, in_send, row).astype(bf16), row)

    wo_mine, wo_keep, wo_send = local_kernel(
        out_weight_grad,
        "out_weight_grad",
        (where, gattn, gated_rows),
        [SMEM, VMEM, VMEM],
        [sds((feats, width), f32), sds((feats, width), f32), sds((2 * feats, width), bf16)],
        [pltpu.VMEM((width, width), f32)],
        flops=2 * block * width * width,
    )
    wo_recv = swap(wo_send, "hid", 1).astype(f32)
    wo_far = swap((wo_keep + wo_recv[feats:]).astype(bf16), "hid", 2)
    grad_w_out = wo_mine + wo_recv[:feats] + wo_far.astype(f32)
    last = jnp.concatenate([grad_w_qkv, grad_w_out], 0)
    last = gather_rows(scatter_rows(*cut_half(last, row & 1), row).astype(bf16), row)
    grad_w_qkv = last[: 3 * feats].reshape(3, feats, width)
    grad_w_out = last[3 * feats :]

    shared = jnp.concatenate([sums1, sums2], 0)
    ig_all = ig_sum[:1] + ig_sum_x[:1]
    ig_send = lax.dynamic_slice_in_dim(ig_all, (1 - core) * units, units, 1)
    with_core = swap(jnp.concatenate([shared, ig_send], 0), "hid", 1)
    shared = shared + with_core[:8]
    shared = shared + swap(shared, "hid", 2)
    ig_mine = lax.dynamic_slice_in_dim(ig_all, core * units, units, 1) + with_core[8:]
    head_row = jnp.sum(head_sums, axis=1)[None]
    vec = jnp.concatenate(
        [
            shared,
            ig_mine,
            bin_sum[:1],
            jnp.pad(bias_sums[:1], ((0, 0), (0, width - 3 * feats))),
            jnp.pad(head_row, ((0, 0), (0, width - 8))),
        ],
        0,
    )
    for k in range(3):
        vec = vec + swap(vec, "rows", 1 << k)
    vec = far_rows_sum(vec)
    cols = vecs[3]
    own = lax.dynamic_slice_in_dim(vec[:8], hid * feats, feats, 1)
    grad_branch_gate = jnp.stack([jnp.sum(vec[3] * cols), jnp.sum(vec[7] * cols)])
    hidden = (branch_gate[0] * own[3] + branch_gate[1] * own[7]) * kept
    return (
        output,
        grad_tokens,
        grad_w_qkv,
        jnp.stack([vec[10, :feats], vec[10, 2 * feats : 3 * feats]]),
        grad_w_out,
        own[2],
        grad_w_in,
        vec[9],
        grad_w_back,
        own[6],
        jnp.stack([own[0], own[4]]),
        jnp.stack([own[1], own[5]]),
        vec[11, : feats // HEAD_DIM] / head_gate,
        vec[8],
        grad_branch_gate,
        hidden,
    )


def solution(mesh):
    return jax.shard_map(
        shards,
        mesh=mesh,
        in_specs=(
            P("hid", "rows"),
            P(None, "hid", None),
            P(None, "hid"),
            P("hid", None),
            P("hid"),
            P(None, "hid"),
            P("hid"),
            P("hid", None),
            P("hid"),
            P(None, "hid"),
            P(None, "hid"),
            P("hid"),
            P("hid"),
            P(),
            P("hid"),
            P("hid"),
            P("rows", None),
            P("hid", "rows"),
        ),
        out_specs=(
            P("hid", "rows"),
            P("hid", "rows"),
            P(None, "hid", None),
            P(None, "hid"),
            P("hid", None),
            P("hid"),
            P(None, "hid"),
            P("hid"),
            P("hid", None),
            P("hid"),
            P(None, "hid"),
            P(None, "hid"),
            P("hid"),
            P("hid"),
            P(),
            P("hid"),
        ),
        check_vma=False,
    )
```

```python
import jax
import jax.numpy as jnp
from jax import lax
from jax.experimental import pallas as pl
from jax.experimental.pallas import tpu as pltpu
from jax.sharding import PartitionSpec as P

HEAD_DIM = 64
norm_eps = 1e-06
masked_score = -1e30
bf16 = jnp.bfloat16
f32 = jnp.float32
MIB = 1 << 20
HBM_BYTES_PER_MICRO = 3690000

SPECS = {
    "S": pl.BlockSpec(memory_space=pltpu.SMEM),
    "V": pl.BlockSpec(memory_space=pltpu.VMEM),
}


def swap(block, axis, bit):
    return lax.ppermute(block, axis, [(i, i ^ bit) for i in range(lax.axis_size(axis))])


def after(block, *others):
    return lax.optimization_barrier((block, *others))[0]


def sds(shape, dtype):
    return jax.ShapeDtypeStruct(shape, dtype)


def local_kernel(body, name, args, kinds, outs, scratch=(), micros=0.6, vmem=16):
    return pl.pallas_call(
        body,
        name=name,
        out_shape=outs,
        in_specs=[SPECS[k] for k in kinds],
        out_specs=[SPECS["V"]] * len(outs),
        scratch_shapes=list(scratch),
        compiler_params=pltpu.CompilerParams(vmem_limit_bytes=vmem * MIB),
        cost_estimate=pl.CostEstimate(
            flops=1, bytes_accessed=int(micros * HBM_BYTES_PER_MICRO), transcendentals=0
        ),
    )(*args)


def dot(left, right):
    return jnp.dot(left, right, preferred_element_type=f32)


def dot_nt(left, right):
    return lax.dot_general(left, right, (((1,), (1,)), ((), ())), preferred_element_type=f32)


def dot_tn(left, right):
    return lax.dot_general(left, right, (((0,), (0,)), ((), ())), preferred_element_type=f32)


def at(index, size):
    return pl.ds(pl.multiple_of(index * size, size), size)


def doc_bounds(lengths, query):
    start = jnp.zeros_like(query)
    stop = jnp.zeros_like(query)
    end = jnp.int32(0)
    for j in range(lengths.shape[1]):
        begin, end = end, end + lengths[0, j]
        inside = (query >= begin) & (query < end)
        start = jnp.where(inside, begin, start)
        stop = jnp.where(inside, end, stop)
    return start, stop


def same_doc(lengths, shape, offset):
    query = lax.broadcasted_iota(jnp.int32, (1, shape[1]), 1) + offset
    start, stop = doc_bounds(lengths, query)
    position = lax.broadcasted_iota(jnp.int32, shape, 0)
    return (position >= start) & (position < stop)


def attn_forward(
    lengths, gate, bias, x0, x1, x2, x3, w_qkv,
    x_all, qkv, logsum, mine, send_core, send_x, x_block, gated,
):
    me = lax.axis_index("hid")
    feats, toks = x0.shape
    block = toks // 4
    for k, piece in enumerate((x0, x1, x2, x3)):
        x_all[at(me ^ k, feats), :] = piece[...]
    x_block[...] = x_all[:, at(me, block)]
    cols = jnp.transpose(bias[...])
    for c in range(3):
        rows = dot(w_qkv[c], x_all[...])
        if c != 1:
            rows = rows + cols[:feats, c // 2 : c // 2 + 1]
        rows = rows.astype(bf16)
        if c == 0:
            rows = rows * jnp.asarray(HEAD_DIM ** (-0.5), bf16)
        qkv[c] = rows
    heads = feats // HEAD_DIM
    for head in range(heads):
        span = slice(head * HEAD_DIM, (head + 1) * HEAD_DIM)
        keys = jnp.transpose(qkv[1, span, :])
        values = qkv[2, span, :]
        for j in range(4):
            chunk = slice(j * block, (j + 1) * block)
            scores = dot(keys, qkv[0, span, chunk])
            scores = jnp.where(
                same_doc(lengths, scores.shape, j * block), scores, masked_score
            )
            peak = jnp.max(scores, axis=0, keepdims=True)
            expo = jnp.exp(scores - peak)
            total = jnp.sum(expo, axis=0, keepdims=True)
            probs = (expo * (1.0 / total)).astype(bf16)
            logsum[head : head + 1, chunk] = peak + jnp.log(total)
            gated[span, chunk] = (dot(values, probs) * gate[head]).astype(bf16)
    mine[...] = gated[:, at(me, block)]
    send_x[:feats, :] = gated[:, at(me ^ 2, block)]
    send_x[feats:, :] = gated[:, at(me ^ 3, block)]
    send_core[...] = gated[:, at(me ^ 1, block)]


def attn_backward(
    lengths, qkv, logsum, u0, u1, u2, u3, grads, head_sums, bias_sums, up
):
    me = lax.axis_index("hid")
    feats, block = u0.shape
    for k, piece in enumerate((u0, u1, u2.at[:feats, :], u3.at[feats:, :])):
        up[:, at(me ^ k, block)] = piece[...]
    heads = feats // HEAD_DIM
    head_sums[...] = jnp.zeros_like(head_sums)
    for head in range(heads):
        span = slice(head * HEAD_DIM, (head + 1) * HEAD_DIM)
        queries, keys_t, values_t = (qkv[c, span, :] for c in range(3))
        keys = jnp.transpose(keys_t)
        values = jnp.transpose(values_t)
        upstream = up[span, :]
        grad_k = jnp.zeros((HEAD_DIM, 4 * block), f32)
        grad_v = jnp.zeros((HEAD_DIM, 4 * block), f32)
        inner_sum = jnp.zeros((1, block), f32)
        for j in range(4):
            chunk = slice(j * block, (j + 1) * block)
            scores = dot(keys, queries[:, chunk])
            scores = jnp.where(
                same_doc(lengths, scores.shape, j * block), scores, masked_score
            )
            probs = jnp.exp(scores - logsum[head : head + 1, chunk])
            grad_p = dot(values, upstream[:, chunk])
            weighted = probs * grad_p
            inner = jnp.sum(weighted, axis=0, keepdims=True)
            inner_sum = inner_sum + inner
            grad_s = (weighted - probs * inner).astype(bf16)
            grad_v = grad_v + dot_nt(upstream[:, chunk], probs.astype(bf16))
            grad_k = grad_k + dot_nt(queries[:, chunk], grad_s)
            grads[span, chunk] = (dot(keys_t, grad_s) * HEAD_DIM ** (-0.5)).astype(bf16)
        for c, grad in ((1, grad_k), (2, grad_v)):
            rows = slice(c * feats + head * HEAD_DIM, c * feats + (head + 1) * HEAD_DIM)
            grads[rows, :] = grad.astype(bf16)
        head_sums[head : head + 1, :] = inner_sum
    ones = jnp.ones((8, 4 * block), bf16)
    bias_sums[...] = dot_nt(ones, grads[...])


def qk_weight_grad(grads, x_all, keep, send, full):
    parity = lax.axis_index("rows") & 1
    n = keep.shape[0]
    full[...] = dot_nt(grads[: 2 * n, :], x_all[...])
    send[...] = full[at(parity ^ 1, n), :].astype(bf16)
    keep[...] = full[at(parity, n), :]


def vo_weight_grad(grads, x_all, wo_mine, wo_core, wo_far, keep, send, full):
    parity = (lax.axis_index("rows") >> 1) & 1
    n = keep.shape[0]
    full[:n, :] = dot_nt(grads[2 * n :, :], x_all[...])
    full[n:, :] = wo_mine[...] + wo_core[:n, :].astype(f32) + wo_far[...].astype(f32)
    send[...] = full[at(parity ^ 1, n), :].astype(bf16)
    keep[...] = full[at(parity, n), :]


def add_low(mine, other, total):
    total[...] = (mine[...].astype(f32) + other[...].astype(f32)).astype(total.dtype)


def add_second(mine, other, total):
    n = mine.shape[0]
    total[...] = (mine[...] + other[n:, :].astype(f32)).astype(total.dtype)


def add_two(mine, first, second, total):
    n = mine.shape[0]
    both = first[:n, :].astype(f32) + second[...].astype(f32)
    total[...] = (mine[...] + both).astype(total.dtype)


def qkv_input_grad(grads, w_qkv, dres, mine, mine_x, send, full):
    me = lax.axis_index("hid")
    feats = mine.shape[0]
    block = dres.shape[0]
    total = None
    for c in range(3):
        part = dot(jnp.transpose(w_qkv[c]), grads[c * feats : (c + 1) * feats, :])
        total = part if total is None else total + part
    full[...] = total
    full[:, at(me, block)] += jnp.transpose(dres[...])
    send[:feats, :] = full[at(me ^ 1, feats), :].astype(bf16)
    send[feats:, :] = full[at(me ^ 3, feats), :].astype(bf16)
    mine[...] = full[at(me, feats), :]
    mine_x[...] = full[at(me ^ 2, feats), :]


def place_rows(own, from_core, from_x, far, whole):
    me, n = lax.axis_index("hid"), own.shape[0]
    for k, piece in enumerate((own, from_core, from_x, far)):
        whole[at(me ^ k, n), :] = piece[...]


def row_norm(values):
    mean = jnp.mean(values, axis=1, keepdims=True)
    centered = values - mean
    spread = jnp.mean(centered * centered, axis=1, keepdims=True)
    inv = lax.rsqrt(spread + norm_eps)
    return centered * inv, inv


def attn_out(
    branch, g0, g1, g2, g3, x_block, vecs, wo,
    normed, normed_low, hat, inv_out, pre, gated_rows, heads_all,
):
    me = lax.axis_index("hid")
    feats = g0.shape[0]
    for k, piece in enumerate((g0, g1, g2.at[:feats, :], g3.at[feats:, :])):
        heads_all[at(me ^ k, feats), :] = piece[...]
    gated = jnp.transpose(heads_all[...])
    gated_rows[...] = gated
    tokens = jnp.transpose(x_block[...].astype(f32))
    attn = dot_nt(gated, wo[...]) + vecs[0:1, :]
    pre[...] = attn
    resid = tokens + branch[0] * attn * vecs[3:4, :]
    x_hat, inv = row_norm(resid)
    value = x_hat * vecs[1:2, :] + vecs[2:3, :]
    normed_low[...] = value.astype(bf16)
    normed[...] = value
    hat[...] = x_hat
    inv_out[...] = jnp.broadcast_to(inv, inv_out.shape)


def attn_out_back(
    branch, part, recv, dres2, hat, inv, pre, vecs, wo,
    dres, grad_attn, sums, up_mine, up_core, up_x, ups,
):
    me = lax.axis_index("hid")
    feats = up_mine.shape[0]
    grad = part[...] + recv[...].astype(f32) + dres2[...]
    x_hat = hat[...]
    scaled = grad * vecs[1:2, :]
    mean_plain = jnp.mean(scaled, axis=1, keepdims=True)
    mean_along = jnp.mean(scaled * x_hat, axis=1, keepdims=True)
    grad_resid = inv[:, 0:1] * (scaled - mean_plain - x_hat * mean_along)
    dres[...] = grad_resid
    low = (grad_resid * (branch[0] * vecs[3:4, :])).astype(bf16)
    grad_attn[...] = low
    grad_gated = dot(low, wo[...])
    upstream = (grad_gated * vecs[7:8, :]).astype(bf16)
    ups[...] = jnp.transpose(upstream)
    up_mine[...] = ups[at(me, feats), :]
    up_core[...] = ups[at(me ^ 1, feats), :]
    up_x[:feats, :] = ups[at(me ^ 2, feats), :]
    up_x[feats:, :] = ups[at(me ^ 3, feats), :]
    sums[0:1, :] = jnp.sum(grad * x_hat, axis=0, keepdims=True)
    sums[1:2, :] = jnp.sum(grad, axis=0, keepdims=True)
    sums[2:3, :] = jnp.sum(low.astype(f32), axis=0, keepdims=True)
    sums[3:4, :] = jnp.sum(grad_resid * pre[...], axis=0, keepdims=True)


def out_weight_grad(grad_attn, gated_rows, mine, mine_x, send, full):
    me = lax.axis_index("hid")
    feats = mine.shape[0]
    full[...] = dot_tn(grad_attn[...], gated_rows[...])
    send[:feats, :] = full[at(me ^ 1, feats), :].astype(bf16)
    send[feats:, :] = full[at(me ^ 3, feats), :].astype(bf16)
    mine[...] = full[at(me, feats), :]
    mine_x[...] = full[at(me ^ 2, feats), :]


def cut_inputs(w_back, cotangent, back_half, cot_send):
    other, parity = 1 - lax.axis_index("hid") // 2, lax.axis_index("rows") & 1
    back_half[...] = w_back[:, at(2 * other + parity, back_half.shape[1])]
    cot_send[...] = cotangent[:, at(other, cot_send.shape[1])]


def place_units(wi_own, wi_core, own, core_rows, xa, xb, fa, fb, wi, wb):
    me, core, chip, parity = lax.axis_index("hid"), lax.axis_index("hid") & 1, lax.axis_index("hid") // 2, lax.axis_index("rows") & 1
    n, half = xa.shape
    units = wi_own.shape[1]
    wi[:, at(core, units)] = wi_own[...]
    wi[:, at(core ^ 1, units)] = wi_core[...]
    wb[at(me, n), :] = own[:, at(chip, 2 * half)]
    wb[at(me ^ 1, n), :] = core_rows[:, at(chip, 2 * half)]
    for owner, first, second in ((me ^ 2, xa, xb), (me ^ 3, fa, fb)):
        wb[at(owner, n), at(parity, half)] = first[...]
        wb[at(owner, n), at(parity ^ 1, half)] = second[...]


def ffn_forward(
    rows, unit_rows, wi, wb, act, slope, inter_mine, inter_core, part, inter,
):
    ffn_units(rows, unit_rows, wi, act, slope, inter_mine, inter_core, inter)
    part[...] = dot_nt(inter[...], wb[...])


def ffn_forward_far(
    rows, unit_rows, wi, wb, core_mine, act, slope, inter_mine, part, core_pair, inter,
):
    n = rows.shape[0]
    core_pair[:n, :] = core_mine[...]
    ffn_units(rows, unit_rows, wi, act, slope, inter_mine, core_pair.at[n:, :], inter)
    part[...] = dot_nt(inter[...], wb[...]).astype(part.dtype)


def ffn_units(rows, unit_rows, wi, act, slope, inter_mine, inter_core, inter):
    core = lax.axis_index("hid") & 1
    units = wi.shape[1]
    step = 256
    for j in range(units // step):
        cut = slice(j * step, (j + 1) * step)
        u = dot(rows[...], wi[:, cut]) + unit_rows[0:1, cut]
        cdf = 0.5 * (1.0 + lax.erf(u * 0.7071067811865476))
        value = u * cdf
        act[:, cut] = value
        slope[:, cut] = cdf + u * (jnp.exp(-0.5 * u * u) * 0.3989422804014327)
        inter[:, cut] = (value * unit_rows[1:2, cut]).astype(bf16)
    inter_mine[...] = inter[:, at(core, units // 2)]
    inter_core[...] = inter[:, at(core ^ 1, units // 2)]


def ffn_backward(
    rows, act, slope, unit_rows, wi, wb, gpre_mine, gpre_core, part, sums, gpre,
):
    ffn_units_back(rows, act, slope, unit_rows, wb, gpre_mine, gpre_core, sums, gpre)
    part[...] = dot_nt(gpre[...], wi[...])


def ffn_backward_far(
    rows, act, slope, unit_rows, wi, wb, core_mine,
    gpre_mine, part, sums, core_pair, gpre,
):
    n = rows.shape[0]
    core_pair[:n, :] = core_mine[...]
    ffn_units_back(
        rows, act, slope, unit_rows, wb, gpre_mine, core_pair.at[n:, :], sums, gpre
    )
    part[...] = dot_nt(gpre[...], wi[...]).astype(part.dtype)


def ffn_units_back(rows, act, slope, unit_rows, wb, gpre_mine, gpre_core, sums, gpre):
    core = lax.axis_index("hid") & 1
    units = wb.shape[1]
    step = 256
    for j in range(units // step):
        cut = slice(j * step, (j + 1) * step)
        ginter = dot(rows[...], wb[:, cut])
        sums[:, cut] = jnp.broadcast_to(
            jnp.sum(ginter * act[:, cut], axis=0, keepdims=True), (8, step)
        )
        gpre[:, cut] = (ginter * unit_rows[1:2, cut] * slope[:, cut]).astype(bf16)
    gpre_mine[...] = gpre[:, at(core, units // 2)]
    gpre_core[...] = gpre[:, at(core ^ 1, units // 2)]


def ffn_weight_grads(
    n0, n1, n2, n3, e0, e1, e_core, p0, p1, p_core, f0, f1, f2, f3,
    in_keep, in_send, back_keep, back_send, bias_sums, left, right, full,
):
    parity = lax.axis_index("rows") & 1
    in_parity = (lax.axis_index("rows") >> 1) & 1
    half = full.shape[0] // 2

    def fill(target, pieces):
        start = 0
        for piece in pieces:
            target[start : start + piece.shape[0], :] = piece[...]
            start += piece.shape[0]

    fill(left, (f0, f1, f2, f3))
    fill(right, (e0, e1, e_core))
    full[...] = dot_tn(left[...], right[...])
    owners, subs = 4, 8
    rows = full.shape[0] // (owners * subs)
    for q in range(subs // 2):
        for h in range(owners):
            to = slice((q * owners + h) * rows, (q * owners + h + 1) * rows)
            base = h * subs * rows + q * rows
            kept = base + parity * (subs // 2) * rows
            sent = base + (parity ^ 1) * (subs // 2) * rows
            back_keep[to, :] = full[pl.ds(pl.multiple_of(kept, rows), rows), :]
            left_rows = full[pl.ds(pl.multiple_of(sent, rows), rows), :]
            back_send[to, :] = left_rows.astype(bf16)
    fill(left, (n0, n1, n2, n3))
    fill(right, (p0, p1, p_core))
    full[...] = dot_tn(left[...], right[...])
    in_send[...] = full[at(in_parity ^ 1, half), :].astype(bf16)
    in_keep[...] = full[at(in_parity, half), :]
    bias_sums[...] = jnp.broadcast_to(
        jnp.sum(right[...].astype(f32), axis=0, keepdims=True), bias_sums.shape
    )


def second_norm(
    branch, part, recv, normed, cot0, cot1, cot2, cot3, vecs,
    grad_low, dres, sums, out_mine, out_x, out_send, cots, outs,
):
    me = lax.axis_index("hid")
    feats = cot0.shape[0]
    block = part.shape[0]
    core = me & 1
    cots[at(me, feats), :] = cot0[:, at(me, block)]
    cots[at(me ^ 1, feats), :] = cot1[:, at(me, block)]
    cots[at(me ^ 2, feats), :] = cot2[:, at(core, block)]
    cots[at(me ^ 3, feats), :] = cot3[:, at(core, block)]
    ffn = part[...] + recv[...].astype(f32) + vecs[4:5, :]
    resid = normed[...] + branch[1] * ffn * vecs[3:4, :]
    x_hat, inv = row_norm(resid)
    grad_out = jnp.transpose(cots[...].astype(f32))
    scaled = grad_out * vecs[5:6, :]
    mean_plain = jnp.mean(scaled, axis=1, keepdims=True)
    mean_along = jnp.mean(scaled * x_hat, axis=1, keepdims=True)
    grad_resid = inv * (scaled - mean_plain - x_hat * mean_along)
    low = (grad_resid * (branch[1] * vecs[3:4, :])).astype(bf16)
    grad_low[...] = low
    dres[...] = grad_resid
    value = x_hat * vecs[5:6, :] + vecs[6:7, :]
    outs[...] = jnp.transpose(value).astype(bf16)
    out_mine[...] = outs[at(me, feats), :]
    out_x[...] = outs[at(me ^ 2, feats), :]
    out_send[:feats, :] = outs[at(me ^ 1, feats), :]
    out_send[feats:, :] = outs[at(me ^ 3, feats), :]
    sums[0:1, :] = jnp.sum(grad_out * x_hat, axis=0, keepdims=True)
    sums[1:2, :] = jnp.sum(grad_out, axis=0, keepdims=True)
    sums[2:3, :] = jnp.sum(low.astype(f32), axis=0, keepdims=True)
    sums[3:4, :] = jnp.sum(grad_resid * ffn, axis=0, keepdims=True)


def pack_vectors(
    head_gate, b_out, gain, bias, hidden_gate, hidden_mask, b_back, b_in, inter_gate, b_qv,
    packed, qv,
):
    feats = b_out.shape[0]

    def row(ref):
        return ref[...].reshape(1, ref.shape[0])

    packed[...] = jnp.zeros_like(packed)
    packed[0:1, :feats] = row(b_out)
    packed[1:2, :feats] = gain[0:1, :]
    packed[2:3, :feats] = bias[0:1, :]
    packed[3:4, :feats] = row(hidden_gate) * row(hidden_mask).astype(f32)
    packed[4:5, :feats] = row(b_back)
    packed[5:6, :feats] = gain[1:2, :]
    packed[6:7, :feats] = bias[1:2, :]
    packed[7:8, :feats] = jnp.concatenate(
        [jnp.full((1, HEAD_DIM), head_gate[i], f32) for i in range(feats // HEAD_DIM)], axis=1
    )
    packed[0:1, 256:] = row(b_in)
    packed[1:2, 256:] = row(inter_gate)
    qv[...] = jnp.zeros_like(qv)
    qv[0:2, :feats] = b_qv[...]


def place_vectors(p0, p1, p2, p3, vecs, unit_rows, cols):
    me, core = lax.axis_index("hid"), lax.axis_index("hid") & 1
    feats = cols.shape[0] // 4
    units = p0.shape[1] - 256
    for k, piece in enumerate((p0, p1, p2, p3)):
        cols[at(me ^ k, feats), :] = jnp.transpose(piece[:, :256])[:feats, :]
    vecs[...] = jnp.transpose(cols[...])
    unit_rows[:, at(core, units)] = p0[0:2, 256:]
    unit_rows[:, at(core ^ 1, units)] = p1[0:2, 256:]


def pack_sums(sums1, sums2, ig0, ig1, bin_sum, keep, send):
    core = lax.axis_index("hid") & 1
    units = keep.shape[1]
    keep[0:4, :] = sums1[...]
    keep[4:8, :] = sums2[...]
    keep[8:, :] = jnp.zeros((keep.shape[0] - 8, units), f32)
    send[...] = keep[...]
    keep[8:9, :] = ig0[0:1, at(core, units)] + ig1[0:1, at(core, units)]
    send[8:9, :] = ig0[0:1, at(core ^ 1, units)] + ig1[0:1, at(core ^ 1, units)]
    keep[9:10, :] = bin_sum[0:1, :]


def add_rows(mine, other, total):
    total[...] = mine[...] + other[...]


def last_sums(shared, other, head_sums, bias_sums, total):
    total[...] = shared[...]
    total[0:8, :] += other[0:8, :]
    width = bias_sums.shape[1]
    total[10:11, :width] = bias_sums[0:1, :]
    heads = jnp.sum(jnp.transpose(head_sums[...]), axis=0, keepdims=True)
    total[11:12, :8] = heads


def vector_outputs(
    branch, head_gate, vec, vecs, hidden_mask,
    g_qv, g_bout, g_bin, g_bback, g_gain, g_bias, g_head, g_inter, g_branch, g_hidden, cols,
):
    me = lax.axis_index("hid")
    feats = g_bout.shape[0]
    cols[...] = jnp.transpose(vec[0:8, :])
    own = jnp.transpose(cols[at(me, feats), :])
    g_gain[0:1, :] = own[0:1, :]
    g_gain[1:2, :] = own[4:5, :]
    g_bias[0:1, :] = own[1:2, :]
    g_bias[1:2, :] = own[5:6, :]
    g_bout[...] = own[2, :]
    g_bback[...] = own[6, :]
    mask = hidden_mask[...].astype(f32)
    g_hidden[...] = (branch[0] * own[3, :] + branch[1] * own[7, :]) * mask
    g_inter[...] = vec[8, :]
    g_bin[...] = vec[9, :]
    g_qv[0:1, :] = vec[10:11, :feats]
    rolled = vec[10:11, 2 * feats : 3 * feats]
    g_qv[1:2, :] = rolled
    lane = lax.broadcasted_iota(jnp.int32, (1, 128), 1)
    gates = jnp.ones((1, 128), f32)
    for i in range(feats // HEAD_DIM):
        gates = jnp.where(lane == i, head_gate[i], gates)
    g_head[...] = (vec[11:12, :128] / gates)[0, : feats // HEAD_DIM]
    part0 = jnp.sum(vec[3:4, :] * vecs[3:4, :], axis=1, keepdims=True)
    part1 = jnp.sum(vec[7:8, :] * vecs[3:4, :], axis=1, keepdims=True)
    both = jnp.where(lane == 0, part0, part1)
    g_branch[...] = both[0, :2]


def row_step(k):
    def body(keep, recv, keep_next, send_next):
        bit = (lax.axis_index("rows") >> k) & 1
        n = keep_next.shape[0]
        sent = keep[at(bit ^ 1, n), :] + recv[at(bit ^ 1, n), :].astype(f32)
        send_next[...] = sent.astype(bf16)
        keep_next[...] = keep[at(bit, n), :] + recv[at(bit, n), :].astype(f32)

    return body


def along(block, bit):
    return swap(block, "rows", 1 << bit)


def reduce_step(keep, recv, bit, gate):
    n, width = keep.shape
    return local_kernel(
        row_step(bit),
        "row_step",
        (after(keep, *gate), recv),
        "VV",
        [sds((n // 2, width), f32), sds((n // 2, width), bf16)],
    )


def far_rows_sum(chunk):
    count = lax.axis_size("rows")
    if count == 8:
        return chunk
    groups = [[i + 8 * j for j in range(count // 8)] for i in range(8)]
    return lax.psum(chunk, "rows", axis_index_groups=groups)


def last_step(keep, recv, gate):
    kind = bf16 if lax.axis_size("rows") == 8 else f32
    (chunk,) = local_kernel(
        add_low, "last_step", (after(keep, *gate), recv), "VV", [sds(keep.shape, kind)]
    )
    return far_rows_sum(chunk).astype(bf16)


def in_order(k):
    def body(mine, other, both):
        bit = (lax.axis_index("rows") >> k) & 1
        n = mine.shape[0]
        both[at(bit, n), :] = mine[...]
        both[at(bit ^ 1, n), :] = other[...]

    return body


def join_step(mine, other, bit, gate):
    n, width = mine.shape
    (both,) = local_kernel(
        in_order(bit), "in_order", (after(mine, *gate), other), "VV", [sds((2 * n, width), bf16)]
    )
    return both


def in_gradient(k):
    def body(mine, other, grad):
        bit = (lax.axis_index("rows") >> k) & 1
        n = mine.shape[0]
        grad[at(bit, n), :] = mine[...].astype(f32)
        grad[at(bit ^ 1, n), :] = other[...].astype(f32)

    return body


def back_gradient(mine, other, grad, wide):
    bit = lax.axis_index("rows") & 1
    units = mine.shape[1]
    rows = grad.shape[0] // 8
    for side, half in ((bit, mine), (bit ^ 1, other)):
        wide[...] = half[...].astype(f32)
        for q in range(4):
            for owner in range(4):
                block = wide[(q * 4 + owner) * rows : (q * 4 + owner + 1) * rows, :]
                to = pl.ds(pl.multiple_of((side * 4 + q) * rows, rows), rows)
                grad[to, owner * units : (owner + 1) * units] = block


def attn_gradients(qk_mine, qk_other, vo_mine, vo_other, grad_qkv, grad_out):
    y, z = lax.axis_index("rows") & 1, (lax.axis_index("rows") >> 1) & 1
    n = qk_mine.shape[0]
    grad_qkv[at(y, n), :] = qk_mine[...].astype(f32)
    grad_qkv[at(y ^ 1, n), :] = qk_other[...].astype(f32)
    mine, other = vo_mine[...].astype(f32), vo_other[...].astype(f32)
    grad_qkv[2 * n :, :] = jnp.where(z == 0, mine, other)
    grad_out[...] = jnp.where(z == 0, other, mine)


def split_owners(keep, recv, mine, mine_x, send, full):
    me = lax.axis_index("hid")
    n = mine.shape[0]
    full[...] = keep[...] + recv[...].astype(f32)
    mine[...] = full[at(me, n), :]
    mine_x[...] = full[at(me ^ 2, n), :]
    send[:n, :] = full[at(me ^ 1, n), :]
    send[n:, :] = full[at(me ^ 3, n), :]


def join_owners(mine, from_core, from_x, chunk, full):
    me, n = lax.axis_index("hid"), mine.shape[0]
    full[at(me, n), :] = mine[...]
    full[at(me ^ 1, n), :] = from_core[:n, :]
    full[at(me ^ 2, n), :] = from_x[:n, :]
    full[at(me ^ 3, n), :] = from_x[n:, :]
    chunk[...] = full[...].astype(chunk.dtype)


def second_half(mine, recv, both):
    n = mine.shape[0]
    both[:n, :] = mine[...]
    both[n:, :] = recv[n:, :]


def place_blocks(mine, from_core, from_x, whole):
    me = lax.axis_index("hid")
    rows, n = mine.shape
    whole[:, at(me, n)] = mine[...]
    whole[:, at(me ^ 1, n)] = from_core[:rows, :]
    whole[:, at(me ^ 2, n)] = from_x[:rows, :]
    whole[:, at(me ^ 3, n)] = from_x[rows:, :]


def shards(
    tokens, w_qkv, b_qv, w_out, b_out, w_in, b_in, w_back, b_back, norm_gain, norm_bias,
    head_gate, inter_gate, branch_gate, hidden_gate, hidden_mask, doc_lengths, cotangent,
):
    feats, toks = tokens.shape
    width = 4 * feats
    units = w_in.shape[1]
    block = toks // 4
    tokens_x = swap(tokens, "hid", 2)
    tokens_core = swap(tokens, "hid", 1)
    out_x = swap(w_out, "hid", 2)
    back_half, cot_send = local_kernel(
        cut_inputs,
        "cut_inputs",
        (w_back, cotangent),
        "VV",
        [sds((feats, units), bf16), sds((feats, 2 * block), bf16)],
    )
    back_xa = swap(back_half, "hid", 2)
    wi_core = swap(w_in, "hid", 1)
    wo_core = swap(w_out, "hid", 1)
    cot_core = swap(cotangent, "hid", 1)
    back_core = swap(w_back, "hid", 1)
    packed, qv_rows = local_kernel(
        pack_vectors,
        "pack_vectors",
        (
            head_gate, b_out, norm_gain, norm_bias, hidden_gate, hidden_mask, b_back,
            b_in, inter_gate, b_qv,
        ),
        "S" + "V" * 9,
        [sds((8, 256 + units), f32), sds((8, 256), f32)],
    )
    tokens_far = swap(
        after(tokens_x, tokens_core, wi_core, wo_core, cot_core, back_core, back_half), "hid", 1
    )

    head_block = sds((feats, block), bf16)
    two_blocks = sds((2 * feats, block), bf16)
    x_all, qkv, logsum, g0, g_core, g_x, x_block = local_kernel(
        attn_forward,
        "attn_forward",
        (
            doc_lengths, head_gate, qv_rows,
            tokens, tokens_core, tokens_x, tokens_far, w_qkv,
        ),
        "SSVVVVVV",
        [
            sds((width, toks), bf16),
            sds((3, feats, toks), bf16),
            sds((8, toks), f32),
            head_block,
            head_block,
            two_blocks,
            sds((width, block), bf16),
        ],
        [pltpu.VMEM((feats, toks), bf16)],
        micros=5.4,
    )
    g2 = swap(g_x, "hid", 2)
    g1 = swap(g_core, "hid", 1)
    packed_x = swap(after(packed, g0), "hid", 2)
    packed_core = swap(after(packed, g0), "hid", 1)
    g3 = swap(after(g2, packed_x, packed_core), "hid", 1)
    packed_far = swap(packed_x, "hid", 1)
    out_far = swap(after(out_x, g0), "hid", 1)
    back_xb = swap(after(back_xa, g1), "rows", 1)
    back_fa = swap(after(back_xa, g1), "hid", 1)
    cot_x = swap(after(cot_send, g1), "hid", 2)
    (wo,) = local_kernel(
        place_rows,
        "place_rows",
        (w_out, wo_core, out_x, out_far),
        "VVVV",
        [sds((width, width), bf16)],
    )
    vecs, unit_rows = local_kernel(
        place_vectors,
        "place_vectors",
        (after(packed, cot_x), packed_core, packed_x, packed_far),
        "VVVV",
        [sds((8, width), f32), sds((2, 2 * units), f32)],
        [pltpu.VMEM((width, 8), f32)],
    )

    normed, normed_low, hat, inv, attn_pre, gated_rows = local_kernel(
        attn_out,
        "attn_out",
        (branch_gate, g0, g1, g2, g3, x_block, vecs, wo),
        "SVVVVVVV",
        [
            sds((block, width), f32),
            sds((block, width), bf16),
            sds((block, width), f32),
            sds((block, 128), f32),
            sds((block, width), f32),
            sds((block, width), bf16),
        ],
        [pltpu.VMEM((width, block), bf16)],
        micros=1.3,
    )

    normed_x = swap(normed_low, "hid", 2)
    n2 = swap(normed_low, "hid", 1)
    back_fb = swap(after(back_xb, normed_x), "hid", 1)
    wi, wb = local_kernel(
        place_units,
        "place_units",
        (w_in, wi_core, w_back, back_core, back_xa, back_xb, back_fa, back_fb),
        "V" * 8,
        [sds((width, 2 * units), bf16), sds((width, 2 * units), bf16)],
        micros=0.85,
    )

    act_block = sds((block, 2 * units), f32)
    half_block = sds((block, units), bf16)
    pair_block = sds((2 * block, units), bf16)
    rows_block = sds((block, width), bf16)
    ffn_scratch = [pltpu.VMEM((block, 2 * units), bf16)]
    act, slope, e0, inter_core, ffn_part = local_kernel(
        ffn_forward,
        "ffn_forward",
        (normed_low, unit_rows, wi, wb),
        "VVVV",
        [act_block, act_block, half_block, half_block, sds((block, width), f32)],
        ffn_scratch,
        micros=1.85,
    )
    act_x, slope_x, e1, ffn_send, e_pair = local_kernel(
        ffn_forward_far,
        "ffn_forward_far",
        (normed_x, unit_rows, wi, wb, inter_core),
        "VVVVV",
        [act_block, act_block, half_block, rows_block, pair_block],
        ffn_scratch,
        micros=1.85,
    )
    ffn_recv = swap(ffn_send, "hid", 2)
    cot_far = swap(after(cot_x, normed_x), "hid", 1)
    n3 = swap(after(normed_x, ffn_send), "hid", 1)
    e_core = swap(after(e_pair, ffn_send), "hid", 1)

    out_block = sds((feats, block), bf16)
    gffn, dres2, sums2, res_mine, res_x, res_send = local_kernel(
        second_norm,
        "second_norm",
        (
            branch_gate, after(ffn_part, n3, e_core), ffn_recv, normed,
            cotangent, cot_core, cot_x, cot_far, vecs,
        ),
        "S" + "V" * 8,
        [
            sds((block, width), bf16),
            sds((block, width), f32),
            sds((4, width), f32),
            out_block,
            out_block,
            sds((2 * feats, block), bf16),
        ],
        [pltpu.VMEM((width, block), bf16), pltpu.VMEM((width, block), bf16)],
        micros=1.2,
    )

    gffn_x = swap(gffn, "hid", 2)
    f2 = swap(gffn, "hid", 1)
    sums_block = sds((8, 2 * units), f32)
    p0, gpre_core, gn_part, ig_sum = local_kernel(
        ffn_backward,
        "ffn_backward",
        (gffn, act, slope, unit_rows, wi, wb),
        "VVVVVV",
        [half_block, half_block, sds((block, width), f32), sums_block],
        ffn_scratch,
        micros=1.85,
    )
    p1, gn_send, ig_sum_x, p_pair = local_kernel(
        ffn_backward_far,
        "ffn_backward_far",
        (after(gffn_x, f2), act_x, slope_x, unit_rows, wi, wb, gpre_core),
        "VVVVVVV",
        [half_block, rows_block, sums_block, pair_block],
        ffn_scratch,
        micros=1.85,
    )
    gn_recv = swap(gn_send, "hid", 2)
    f3 = swap(after(gffn_x, gn_send), "hid", 1)
    p_core = swap(p_pair, "hid", 1)
    in_keep, in_send, back_keep, back_send, bin_sum = local_kernel(
        ffn_weight_grads,
        "ffn_weight_grads",
        (
            normed_low, normed_x, n2, n3, e0, e1, e_core,
            p0, p1, p_core, gffn, gffn_x, f2, f3,
        ),
        "V" * 14,
        [
            sds((width // 2, units), f32),
            sds((width // 2, units), bf16),
            sds((width // 2, units), f32),
            sds((width // 2, units), bf16),
            sds((8, units), f32),
        ],
        [
            pltpu.VMEM((toks, width), bf16),
            pltpu.VMEM((toks, units), bf16),
            pltpu.VMEM((width, units), f32),
        ],
        micros=2.5,
    )

    back_recv = swap(after(back_send, gn_recv), "rows", 1)
    in_recv = swap(after(in_send, gn_recv), "rows", 2)

    dres1, gattn, sums1, u0, up_core, up_x = local_kernel(
        attn_out_back,
        "attn_out_back",
        (
            branch_gate, after(gn_part, in_send), gn_recv, dres2, hat, inv, attn_pre,
            vecs, wo,
        ),
        "S" + "V" * 8,
        [
            sds((block, width), f32),
            sds((block, width), bf16),
            sds((4, width), f32),
            head_block,
            head_block,
            two_blocks,
        ],
        [pltpu.VMEM((width, block), bf16)],
        micros=1.3,
    )
    u2 = swap(up_x, "hid", 2)
    u1 = swap(up_core, "hid", 1)
    u3 = swap(u2, "hid", 1)

    weight_block = sds((feats, width), f32)
    low_block = sds((feats, width), bf16)
    wo_mine, wo_keep, wo_send = local_kernel(
        out_weight_grad,
        "out_weight_grad",
        (gattn, gated_rows),
        "VV",
        [weight_block, weight_block, sds((2 * feats, width), bf16)],
        [pltpu.VMEM((width, width), f32)],
        micros=1.2,
    )
    wo_grad_core = swap(after(wo_send, u1), "hid", 1)

    grads, head_sums, bias_sums = local_kernel(
        attn_backward,
        "attn_backward",
        (doc_lengths, qkv, logsum, u0, u1, u2, u3),
        "SVVVVVV",
        [
            sds((3 * feats, toks), bf16),
            sds((8, block), f32),
            sds((8, 3 * feats), f32),
        ],
        [pltpu.VMEM((feats, toks), bf16)],
        micros=5.0,
    )
    (wo_low,) = local_kernel(add_second, "wo_low", (wo_keep, wo_grad_core), "VV", [low_block])
    wo_far = swap(after(wo_low, u3), "hid", 2)

    qk_keep, qk_send = local_kernel(
        qk_weight_grad,
        "qk_weight_grad",
        (grads, x_all),
        "VV",
        [weight_block, low_block],
        [pltpu.VMEM((2 * feats, width), f32)],
        micros=1.2,
    )
    vo_keep, vo_send = local_kernel(
        vo_weight_grad,
        "vo_weight_grad",
        (after(grads, qk_send), x_all, wo_mine, wo_grad_core, wo_far),
        "VVVVV",
        [weight_block, low_block],
        [pltpu.VMEM((2 * feats, width), f32)],
        micros=1.1,
    )
    gx_block = sds((feats, toks), f32)
    gx_low = sds((feats, toks), bf16)
    gx_mine, gx_x, gx_send = local_kernel(
        qkv_input_grad,
        "qkv_input_grad",
        (after(grads, vo_send), w_qkv, dres1),
        "VVV",
        [gx_block, gx_block, sds((2 * feats, toks), bf16)],
        [pltpu.VMEM((width, toks), f32)],
        micros=1.5,
    )
    gx_core = swap(gx_send, "hid", 1)
    (gx_send,) = local_kernel(add_second, "gx_send", (gx_x, gx_core), "VV", [gx_low])
    gx_far = swap(gx_send, "hid", 2)
    res_core = swap(after(res_send, grads), "hid", 1)
    (res_send,) = local_kernel(
        second_half, "out_join", (res_x, res_core), "VV", [sds((2 * feats, block), bf16)]
    )
    rows16 = sds((16, units), f32)
    vec_keep, vec_send = local_kernel(
        pack_sums,
        "pack_sums",
        (sums1, sums2, ig_sum, ig_sum_x, bin_sum),
        "VVVVV",
        [rows16, rows16],
    )

    def vector_step(vec, hop, body=add_rows, *more):
        (vec,) = local_kernel(body, body.__name__, (vec, hop) + more, "VV" + "V" * len(more), [rows16])
        return vec

    y, z, far = 0, 1, 2
    qk_recv = along(qk_send, y)
    vo_recv = along(vo_send, z)
    turn = (qk_send, vo_send)
    back_keep, back_send = reduce_step(back_keep, back_recv, z, turn)
    in_keep, in_send = reduce_step(in_keep, in_recv, y, turn)
    back_recv, in_recv = along(back_send, z), along(in_send, y)
    vec_hop = swap(after(vec_send, vo_send), "hid", 1)
    turn = (back_send, in_send, gx_core, vec_hop)
    qk_keep, qk_send = reduce_step(qk_keep, qk_recv, z, turn)
    vo_keep, vo_send = reduce_step(vo_keep, vo_recv, y, turn)
    qk_recv, vo_recv = along(qk_send, z), along(vo_send, y)
    vec = vector_step(vec_keep, vec_hop)
    vec_hop = swap(vec, "hid", 2)
    turn = (qk_send, vo_send, gx_far, vec_hop)
    back_keep, back_send = reduce_step(back_keep, back_recv, far, turn)
    in_keep, in_send = reduce_step(in_keep, in_recv, far, turn)
    back_recv, in_recv = along(back_send, far), along(in_send, far)
    vec = vector_step(vec, vec_hop, last_sums, head_sums, bias_sums)
    vec_hop = along(vec, y)
    res_far = swap(after(res_send, gx_far), "hid", 2)
    turn = (back_send, in_send, res_far)
    qk_keep, qk_send = reduce_step(qk_keep, qk_recv, far, turn)
    vo_keep, vo_send = reduce_step(vo_keep, vo_recv, far, turn)
    qk_recv, vo_recv = along(qk_send, far), along(vo_send, far)

    turn = (qk_send, vo_send, vec_hop)
    sub = sds((back_keep.shape[0] // 4, units), f32)
    two = sds((back_keep.shape[0] // 2, units), f32)
    back_keep = after(back_keep, *turn)
    if lax.axis_size("rows") > 8:
        back_keep = far_rows_sum(back_keep + back_recv.astype(f32))
        back_recv = jnp.zeros_like(back_recv)
    b_mine, b_x, b_send = local_kernel(
        split_owners,
        "split_owners",
        (back_keep, back_recv),
        "VV",
        [sub, sub, two],
        [pltpu.VMEM(back_keep.shape, f32)],
    )
    b_core = swap(b_send, "hid", 1)
    in_mine = last_step(in_keep, in_recv, turn)
    in_other = along(in_mine, far)
    (b_send,) = local_kernel(second_half, "back_join", (b_x, b_core), "VV", [two])
    b_far = swap(b_send, "hid", 2)
    vec = vector_step(vec, vec_hop)
    vec_hop = along(vec, z)
    turn = (in_mine, b_send)
    qk_mine = last_step(qk_keep, qk_recv, turn)
    vo_mine = last_step(vo_keep, vo_recv, turn)
    qk_other, vo_other = along(qk_mine, far), along(vo_mine, far)
    turn = (qk_mine, vo_mine, vec_hop)
    (back_mine,) = local_kernel(
        join_owners,
        "join_owners",
        (after(b_mine, *turn), b_core, b_far),
        "VVV",
        [sds(back_keep.shape, bf16)],
        [pltpu.VMEM(back_keep.shape, f32)],
    )
    back_other = along(back_mine, far)
    in_mine = join_step(in_mine, in_other, far, turn)
    in_other = along(in_mine, y)
    vec = vector_step(vec, vec_hop)
    vec_hop = along(vec, far)
    turn = (back_mine, in_mine)
    qk_mine = join_step(qk_mine, qk_other, far, turn)
    vo_mine = join_step(vo_mine, vo_other, far, turn)
    qk_other, vo_other = along(qk_mine, z), along(vo_mine, y)
    turn = (qk_mine, vo_mine, vec_hop)
    back_mine = join_step(back_mine, back_other, far, turn)
    back_other = along(back_mine, z)
    in_mine = join_step(in_mine, in_other, y, turn)
    in_other = along(in_mine, z)
    vec = vector_step(vec, vec_hop)
    turn = (back_mine, in_mine)
    qk_mine = join_step(qk_mine, qk_other, z, turn)
    vo_mine = join_step(vo_mine, vo_other, y, turn)
    qk_other, vo_other = along(qk_mine, y), along(vo_mine, z)
    turn = (qk_mine, vo_mine)
    back_mine = join_step(back_mine, back_other, z, turn)
    back_other = along(back_mine, y)
    (grad_w_in,) = local_kernel(
        in_gradient(z),
        "in_gradient",
        (in_mine, in_other),
        "VV",
        [sds((width, units), f32)],
        micros=2.1,
    )
    grad_qkv, grad_w_out = local_kernel(
        attn_gradients,
        "attn_gradients",
        (qk_mine, qk_other, vo_mine, vo_other),
        "VVVV",
        [sds((3 * feats, width), f32), weight_block],
        micros=2.1,
    )
    (grad_w_back,) = local_kernel(
        back_gradient,
        "back_gradient",
        (back_mine, back_other),
        "VV",
        [sds((feats, 4 * units), f32)],
        [pltpu.VMEM(back_mine.shape, f32)],
        micros=2.1,
    )
    grad_w_qkv = grad_qkv.reshape(3, feats, width)

    (grad_tokens,) = local_kernel(add_two, "grad_tokens", (gx_mine, gx_core, gx_far), "VVV", [gx_low])
    (output,) = local_kernel(
        place_blocks,
        "place_blocks",
        (res_mine, res_core, res_far),
        "VVV",
        [sds((feats, toks), bf16)],
        micros=1.2,
    )

    vec = far_rows_sum(vec)
    (
        grad_b_qv, grad_b_out, grad_b_in, grad_b_back, grad_norm_gain, grad_norm_bias,
        grad_head_gate, grad_inter_gate, grad_branch_gate, grad_hidden_gate,
    ) = local_kernel(
        vector_outputs,
        "vector_outputs",
        (branch_gate, head_gate, vec, vecs, hidden_mask),
        "SSVVV",
        [
            sds((2, feats), f32),
            sds((feats,), f32),
            sds((units,), f32),
            sds((feats,), f32),
            sds((2, feats), f32),
            sds((2, feats), f32),
            sds((feats // HEAD_DIM,), f32),
            sds((units,), f32),
            sds((2,), f32),
            sds((feats,), f32),
        ],
        [pltpu.VMEM((width, 8), f32)],
        micros=1.4,
    )
    return (
        output,
        grad_tokens,
        grad_w_qkv,
        grad_b_qv,
        grad_w_out,
        grad_b_out,
        grad_w_in,
        grad_b_in,
        grad_w_back,
        grad_b_back,
        grad_norm_gain,
        grad_norm_bias,
        grad_head_gate,
        grad_inter_gate,
        grad_branch_gate,
        grad_hidden_gate,
    )


def solution(mesh):
    return jax.shard_map(
        shards,
        mesh=mesh,
        in_specs=(
            P("hid", "rows"),
            P(None, "hid", None),
            P(None, "hid"),
            P("hid", None),
            P("hid"),
            P(None, "hid"),
            P("hid"),
            P("hid", None),
            P("hid"),
            P(None, "hid"),
            P(None, "hid"),
            P("hid"),
            P("hid"),
            P(),
            P("hid"),
            P("hid"),
            P("rows", None),
            P("hid", "rows"),
        ),
        out_specs=(
            P("hid", "rows"),
            P("hid", "rows"),
            P(None, "hid", None),
            P(None, "hid"),
            P("hid", None),
            P("hid"),
            P(None, "hid"),
            P("hid"),
            P("hid", None),
            P("hid"),
            P(None, "hid"),
            P(None, "hid"),
            P("hid"),
            P("hid"),
            P(),
            P("hid"),
        ),
        check_vma=False,
    )
```

```python
import jax
import jax.numpy as jnp
from jax import lax
from jax.experimental import pallas as pl
from jax.experimental.pallas import tpu as pltpu
from jax.sharding import PartitionSpec as P

HEAD_DIM = 64
norm_eps = 1e-06
masked_score = -1e30
bf16 = jnp.bfloat16
f32 = jnp.float32
MIB = 1 << 20
WIDE = 512
HBM_BYTES_PER_MICRO = 3690000

SPECS = {
    "S": pl.BlockSpec(memory_space=pltpu.SMEM),
    "V": pl.BlockSpec(memory_space=pltpu.VMEM),
}


def swap(block, axis, bit):
    return lax.ppermute(block, axis, [(i, i ^ bit) for i in range(lax.axis_size(axis))])


def after(block, *others):
    return lax.optimization_barrier((block, *others))[0]


def sds(shape, dtype):
    return jax.ShapeDtypeStruct(shape, dtype)


def local_kernel(body, name, args, kinds, outs, scratch=(), micros=0.6, vmem=16):
    return pl.pallas_call(
        body,
        name=name,
        out_shape=outs,
        in_specs=[SPECS[k] for k in kinds],
        out_specs=[SPECS["V"]] * len(outs),
        scratch_shapes=list(scratch),
        compiler_params=pltpu.CompilerParams(vmem_limit_bytes=vmem * MIB),
        cost_estimate=pl.CostEstimate(
            flops=1, bytes_accessed=int(micros * HBM_BYTES_PER_MICRO), transcendentals=0
        ),
    )(*args)


def dot(left, right):
    return jnp.dot(left, right, preferred_element_type=f32)


def dot_nt(left, right):
    return lax.dot_general(left, right, (((1,), (1,)), ((), ())), preferred_element_type=f32)


def dot_tn(left, right):
    return lax.dot_general(left, right, (((0,), (0,)), ((), ())), preferred_element_type=f32)


def at(index, size):
    return pl.ds(pl.multiple_of(index * size, size), size)


def begin(given, w_out, w_back, bounds, small, out_half, back_half):
    toks = bounds.shape[1]
    query = lax.broadcasted_iota(jnp.int32, (1, toks), 1).astype(f32)
    start, stop = jnp.zeros_like(query), jnp.zeros_like(query)
    end = jnp.zeros((1, 1), f32)
    for j in range(4):
        first, end = end, end + given[3:4, j : j + 1]
        inside = (query >= first) & (query < end)
        start = jnp.where(inside, first, start)
        stop = jnp.where(inside, end, stop)
    bounds[0:1, :] = start.astype(jnp.int32)
    bounds[1:2, :] = stop.astype(jnp.int32)
    feats = given.shape[1]
    small[...] = jnp.zeros_like(small)
    small[0:2, :feats] = given[0:2, :]
    heads = feats // HEAD_DIM
    small[2:3, :feats] = jnp.concatenate(
        [jnp.broadcast_to(given[2:3, i : i + 1], (1, HEAD_DIM)) for i in range(heads)], axis=1
    )
    other, parity = 1 - lax.axis_index("hid") // 2, lax.axis_index("rows") & 1
    out_half[...] = w_out[at(parity, out_half.shape[0]), :]
    back_half[...] = w_back[:, at(2 * other + parity, back_half.shape[1])]


def fill_mask(bounds, mask):
    toks = mask.shape[0]
    for j in range(toks // WIDE):
        chunk = slice(j * WIDE, (j + 1) * WIDE)
        position = lax.broadcasted_iota(jnp.int32, (toks, WIDE), 0)
        same = (position >= bounds[0:1, chunk]) & (position < bounds[1:2, chunk])
        mask[:, chunk] = jnp.where(same, 0.0, masked_score)


def attn_forward(
    bounds, small, x0, x1, x2, x3, w_qkv,
    x_all, qkv, logsum, mine, send_core, send_x, x_block, gated, mask,
):
    me = lax.axis_index("hid")
    feats, toks = x0.shape
    block = toks // 4
    for k, piece in enumerate((x0, x1, x2, x3)):
        x_all[at(me ^ k, feats), :] = piece[...]
    x_block[...] = x_all[:, at(me, block)]
    cols = jnp.transpose(small[...])
    for c in range(3):
        rows = dot(w_qkv[c], x_all[...])
        if c != 1:
            rows = rows + cols[:feats, c // 2 : c // 2 + 1]
        rows = rows.astype(bf16)
        if c == 0:
            rows = rows * jnp.asarray(HEAD_DIM ** (-0.5), bf16)
        qkv[c] = rows
    fill_mask(bounds, mask)
    heads = feats // HEAD_DIM
    for head in range(heads):
        span = slice(head * HEAD_DIM, (head + 1) * HEAD_DIM)
        keys = jnp.transpose(qkv[1, span, :])
        values = qkv[2, span, :]
        for j in range(4 * block // WIDE):
            chunk = slice(j * WIDE, (j + 1) * WIDE)
            scores = dot(keys, qkv[0, span, chunk])
            scores = scores + mask[:, chunk]
            peak = jnp.max(scores, axis=0, keepdims=True)
            expo = jnp.exp(scores - peak)
            total = jnp.sum(expo, axis=0, keepdims=True)
            probs = (expo * (1.0 / total)).astype(bf16)
            logsum[head : head + 1, chunk] = peak + jnp.log(total)
            gated[span, chunk] = (dot(values, probs) * cols[span, 2:3]).astype(bf16)
    mine[...] = gated[:, at(me, block)]
    send_x[:feats, :] = gated[:, at(me ^ 2, block)]
    send_x[feats:, :] = gated[:, at(me ^ 3, block)]
    send_core[...] = gated[:, at(me ^ 1, block)]


def attn_backward(
    bounds, qkv, logsum, u0, u1, u2, u3, grads, head_sums, bias_sums, up, mask
):
    me = lax.axis_index("hid")
    feats, block = u0.shape
    pieces = (u0, u1.at[:feats, :], u2.at[:feats, :], u3.at[feats : 2 * feats, :])
    for k, piece in enumerate(pieces):
        up[:, at(me ^ k, block)] = piece[...]
    fill_mask(bounds, mask)
    heads = feats // HEAD_DIM
    head_sums[...] = jnp.zeros_like(head_sums)
    for head in range(heads):
        span = slice(head * HEAD_DIM, (head + 1) * HEAD_DIM)
        queries, keys_t, values_t = (qkv[c, span, :] for c in range(3))
        keys = jnp.transpose(keys_t)
        values = jnp.transpose(values_t)
        upstream = up[span, :]
        grad_k = jnp.zeros((HEAD_DIM, 4 * block), f32)
        grad_v = jnp.zeros((HEAD_DIM, 4 * block), f32)
        inner_sum = jnp.zeros((1, WIDE), f32)
        for j in range(4 * block // WIDE):
            chunk = slice(j * WIDE, (j + 1) * WIDE)
            scores = dot(keys, queries[:, chunk])
            scores = scores + mask[:, chunk]
            probs = jnp.exp(scores - logsum[head : head + 1, chunk])
            grad_p = dot(values, upstream[:, chunk])
            weighted = probs * grad_p
            inner = jnp.sum(weighted, axis=0, keepdims=True)
            inner_sum = inner_sum + inner
            grad_s = (weighted - probs * inner).astype(bf16)
            grad_v = grad_v + dot_nt(upstream[:, chunk], probs.astype(bf16))
            grad_k = grad_k + dot_nt(queries[:, chunk], grad_s)
            grads[span, chunk] = (dot(keys_t, grad_s) * HEAD_DIM ** (-0.5)).astype(bf16)
        for c, grad in ((1, grad_k), (2, grad_v)):
            rows = slice(c * feats + head * HEAD_DIM, c * feats + (head + 1) * HEAD_DIM)
            grads[rows, :] = grad.astype(bf16)
        head_sums[head : head + 1, :] = sum(
            inner_sum[:, k * block : (k + 1) * block] for k in range(WIDE // block)
        )
    ones = jnp.ones((8, 4 * block), bf16)
    bias_sums[...] = dot_nt(ones, grads[...])


def all_sums(sums, u1, u2, u3, ig_mine, p_core, bin_sum, head_sums, bias_sums, vec):
    blocks = sums.shape[1] // 128
    feats = (u2.shape[0] - 16 * blocks) // 2
    total = sums[...] + get_sums(u1, feats, 8, blocks)
    vec[0:8, :] = (total + get_sums(u2, 2 * feats, 8, blocks)) + get_sums(u3, 2 * feats, 8, blocks)
    vec[8:, :] = jnp.zeros((vec.shape[0] - 8, vec.shape[1]), f32)
    pair = p_core[p_core.shape[0] - 16 :, :].astype(f32)
    vec[8:9, :] = ig_mine[0:1, :] + (pair[0:1, :] + pair[8:9, :])
    vec[9:10, :] = bin_sum[0:1, :]
    width = bias_sums.shape[1]
    vec[10:11, :width] = bias_sums[0:1, :]
    vec[11:12, :8] = jnp.sum(jnp.transpose(head_sums[...]), axis=0, keepdims=True)


def pair_value(pair):
    n = pair.shape[0] // 2
    return pair[:n, :].astype(f32) + pair[n:, :].astype(f32)


def qk_weight_grad(
    grads, x_all, sums, u1, u2, u3, ig_mine, p_core, bin_sum, head_sums, bias_sums,
    keep, send, pair, full, vec,
):
    parity = lax.axis_index("rows") & 1
    n = keep.shape[0]
    full[...] = dot_nt(grads[: 2 * n, :], x_all[...])
    all_sums(sums, u1, u2, u3, ig_mine, p_core, bin_sum, head_sums, bias_sums, vec)
    send[:n, :] = full[at(parity ^ 1, n), :].astype(bf16)
    send[n:, :] = high_low(vec[...])
    pair[...] = high_low(vec[...])
    keep[...] = full[at(parity, n), :]


def vo_weight_grad(grads, x_all, wo_mine, wo_core, wo_far, keep, send, full):
    parity = lax.axis_index("rows") & 1
    n = keep.shape[0]
    full[:n, :] = dot_nt(grads[2 * n :, :], x_all[...])
    full[n:, :] = wo_mine[...] + wo_core[:n, :].astype(f32) + wo_far[...].astype(f32)
    send[...] = full[at(parity ^ 1, n), :].astype(bf16)
    keep[...] = full[at(parity, n), :]


def add_low(mine, other, total):
    total[...] = (mine[...].astype(f32) + other[...].astype(f32)).astype(total.dtype)


def add_second(mine, other, total):
    n = mine.shape[0]
    total[...] = (mine[...] + other[n:, :].astype(f32)).astype(total.dtype)


def tokens_step(mine, res_x, recv, send):
    n, toks = mine.shape
    block = res_x.shape[1]
    send[:, :toks] = (mine[...] + recv[n:, :toks].astype(f32)).astype(bf16)
    send[:, toks : toks + block] = res_x[...]
    send[:, toks + block :] = recv[n:, toks:]


def tokens_outputs(mine, res_mine, from_core, from_x, grad, output):
    me = lax.axis_index("hid")
    n, toks = mine.shape
    block = res_mine.shape[1]
    both = from_core[:n, :toks].astype(f32) + from_x[:, :toks].astype(f32)
    grad[...] = (mine[...] + both).astype(bf16)
    output[:, at(me, block)] = res_mine[...]
    output[:, at(me ^ 1, block)] = from_core[:n, toks:]
    output[:, at(me ^ 2, block)] = from_x[:, toks : toks + block]
    output[:, at(me ^ 3, block)] = from_x[:, toks + block :]


def qkv_input_grad(grads, w_qkv, dres, res_send, mine, mine_x, send, full):
    me = lax.axis_index("hid")
    feats = mine.shape[0]
    block = dres.shape[0]
    total = None
    for c in range(3):
        part = dot(jnp.transpose(w_qkv[c]), grads[c * feats : (c + 1) * feats, :])
        total = part if total is None else total + part
    full[...] = total
    full[:, at(me, block)] += jnp.transpose(dres[...])
    toks = full.shape[1]
    send[:feats, :toks] = full[at(me ^ 1, feats), :].astype(bf16)
    send[feats:, :toks] = full[at(me ^ 3, feats), :].astype(bf16)
    send[:, toks:] = res_send[...]
    mine[...] = full[at(me, feats), :]
    mine_x[...] = full[at(me ^ 2, feats), :]


def place_rows(own, core_rows, xa, xb, fa, fb, whole):
    me, parity = lax.axis_index("hid"), lax.axis_index("rows") & 1
    n = own.shape[0]
    half = n // 2
    whole[at(me, n), :] = own[...]
    whole[at(me ^ 1, n), :] = core_rows[...]
    for owner, first, second in ((me ^ 2, xa, xb), (me ^ 3, fa, fb)):
        whole[at(2 * owner + parity, half), :] = first[...]
        whole[at(2 * owner + (parity ^ 1), half), :] = second[...]


def row_norm(values):
    mean = jnp.mean(values, axis=1, keepdims=True)
    centered = values - mean
    spread = jnp.mean(centered * centered, axis=1, keepdims=True)
    inv = lax.rsqrt(spread + norm_eps)
    return centered * inv, inv


def attn_out(
    g0, g1, g2, g3, x_block, vecs, wo, cotangent,
    normed, send, hat, inv_out, pre, gated_rows, heads_all,
):
    me = lax.axis_index("hid")
    feats = g0.shape[0]
    for k, piece in enumerate((g0, g1.at[:feats, :], g2.at[:feats, :], g3.at[feats : 2 * feats, :])):
        heads_all[at(me ^ k, feats), :] = piece[...]
    gated = jnp.transpose(heads_all[...])
    gated_rows[...] = gated
    tokens = jnp.transpose(x_block[...].astype(f32))
    attn = dot_nt(gated, wo[...]) + vecs[0:1, :]
    pre[...] = attn
    n = normed.shape[0]
    resid = tokens + attn * vecs[8:9, :]
    x_hat, inv = row_norm(resid)
    value = x_hat * vecs[1:2, :] + vecs[2:3, :]
    send[:n, :] = value.astype(bf16)
    rows = feats // 3
    for k in range(3):
        piece = cotangent[k * rows : (k + 1) * rows, at(1 - me // 2, 2 * n)]
        send[n:, k * 2 * n : (k + 1) * 2 * n] = piece
    normed[...] = value
    hat[...] = x_hat
    inv_out[...] = jnp.broadcast_to(inv, inv_out.shape)


def high_low(values):
    high = values.astype(bf16).astype(f32)
    return jnp.concatenate([high, values - high], axis=0).astype(bf16)


def put_sums(sums, ref, start):
    pairs = high_low(sums)
    count = pairs.shape[0]
    for t in range(sums.shape[1] // 128):
        ref[start + t * count : start + (t + 1) * count, :] = pairs[:, t * 128 : (t + 1) * 128]


def get_sums(ref, start, count, blocks):
    parts = []
    for t in range(blocks):
        pair = ref[start + 2 * count * t : start + 2 * count * (t + 1), :].astype(f32)
        parts.append(pair[:count, :] + pair[count:, :])
    return jnp.concatenate(parts, axis=1)


def attn_out_back(
    part, recv, dres2, hat, inv, pre, vecs, wo, sums2,
    dres, grad_attn, sums, up_mine, up_core, up_x, ups,
):
    me = lax.axis_index("hid")
    feats = up_mine.shape[0]
    grad = part[...] + recv[...].astype(f32) + dres2[...]
    x_hat = hat[...]
    scaled = grad * vecs[1:2, :]
    mean_plain = jnp.mean(scaled, axis=1, keepdims=True)
    mean_along = jnp.mean(scaled * x_hat, axis=1, keepdims=True)
    grad_resid = inv[:, 0:1] * (scaled - mean_plain - x_hat * mean_along)
    dres[...] = grad_resid
    low = (grad_resid * vecs[8:9, :]).astype(bf16)
    grad_attn[...] = low
    grad_gated = dot(low, wo[...])
    upstream = (grad_gated * vecs[7:8, :]).astype(bf16)
    ups[...] = jnp.transpose(upstream)
    up_mine[...] = ups[at(me, feats), :]
    up_core[:feats, :] = ups[at(me ^ 1, feats), :]
    up_x[:feats, :] = ups[at(me ^ 2, feats), :]
    up_x[feats : 2 * feats, :] = ups[at(me ^ 3, feats), :]
    sums[0:1, :] = jnp.sum(grad * x_hat, axis=0, keepdims=True)
    sums[1:2, :] = jnp.sum(grad, axis=0, keepdims=True)
    sums[2:3, :] = jnp.sum(low.astype(f32), axis=0, keepdims=True)
    sums[3:4, :] = jnp.sum(grad_resid * pre[...], axis=0, keepdims=True)
    sums[4:8, :] = sums2[...]
    for ref, start in ((up_core, feats), (up_x, 2 * feats)):
        put_sums(sums[...], ref, start)


def out_weight_grad(grad_attn, gated_rows, mine, mine_x, send, full):
    me = lax.axis_index("hid")
    feats = mine.shape[0]
    full[...] = dot_tn(grad_attn[...], gated_rows[...])
    send[:feats, :] = full[at(me ^ 1, feats), :].astype(bf16)
    send[feats:, :] = full[at(me ^ 3, feats), :].astype(bf16)
    mine[...] = full[at(me, feats), :]
    mine_x[...] = full[at(me ^ 2, feats), :]


def place_units(wi_own, wi_core, own, core_rows, xa, xb, fa, fb, wi, wb):
    me, core, chip, parity = lax.axis_index("hid"), lax.axis_index("hid") & 1, lax.axis_index("hid") // 2, lax.axis_index("rows") & 1
    n, half = xa.shape
    units = wi_own.shape[1]
    wi[:, at(core, units)] = wi_own[...]
    wi[:, at(core ^ 1, units)] = wi_core[...]
    wb[at(me, n), :] = own[:, at(chip, 2 * half)]
    wb[at(me ^ 1, n), :] = core_rows[:, at(chip, 2 * half)]
    for owner, first, second in ((me ^ 2, xa, xb), (me ^ 3, fa, fb)):
        wb[at(owner, n), at(parity, half)] = first[...]
        wb[at(owner, n), at(parity ^ 1, half)] = second[...]


def ffn_forward(
    rows, unit_rows, wi, wb, core_far, act, slope, inter_mine, part, core_pair, inter
):
    n = part.shape[0]
    core_pair[n:, :] = core_far[...]
    ffn_units(rows[: part.shape[0], :], unit_rows, wi, act, slope, inter_mine, core_pair.at[:n, :], inter)
    part[...] = dot_nt(inter[...], wb[...])


def ffn_forward_far(
    rows, unit_rows, wi, wb, act, slope, inter_mine, inter_core, part, inter
):
    ffn_units(rows[: part.shape[0], :], unit_rows, wi, act, slope, inter_mine, inter_core, inter)
    part[...] = dot_nt(inter[...], wb[...]).astype(part.dtype)


def ffn_units(rows, unit_rows, wi, act, slope, inter_mine, inter_core, inter):
    core = lax.axis_index("hid") & 1
    units = wi.shape[1]
    step = 256
    for j in range(units // step):
        cut = slice(j * step, (j + 1) * step)
        u = dot(rows, wi[:, cut]) + unit_rows[0:1, cut]
        cdf = 0.5 * (1.0 + lax.erf(u * 0.7071067811865476))
        value = u * cdf
        act[:, cut] = value
        slope[:, cut] = cdf + u * (jnp.exp(-0.5 * u * u) * 0.3989422804014327)
        inter[:, cut] = (value * unit_rows[1:2, cut]).astype(bf16)
    inter_mine[...] = inter[:, at(core, units // 2)]
    inter_core[...] = inter[:, at(core ^ 1, units // 2)]


def ffn_backward(
    rows, act, slope, unit_rows, wi, wb, gpre_mine, gpre_core, part, sums, gpre,
):
    ffn_units_back(rows, act, slope, unit_rows, wb, gpre_mine, gpre_core, sums, gpre)
    part[...] = dot_nt(gpre[...], wi[...])


def ffn_backward_far(
    rows, act, slope, unit_rows, wi, wb, core_mine, sums_mine,
    gpre_mine, part, sums, core_pair, gpre, all_sums,
):
    core, n = lax.axis_index("hid") & 1, rows.shape[0]
    units = gpre_mine.shape[1]
    core_pair[:n, :] = core_mine[...]
    ffn_units_back(
        rows, act, slope, unit_rows, wb, gpre_mine, core_pair.at[n : 2 * n, :], all_sums, gpre
    )
    part[...] = dot_nt(gpre[...], wi[...]).astype(part.dtype)
    all_sums[...] += sums_mine[...]
    sums[...] = all_sums[:, at(core, units)]
    core_pair[2 * n :, :] = high_low(all_sums[:, at(core ^ 1, units)])


def ffn_units_back(rows, act, slope, unit_rows, wb, gpre_mine, gpre_core, sums, gpre):
    core = lax.axis_index("hid") & 1
    units = wb.shape[1]
    step = 256
    for j in range(units // step):
        cut = slice(j * step, (j + 1) * step)
        ginter = dot(rows[...], wb[:, cut])
        sums[:, cut] = jnp.broadcast_to(
            jnp.sum(ginter * act[:, cut], axis=0, keepdims=True), (8, step)
        )
        gpre[:, cut] = (ginter * unit_rows[1:2, cut] * slope[:, cut]).astype(bf16)
    gpre_mine[...] = gpre[:, at(core, units // 2)]
    gpre_core[...] = gpre[:, at(core ^ 1, units // 2)]


def ffn_weight_grads(
    n0, n1, n2, n3, e0, e1, e_core, p0, p1, p_core, f0, f1, f2, f3,
    back0_keep, back0_send, back1_keep, back1_send, in0_keep, in0_send, in1_keep, in1_send,
    bias_sums, left, right, full,
):
    parity = lax.axis_index("rows") & 1

    def fill(target, pieces):
        start = 0
        for piece in pieces:
            count = piece.shape[0] // 128 * 128
            target[start : start + count, :] = piece[:count, :]
            start += count

    fill(left, (f0, f1, f2, f3))
    fill(right, (e0, e1, e_core))
    full[...] = dot_tn(left[...], right[...])
    owners, parts = 4, 4
    rows = full.shape[0] // (owners * parts)
    for k, (keep, send) in enumerate(((back0_keep, back0_send), (back1_keep, back1_send))):
        for h in range(owners):
            to = slice(h * rows, (h + 1) * rows)
            send[to, :] = full[at(h * parts + 2 * k + (parity ^ 1), rows), :].astype(bf16)
            keep[to, :] = full[at(h * parts + 2 * k + parity, rows), :]
    fill(left, (n0, n1, n2, n3))
    fill(right, (p0, p1, p_core))
    full[...] = dot_tn(left[...], right[...])
    rows = full.shape[0] // 4
    for k, (keep, send) in enumerate(((in0_keep, in0_send), (in1_keep, in1_send))):
        send[...] = full[at(2 * k + (parity ^ 1), rows), :].astype(bf16)
        keep[...] = full[at(2 * k + parity, rows), :]
    bias_sums[...] = jnp.broadcast_to(
        jnp.sum(right[...].astype(f32), axis=0, keepdims=True), bias_sums.shape
    )


def second_norm(
    part, recv, normed, cot0, cot1, n_x, n_far, vecs,
    grad_low, dres, sums, out_mine, out_x, out_send, cots, outs,
):
    me = lax.axis_index("hid")
    feats = cot0.shape[0]
    block = part.shape[0]
    core = me & 1
    cots[at(me, feats), :] = cot0[:, at(me, block)]
    cots[at(me ^ 1, feats), :] = cot1[:, at(me, block)]
    rows = feats // 3
    for owner, pieces in ((me ^ 2, n_x), (me ^ 3, n_far)):
        for k in range(3):
            to = pl.ds(pl.multiple_of(owner * feats + k * rows, rows), rows)
            cots[to, :] = pieces[block:, at(2 * k + core, block)]
    ffn = part[...] + recv[...].astype(f32) + vecs[4:5, :]
    resid = normed[...] + ffn * vecs[9:10, :]
    x_hat, inv = row_norm(resid)
    grad_out = jnp.transpose(cots[...].astype(f32))
    scaled = grad_out * vecs[5:6, :]
    mean_plain = jnp.mean(scaled, axis=1, keepdims=True)
    mean_along = jnp.mean(scaled * x_hat, axis=1, keepdims=True)
    grad_resid = inv * (scaled - mean_plain - x_hat * mean_along)
    low = (grad_resid * vecs[9:10, :]).astype(bf16)
    grad_low[...] = low
    dres[...] = grad_resid
    value = x_hat * vecs[5:6, :] + vecs[6:7, :]
    outs[...] = jnp.transpose(value).astype(bf16)
    out_mine[...] = outs[at(me, feats), :]
    out_x[...] = outs[at(me ^ 2, feats), :]
    out_send[:feats, :] = outs[at(me ^ 1, feats), :]
    out_send[feats:, :] = outs[at(me ^ 3, feats), :]
    sums[0:1, :] = jnp.sum(grad_out * x_hat, axis=0, keepdims=True)
    sums[1:2, :] = jnp.sum(grad_out, axis=0, keepdims=True)
    sums[2:3, :] = jnp.sum(low.astype(f32), axis=0, keepdims=True)
    sums[3:4, :] = jnp.sum(grad_resid * ffn, axis=0, keepdims=True)


VECTORS = 16


def add_vectors(
    head_gate, branch, b_out, gain, bias, hidden_gate, hidden_mask, b_back, ctx_core, ctx_x,
    send_core, send_x, columns, rows,
):
    feats = b_out.shape[0]

    def row(ref):
        return ref[...].reshape(1, ref.shape[0])

    cols = row(hidden_gate) * row(hidden_mask).astype(f32)
    rows[...] = jnp.zeros_like(rows)
    rows[0:1, :feats] = row(b_out)
    rows[1:2, :feats] = gain[0:1, :]
    rows[2:3, :feats] = bias[0:1, :]
    rows[3:4, :feats] = cols
    rows[4:5, :feats] = row(b_back)
    rows[5:6, :feats] = gain[1:2, :]
    rows[6:7, :feats] = bias[1:2, :]
    rows[7:8, :feats] = jnp.concatenate(
        [jnp.full((1, HEAD_DIM), head_gate[i], f32) for i in range(feats // HEAD_DIM)], axis=1
    )
    rows[8:9, :feats] = branch[0] * cols
    rows[9:10, :feats] = branch[1] * cols
    rest = jnp.transpose(rows[...])[:feats, :]
    columns[...] = jnp.zeros_like(columns)
    for k in range(3):
        low = rest.astype(bf16)
        columns[:, k * VECTORS : (k + 1) * VECTORS] = low
        rest = rest - low.astype(f32)
    for send, ctx in ((send_core, ctx_core), (send_x, ctx_x)):
        n = ctx.shape[0]
        send[:n, :] = ctx[...]
        send[n:, :] = columns[...]


def place_vectors(p0, p1, p2, p3, b_in, gate, b_in_core, gate_core, vecs, unit_rows, cols):
    me, core = lax.axis_index("hid"), lax.axis_index("hid") & 1
    feats = cols.shape[0] // 4
    units = b_in.shape[0]
    for k, piece in enumerate((p0, p1.at[feats:, :], p2.at[2 * feats :, :], p3.at[2 * feats :, :])):
        parts = piece[...].astype(f32)
        cols[at(me ^ k, feats), :] = (
            parts[:, :VECTORS] + parts[:, VECTORS : 2 * VECTORS]
        ) + parts[:, 2 * VECTORS : 3 * VECTORS]
    vecs[...] = jnp.transpose(cols[...])
    for k, (one, two) in enumerate(((b_in, gate), (b_in_core, gate_core))):
        unit_rows[0:1, at(core ^ k, units)] = one[...].reshape(1, units)
        unit_rows[1:2, at(core ^ k, units)] = two[...].reshape(1, units)


def vector_outputs(
    branch, head_gate, vec, vecs, hidden_mask,
    g_qv, g_bout, g_bin, g_bback, g_gain, g_bias, g_head, g_inter, g_branch, g_hidden, cols,
):
    me = lax.axis_index("hid")
    feats = g_bout.shape[0]
    cols[...] = jnp.transpose(vec[0:8, :])
    own = jnp.transpose(cols[at(me, feats), :])
    g_gain[0:1, :] = own[0:1, :]
    g_gain[1:2, :] = own[4:5, :]
    g_bias[0:1, :] = own[1:2, :]
    g_bias[1:2, :] = own[5:6, :]
    g_bout[...] = own[2, :]
    g_bback[...] = own[6, :]
    mask = hidden_mask[...].astype(f32)
    g_hidden[...] = (branch[0] * own[3, :] + branch[1] * own[7, :]) * mask
    g_inter[...] = vec[8, :]
    g_bin[...] = vec[9, :]
    g_qv[0:1, :] = vec[10:11, :feats]
    rolled = vec[10:11, 2 * feats : 3 * feats]
    g_qv[1:2, :] = rolled
    lane = lax.broadcasted_iota(jnp.int32, (1, 128), 1)
    gates = jnp.ones((1, 128), f32)
    for i in range(feats // HEAD_DIM):
        gates = jnp.where(lane == i, head_gate[i], gates)
    g_head[...] = (vec[11:12, :128] / gates)[0, : feats // HEAD_DIM]
    part0 = jnp.sum(vec[3:4, :] * vecs[3:4, :], axis=1, keepdims=True)
    part1 = jnp.sum(vec[7:8, :] * vecs[3:4, :], axis=1, keepdims=True)
    both = jnp.where(lane == 0, part0, part1)
    g_branch[...] = both[0, :2]


def row_place():
    row = lax.axis_index("rows")
    return row & 1, (row >> 1) & 3


def first_add(keep, recv, total, send):
    total[...] = keep[...] + recv[...].astype(f32)
    send[...] = total[...].astype(bf16)


def first_add_pair(keep, pair, recv, total, send):
    n = keep.shape[0]
    total[...] = keep[...] + recv[:n, :].astype(f32)
    send[:n, :] = total[...].astype(bf16)
    send[n:, :] = high_low(pair_value(pair) + pair_value(recv[n:, :]))


def second_add(keep, recv, send):
    send[...] = (keep[...] + recv[...].astype(f32)).astype(bf16)


def second_add_pair(keep, mine, recv, send):
    n = keep.shape[0]
    send[:n, :] = (keep[...] + recv[:n, :].astype(f32)).astype(bf16)
    send[n:, :] = high_low(pair_value(mine[n:, :]) + pair_value(recv[n:, :]))


def third_add(mine, recv, total):
    total[...] = (mine[...].astype(f32) + recv[...].astype(f32)).astype(bf16)


def third_add_pair(mine, recv, total):
    n = mine.shape[0] - 32
    total[:n, :] = (mine[:n, :].astype(f32) + recv[:n, :].astype(f32)).astype(bf16)
    total[n:, :] = high_low(pair_value(mine[n:, :]) + pair_value(recv[n:, :]))


def choose(mine, recv, total):
    z = row_place()[1]
    outer = (z == 0) | (z == 3)
    total[...] = jnp.where(outer, recv[...], mine[...])


def choose_pair(mine, recv, total, vec):
    n = total.shape[0]
    z = row_place()[1]
    outer = (z == 0) | (z == 3)
    total[...] = jnp.where(outer, recv[:n, :], mine[:n, :])
    vec[...] = jnp.where(outer, pair_value(recv[n:, :]), pair_value(mine[n:, :]))


def split_owners(mine, recv, own, own_x, send):
    me = lax.axis_index("hid")
    n = own.shape[0]

    def rows(k):
        total = mine[at(me ^ k, n), :].astype(f32) + recv[at(me ^ k, n), :].astype(f32)
        return total.astype(bf16)

    own[...] = rows(0)
    own_x[...] = rows(2)
    send[:n, :] = rows(1)
    send[n:, :] = rows(3)


def join_owners(mine, from_core, from_x, chunk):
    me, n = lax.axis_index("hid"), mine.shape[0]
    chunk[at(me, n), :] = mine[...]
    chunk[at(me ^ 1, n), :] = from_core[:n, :]
    chunk[at(me ^ 2, n), :] = from_x[:n, :]
    chunk[at(me ^ 3, n), :] = from_x[n:, :]


def in_gradient(mine0, other0, mine1, other1, grad):
    y = row_place()[0]
    n = mine0.shape[0]
    for k, (mine, other) in enumerate(((mine0, other0), (mine1, other1))):
        grad[at(2 * k + y, n), :] = mine[...].astype(f32)
        grad[at(2 * k + (y ^ 1), n), :] = other[...].astype(f32)


def back_gradient(mine0, other0, mine1, other1, grad):
    y = row_place()[0]
    units = mine0.shape[1]
    n = mine0.shape[0] // 4
    for k, (mine, other) in enumerate(((mine0, other0), (mine1, other1))):
        for side, half in ((y, mine), (y ^ 1, other)):
            for owner in range(4):
                block = half[owner * n : (owner + 1) * n, :].astype(f32)
                grad[at(2 * k + side, n), owner * units : (owner + 1) * units] = block


def attn_gradients(qk_mine, qk_other, vo_mine, vo_other, grad_qkv, grad_out):
    y = row_place()[0]
    n = qk_mine.shape[0]
    grad_qkv[at(y, n), :] = qk_mine[...].astype(f32)
    grad_qkv[at(y ^ 1, n), :] = qk_other[...].astype(f32)
    mine, other = vo_mine[...].astype(f32), vo_other[...].astype(f32)
    grad_qkv[2 * n :, :] = jnp.where(y == 0, mine, other)
    grad_out[...] = jnp.where(y == 0, other, mine)


def second_half(mine, recv, both):
    n = mine.shape[0]
    both[:n, :] = mine[...]
    both[n:, :] = recv[n:, :]


EARLY_TURNS = "313"
TURNS = "41q3v2413241v2341q122vg132q4v12q4vg2qegvq"
FIRST = ("in0", "back0")


def along(block, way="y"):
    pairs = []
    for i in range(lax.axis_size("rows")):
        z = (i >> 1) & 3
        step = {
            "y": 1 - 2 * (i & 1),
            "in": {0: 2, 3: -2}.get(z),
            "mid": {1: 2, 2: -2}.get(z),
            "out": {1: -2, 2: 2}.get(z),
        }[way]
        if step is not None:
            pairs.append((i, i + step))
    return lax.ppermute(block, "rows", pairs)


class Turns:
    def __init__(self):
        self.last = ()

    def held(self, block):
        return after(block, *self.last) if self.last else block

    def mark(self, *blocks):
        self.last = blocks


def far_rows_sum(chunk):
    count = lax.axis_size("rows")
    if count == 8:
        return chunk
    groups = [[i + 8 * j for j in range(count // 8)] for i in range(8)]
    return lax.psum(chunk.astype(f32), "rows", axis_index_groups=groups).astype(chunk.dtype)


def shards(
    tokens, w_qkv, b_qv, w_out, b_out, w_in, b_in, w_back, b_back, norm_gain, norm_bias,
    head_gate, inter_gate, branch_gate, hidden_gate, hidden_mask, doc_lengths, cotangent,
):
    feats, toks = tokens.shape
    width = 4 * feats
    units = w_in.shape[1]
    block = toks // 4
    given = jnp.concatenate(
        [
            b_qv,
            jnp.pad(head_gate, (0, feats - head_gate.shape[0]))[None],
            jnp.pad(doc_lengths.astype(f32), ((0, 0), (0, feats - doc_lengths.shape[1]))),
        ],
        0,
    )
    bounds, small, out_half, back_half = local_kernel(
        begin,
        "begin",
        (given, w_out, w_back),
        "VVV",
        [
            sds((8, toks), jnp.int32),
            sds((8, 256), f32),
            sds((feats // 2, width), bf16),
            sds((feats, units), bf16),
        ],
    )
    tokens_x = swap(tokens, "hid", 2)
    tokens_core = swap(tokens, "hid", 1)
    x_own = swap(tokens_core, "hid", 1)
    out_xa = swap(out_half, "hid", 2)
    back_xa = swap(back_half, "hid", 2)
    wi_core = swap(w_in, "hid", 1)
    wo_core = swap(w_out, "hid", 1)
    cot_core = swap(after(cotangent, back_half), "hid", 1)
    b_in_core = swap(b_in, "hid", 1)
    gate_core = swap(inter_gate, "hid", 1)
    back_core = swap(w_back, "hid", 1)
    tokens_far = swap(
        after(tokens_x, tokens_core, wi_core, wo_core, cot_core, back_core, back_half), "hid", 1
    )

    head_block = sds((feats, block), bf16)
    two_blocks = sds((2 * feats, block), bf16)
    x_all, qkv, logsum, g0, g_core, g_x, x_block = local_kernel(
        attn_forward,
        "attn_forward",
        (
            bounds, small, x_own, tokens_core, tokens_x, tokens_far, w_qkv,
        ),
        "V" * 7,
        [
            sds((width, toks), bf16),
            sds((3, feats, toks), bf16),
            sds((8, toks), f32),
            head_block,
            head_block,
            two_blocks,
            sds((width, block), bf16),
        ],
        [pltpu.VMEM((feats, toks), bf16), pltpu.VMEM((toks, toks), f32)],
        micros=5.4,
    )
    send_core, send_x, columns = local_kernel(
        add_vectors,
        "add_vectors",
        (
            head_gate, branch_gate, after(b_out, x_block), norm_gain, norm_bias, hidden_gate,
            hidden_mask, b_back, g_core, g_x,
        ),
        "SS" + "V" * 8,
        [two_blocks, sds((3 * feats, block), bf16), head_block],
        [pltpu.VMEM((VECTORS, 256), f32)],
    )
    g2 = swap(send_x, "hid", 2)
    g1 = swap(send_core, "hid", 1)
    g3 = swap(after(g2, g1, b_in_core, gate_core), "hid", 1)
    out_xb = swap(after(out_xa, g0), "rows", 1)
    out_fa = swap(after(out_xa, g0), "hid", 1)
    out_fb = swap(out_xb, "hid", 1)
    back_xb = swap(after(back_xa, g1), "rows", 1)
    back_fa = swap(after(back_xa, g1), "hid", 1)
    (wo,) = local_kernel(
        place_rows,
        "place_rows",
        (w_out, wo_core, out_xa, out_xb, out_fa, out_fb),
        "VVVVVV",
        [sds((width, width), bf16)],
    )
    vecs, unit_rows = local_kernel(
        place_vectors,
        "place_vectors",
        (columns, g1, g2, g3, b_in, inter_gate, b_in_core, gate_core),
        "V" * 8,
        [sds((VECTORS, width), f32), sds((2, 2 * units), f32)],
        [pltpu.VMEM((width, VECTORS), f32)],
    )

    normed, n_send, hat, inv, attn_pre, gated_rows = local_kernel(
        attn_out,
        "attn_out",
        (g0, g1, g2, g3, x_block, vecs, wo, cotangent),
        "VVVVVVVV",
        [
            sds((block, width), f32),
            sds((block + feats // 3, width), bf16),
            sds((block, width), f32),
            sds((block, 128), f32),
            sds((block, width), f32),
            sds((block, width), bf16),
        ],
        [pltpu.VMEM((width, block), bf16)],
        micros=1.3,
    )

    n_x = swap(n_send, "hid", 2)
    n_core = swap(n_send, "hid", 1)
    back_fb = swap(after(back_xb, n_x), "hid", 1)
    wi, wb = local_kernel(
        place_units,
        "place_units",
        (w_in, wi_core, w_back, back_core, back_xa, back_xb, back_fa, back_fb),
        "V" * 8,
        [sds((width, 2 * units), bf16), sds((width, 2 * units), bf16)],
        micros=0.85,
    )

    act_block = sds((block, 2 * units), f32)
    half_block = sds((block, units), bf16)
    pair_block = sds((2 * block, units), bf16)
    rows_block = sds((block, width), bf16)
    ffn_scratch = [pltpu.VMEM((block, 2 * units), bf16)]
    act_x, slope_x, e1, inter_core, ffn_send = local_kernel(
        ffn_forward_far,
        "ffn_forward_far",
        (n_x, unit_rows, wi, wb),
        "VVVV",
        [act_block, act_block, half_block, half_block, rows_block],
        ffn_scratch,
        micros=1.85,
    )
    ffn_recv = swap(ffn_send, "hid", 2)
    act, slope, e0, ffn_part, e_pair = local_kernel(
        ffn_forward,
        "ffn_forward",
        (after(n_send, ffn_send), unit_rows, wi, wb, inter_core),
        "VVVVV",
        [act_block, act_block, half_block, sds((block, width), f32), pair_block],
        ffn_scratch,
        micros=1.85,
    )
    n_far = swap(after(n_x, ffn_send), "hid", 1)

    out_block = sds((feats, block), bf16)
    gffn, dres2, sums2, res_mine, res_x, res_send = local_kernel(
        second_norm,
        "second_norm",
        (
            after(ffn_part, n_core), ffn_recv, normed, cotangent, cot_core, n_x, n_far, vecs,
        ),
        "V" * 8,
        [
            sds((block, width), bf16),
            sds((block, width), f32),
            sds((4, width), f32),
            out_block,
            out_block,
            sds((2 * feats, block), bf16),
        ],
        [pltpu.VMEM((width, block), bf16), pltpu.VMEM((width, block), bf16)],
        micros=1.2,
    )

    gffn_x = swap(gffn, "hid", 2)
    e_core = swap(after(e_pair, gffn), "hid", 1)
    f2 = swap(gffn, "hid", 1)
    sums_block = sds((8, 2 * units), f32)
    p0, gpre_core, gn_part, ig_sum = local_kernel(
        ffn_backward,
        "ffn_backward",
        (gffn, act, slope, unit_rows, wi, wb),
        "VVVVVV",
        [half_block, half_block, sds((block, width), f32), sums_block],
        ffn_scratch,
        micros=1.85,
    )
    p1, gn_send, ig_mine, p_pair = local_kernel(
        ffn_backward_far,
        "ffn_backward_far",
        (after(gffn_x, f2, e_core), act_x, slope_x, unit_rows, wi, wb, gpre_core, ig_sum),
        "VVVVVVVV",
        [half_block, rows_block, sds((8, units), f32), sds((2 * block + 16, units), bf16)],
        ffn_scratch + [pltpu.VMEM((8, 2 * units), f32)],
        micros=1.85,
    )
    gn_recv = swap(gn_send, "hid", 2)
    f3 = swap(after(gffn_x, gn_send), "hid", 1)
    p_core = swap(p_pair, "hid", 1)
    *pieces, bin_sum = local_kernel(
        ffn_weight_grads,
        "ffn_weight_grads",
        (
            n_send, n_x, n_core, n_far, e0, e1, e_core,
            p0, p1, p_core, gffn, gffn_x, f2, f3,
        ),
        "V" * 14,
        [
            sds((feats, units), f32),
            sds((feats, units), bf16),
            sds((feats, units), f32),
            sds((feats, units), bf16),
            sds((feats, units), f32),
            sds((feats, units), bf16),
            sds((feats, units), f32),
            sds((feats, units), bf16),
            sds((8, units), f32),
        ],
        [
            pltpu.VMEM((toks, width), bf16),
            pltpu.VMEM((toks, units), bf16),
            pltpu.VMEM((width, units), f32),
        ],
        micros=2.5,
    )

    pieces = dict(zip(("back0", "back1", "in0", "in1"), zip(pieces[0::2], pieces[1::2])))
    early = {name: along(after(pieces[name][1], gn_recv)) for name in FIRST}

    sum_rows = 16 * width // 128
    dres1, gattn, sums1, u0, up_core, up_x = local_kernel(
        attn_out_back,
        "attn_out_back",
        (
            after(gn_part, pieces["in1"][1]), gn_recv, dres2, hat, inv, attn_pre,
            vecs, wo, sums2,
        ),
        "V" * 9,
        [
            sds((block, width), f32),
            sds((block, width), bf16),
            sds((8, width), f32),
            head_block,
            sds((feats + sum_rows, block), bf16),
            sds((2 * feats + sum_rows, block), bf16),
        ],
        [pltpu.VMEM((width, block), bf16)],
        micros=1.3,
    )
    u2 = swap(up_x, "hid", 2)
    u1 = swap(up_core, "hid", 1)
    u3 = swap(u2, "hid", 1)

    weight_block = sds((feats, width), f32)
    low_block = sds((feats, width), bf16)
    wo_mine, wo_keep, wo_send = local_kernel(
        out_weight_grad,
        "out_weight_grad",
        (gattn, gated_rows),
        "VV",
        [weight_block, weight_block, sds((2 * feats, width), bf16)],
        [pltpu.VMEM((width, width), f32)],
        micros=1.2,
    )
    wo_grad_core = swap(after(wo_send, u1), "hid", 1)

    turns = Turns()
    results = {}
    whole_block = sds((feats, width), f32)

    def step(body, args, outs, **more):
        outs = local_kernel(
            body, body.__name__, (turns.held(args[0]),) + args[1:], "V" * len(args), outs, **more
        )
        turns.mark(*outs[-1:])
        return outs

    def sum_chain(name, keep, send, recv=None):
        if recv is None:
            recv = along(turns.held(send))
        yield
        keep, send = step(first_add, (keep, recv), [whole_block, low_block])
        recv = along(send, "in")
        yield
        (mine,) = step(second_add, (keep, recv), [low_block])
        recv = along(mine, "mid")
        yield
        if name.startswith("back"):
            part = sds((feats // 4, units), bf16)
            two = sds((feats // 2, units), bf16)
            mine, mine_x, send = step(split_owners, (mine, recv), [part, part, two])
            from_core = swap(send, "hid", 1)
            yield
            (send,) = step(second_half, (mine_x, from_core), [two])
            from_x = swap(send, "hid", 2)
            yield
            (mine,) = step(join_owners, (mine, from_core, from_x), [low_block])
        else:
            (mine,) = step(third_add, (mine, recv), [low_block])
        recv = along(mine, "out")
        yield
        (mine,) = step(choose, (mine, recv), [low_block])
        yield from last_part(name, mine)

    def last_part(name, mine):
        mine = far_rows_sum(mine)
        other = along(mine)
        yield
        results[name] = (mine, other)
        if name in ("in0", "in1") and "in0" in results and "in1" in results:
            (results["w_in"],) = step(
                in_gradient,
                results["in0"] + results["in1"],
                [sds((width, units), f32)],
                micros=2.1,
            )
        if name in ("back0", "back1") and "back0" in results and "back1" in results:
            (results["w_back"],) = step(
                back_gradient,
                results["back0"] + results["back1"],
                [sds((feats, 4 * units), f32)],
                micros=2.1,
            )
        if name in ("qk", "vo") and "qk" in results and "vo" in results:
            results["w_qkv"], results["w_out"] = step(
                attn_gradients,
                results["qk"] + results["vo"],
                [sds((3 * feats, width), f32), weight_block],
                micros=2.1,
            )

    chains = {
        key: sum_chain(name, *pieces[name], early.get(name))
        for key, name in zip("1234", ("back0", "back1", "in0", "in1"))
    }
    turns.mark(u1)
    for turn in EARLY_TURNS:
        next(chains[turn], None)
    grads, head_sums, bias_sums = local_kernel(
        attn_backward,
        "attn_backward",
        (bounds, turns.held(qkv), logsum, u0, u1, u2, u3),
        "V" * 7,
        [
            sds((3 * feats, toks), bf16),
            sds((8, block), f32),
            sds((8, 3 * feats), f32),
        ],
        [pltpu.VMEM((feats, toks), bf16), pltpu.VMEM((toks, toks), f32)],
        micros=5.0,
    )
    (wo_low,) = local_kernel(add_second, "wo_low", (wo_keep, wo_grad_core), "VV", [low_block])
    wo_far = swap(after(wo_low, u3), "hid", 2)

    gx_block = sds((feats, toks), f32)
    gx_low = sds((feats, toks), bf16)

    def qk_chain():
        with_pair = sds((feats + 32, width), bf16)
        keep, send, pair = local_kernel(
            qk_weight_grad,
            "qk_weight_grad",
            (
                turns.held(grads), x_all, sums1, u1, u2, u3, ig_mine, p_core, bin_sum,
                head_sums, bias_sums,
            ),
            "V" * 11,
            [weight_block, with_pair, sds((32, width), bf16)],
            [pltpu.VMEM((2 * feats, width), f32), pltpu.VMEM((16, width), f32)],
            micros=1.2,
        )
        turns.mark(send)
        recv = along(send)
        yield
        keep, send = step(first_add_pair, (keep, pair, recv), [weight_block, with_pair])
        recv = along(send, "in")
        yield
        (mine,) = step(second_add_pair, (keep, send, recv), [with_pair])
        recv = along(mine, "mid")
        yield
        (mine,) = step(third_add_pair, (mine, recv), [with_pair])
        recv = along(mine, "out")
        yield
        mine, results["sums"] = step(
            choose_pair, (mine, recv), [low_block, sds((16, width), f32)]
        )
        yield from last_part("qk", mine)

    def vo_chain():
        keep, send = local_kernel(
            vo_weight_grad,
            "vo_weight_grad",
            (turns.held(grads), x_all, wo_mine, wo_grad_core, wo_far),
            "VVVVV",
            [weight_block, low_block],
            [pltpu.VMEM((2 * feats, width), f32)],
            micros=1.1,
        )
        turns.mark(send)
        yield from sum_chain("vo", keep, send, along(send))

    def tokens_chain():
        mine, mine_x, send = local_kernel(
            qkv_input_grad,
            "qkv_input_grad",
            (turns.held(grads), w_qkv, dres1, res_send),
            "VVVV",
            [gx_block, gx_block, sds((2 * feats, toks + block), bf16)],
            [pltpu.VMEM((width, toks), f32)],
            micros=1.5,
        )
        turns.mark(send)
        from_core = swap(send, "hid", 1)
        yield
        (send,) = local_kernel(
            tokens_step,
            "tokens_step",
            (turns.held(mine_x), res_x, from_core),
            "VVV",
            [sds((feats, toks + 2 * block), bf16)],
        )
        turns.mark(send)
        from_x = swap(send, "hid", 2)
        yield
        results["tokens"], results["output"] = local_kernel(
            tokens_outputs,
            "tokens_outputs",
            (turns.held(mine), res_mine, from_core, from_x),
            "VVVV",
            [gx_low, gx_low],
            micros=1.2,
        )
        turns.mark(results["tokens"])

    def vector_chain():
        results["vectors"] = local_kernel(
            vector_outputs,
            "vector_outputs",
            (branch_gate, head_gate, far_rows_sum(turns.held(results["sums"])), vecs, hidden_mask),
            "SSVVV",
            [
                sds((2, feats), f32),
                sds((feats,), f32),
                sds((units,), f32),
                sds((feats,), f32),
                sds((2, feats), f32),
                sds((2, feats), f32),
                sds((feats // HEAD_DIM,), f32),
                sds((units,), f32),
                sds((2,), f32),
                sds((feats,), f32),
            ],
            [pltpu.VMEM((width, 8), f32)],
            micros=1.4,
        )
        turns.mark(results["vectors"][0])
        yield

    chains.update(q=qk_chain(), v=vo_chain(), g=tokens_chain(), e=vector_chain())
    turns.mark(grads)
    for turn in TURNS:
        next(chains[turn], None)
    (
        grad_b_qv, grad_b_out, grad_b_in, grad_b_back, grad_norm_gain, grad_norm_bias,
        grad_head_gate, grad_inter_gate, grad_branch_gate, grad_hidden_gate,
    ) = results["vectors"]
    output, grad_tokens = results["output"], results["tokens"]
    grad_w_qkv = results["w_qkv"].reshape(3, feats, width)
    grad_w_out, grad_w_in, grad_w_back = results["w_out"], results["w_in"], results["w_back"]
    return (
        output,
        grad_tokens,
        grad_w_qkv,
        grad_b_qv,
        grad_w_out,
        grad_b_out,
        grad_w_in,
        grad_b_in,
        grad_w_back,
        grad_b_back,
        grad_norm_gain,
        grad_norm_bias,
        grad_head_gate,
        grad_inter_gate,
        grad_branch_gate,
        grad_hidden_gate,
    )


def solution(mesh):
    return jax.shard_map(
        shards,
        mesh=mesh,
        in_specs=(
            P("hid", "rows"),
            P(None, "hid", None),
            P(None, "hid"),
            P("hid", None),
            P("hid"),
            P(None, "hid"),
            P("hid"),
            P("hid", None),
            P("hid"),
            P(None, "hid"),
            P(None, "hid"),
            P("hid"),
            P("hid"),
            P(),
            P("hid"),
            P("hid"),
            P("rows", None),
            P("hid", "rows"),
        ),
        out_specs=(
            P("hid", "rows"),
            P("hid", "rows"),
            P(None, "hid", None),
            P(None, "hid"),
            P("hid", None),
            P("hid"),
            P(None, "hid"),
            P("hid"),
            P("hid", None),
            P("hid"),
            P(None, "hid"),
            P(None, "hid"),
            P("hid"),
            P("hid"),
            P(),
            P("hid"),
        ),
        check_vma=False,
    )
```

```python
import jax
import jax.numpy as jnp
from jax import lax
from jax.experimental import pallas as pl
from jax.experimental.pallas import tpu as pltpu
from jax.sharding import PartitionSpec as P

HEAD_DIM = 64
norm_eps = 1e-06
masked_score = -1e30
bf16 = jnp.bfloat16
f32 = jnp.float32
MIB = 1 << 20
WIDE = 512
HBM_BYTES_PER_MICRO = 3690000

SPECS = {
    "S": pl.BlockSpec(memory_space=pltpu.SMEM),
    "V": pl.BlockSpec(memory_space=pltpu.VMEM),
}


def swap(block, axis, bit):
    return lax.ppermute(block, axis, [(i, i ^ bit) for i in range(lax.axis_size(axis))])


def after(block, *others):
    return lax.optimization_barrier((block, *others))[0]


def sds(shape, dtype):
    return jax.ShapeDtypeStruct(shape, dtype)


def local_kernel(body, name, args, kinds, outs, scratch=(), micros=0.6, vmem=16):
    return pl.pallas_call(
        body,
        name=name,
        out_shape=outs,
        in_specs=[SPECS[k] for k in kinds],
        out_specs=[SPECS["V"]] * len(outs),
        scratch_shapes=list(scratch),
        compiler_params=pltpu.CompilerParams(vmem_limit_bytes=vmem * MIB),
        cost_estimate=pl.CostEstimate(
            flops=1, bytes_accessed=int(micros * HBM_BYTES_PER_MICRO), transcendentals=0
        ),
    )(*args)


def dot(left, right):
    return jnp.dot(left, right, preferred_element_type=f32)


def dot_nt(left, right):
    return lax.dot_general(left, right, (((1,), (1,)), ((), ())), preferred_element_type=f32)


def dot_tn(left, right):
    return lax.dot_general(left, right, (((0,), (0,)), ((), ())), preferred_element_type=f32)


def at(index, size):
    return pl.ds(pl.multiple_of(index * size, size), size)


def begin(given, w_out, w_back, bounds, small, out_half, back_half):
    toks = bounds.shape[1]
    query = lax.broadcasted_iota(jnp.int32, (1, toks), 1).astype(f32)
    start, stop = jnp.zeros_like(query), jnp.zeros_like(query)
    end = jnp.zeros((1, 1), f32)
    for j in range(4):
        first, end = end, end + given[3:4, j : j + 1]
        inside = (query >= first) & (query < end)
        start = jnp.where(inside, first, start)
        stop = jnp.where(inside, end, stop)
    bounds[0:1, :] = start.astype(jnp.int32)
    bounds[1:2, :] = stop.astype(jnp.int32)
    feats = given.shape[1]
    small[...] = jnp.zeros_like(small)
    small[0:2, :feats] = given[0:2, :]
    heads = feats // HEAD_DIM
    small[2:3, :feats] = jnp.concatenate(
        [jnp.broadcast_to(given[2:3, i : i + 1], (1, HEAD_DIM)) for i in range(heads)], axis=1
    )
    other, parity = 1 - lax.axis_index("hid") // 2, lax.axis_index("rows") & 1
    out_half[...] = w_out[at(parity, out_half.shape[0]), :]
    back_half[...] = w_back[:, at(2 * other + parity, back_half.shape[1])]


def fill_mask(bounds, mask):
    toks = mask.shape[0]
    for j in range(toks // WIDE):
        chunk = slice(j * WIDE, (j + 1) * WIDE)
        position = lax.broadcasted_iota(jnp.int32, (toks, WIDE), 0)
        same = (position >= bounds[0:1, chunk]) & (position < bounds[1:2, chunk])
        mask[:, chunk] = jnp.where(same, 0.0, masked_score)


def attn_forward(
    bounds, small, x0, x1, x2, x3, w_qkv,
    x_all, qkv, logsum, mine, send_core, send_x, x_block, gated, mask,
):
    me = lax.axis_index("hid")
    feats, toks = x0.shape
    block = toks // 4
    for k, piece in enumerate((x0, x1, x2, x3)):
        x_all[at(me ^ k, feats), :] = piece[...]
    x_block[...] = x_all[:, at(me, block)]
    cols = jnp.transpose(small[...])
    for c in range(3):
        rows = dot(w_qkv[c], x_all[...])
        if c != 1:
            rows = rows + cols[:feats, c // 2 : c // 2 + 1]
        rows = rows.astype(bf16)
        if c == 0:
            rows = rows * jnp.asarray(HEAD_DIM ** (-0.5), bf16)
        qkv[c] = rows
    fill_mask(bounds, mask)
    heads = feats // HEAD_DIM
    for head in range(heads):
        span = slice(head * HEAD_DIM, (head + 1) * HEAD_DIM)
        keys = jnp.transpose(qkv[1, span, :])
        values = qkv[2, span, :]
        for j in range(4 * block // WIDE):
            chunk = slice(j * WIDE, (j + 1) * WIDE)
            scores = dot(keys, qkv[0, span, chunk])
            scores = scores + mask[:, chunk]
            peak = jnp.max(scores, axis=0, keepdims=True)
            expo = jnp.exp(scores - peak)
            total = jnp.sum(expo, axis=0, keepdims=True)
            probs = (expo * (1.0 / total)).astype(bf16)
            logsum[head : head + 1, chunk] = peak + jnp.log(total)
            gated[span, chunk] = (dot(values, probs) * cols[span, 2:3]).astype(bf16)
    mine[...] = gated[:, at(me, block)]
    send_x[:feats, :] = gated[:, at(me ^ 2, block)]
    send_x[feats:, :] = gated[:, at(me ^ 3, block)]
    send_core[...] = gated[:, at(me ^ 1, block)]


def attn_backward(
    bounds, qkv, logsum, u0, u1, u2, u3, grads, head_sums, bias_sums, up, mask
):
    me = lax.axis_index("hid")
    feats, block = u0.shape
    pieces = (u0, u1.at[:feats, :], u2.at[:feats, :], u3.at[feats : 2 * feats, :])
    for k, piece in enumerate(pieces):
        up[:, at(me ^ k, block)] = piece[...]
    fill_mask(bounds, mask)
    heads = feats // HEAD_DIM
    head_sums[...] = jnp.zeros_like(head_sums)
    for head in range(heads):
        span = slice(head * HEAD_DIM, (head + 1) * HEAD_DIM)
        queries, keys_t, values_t = (qkv[c, span, :] for c in range(3))
        keys = jnp.transpose(keys_t)
        values = jnp.transpose(values_t)
        upstream = up[span, :]
        grad_k = jnp.zeros((HEAD_DIM, 4 * block), f32)
        grad_v = jnp.zeros((HEAD_DIM, 4 * block), f32)
        inner_sum = jnp.zeros((1, WIDE), f32)
        for j in range(4 * block // WIDE):
            chunk = slice(j * WIDE, (j + 1) * WIDE)
            scores = dot(keys, queries[:, chunk])
            scores = scores + mask[:, chunk]
            probs = jnp.exp(scores - logsum[head : head + 1, chunk])
            grad_p = dot(values, upstream[:, chunk])
            weighted = probs * grad_p
            inner = jnp.sum(weighted, axis=0, keepdims=True)
            inner_sum = inner_sum + inner
            grad_s = (weighted - probs * inner).astype(bf16)
            grad_v = grad_v + dot_nt(upstream[:, chunk], probs.astype(bf16))
            grad_k = grad_k + dot_nt(queries[:, chunk], grad_s)
            grads[span, chunk] = (dot(keys_t, grad_s) * HEAD_DIM ** (-0.5)).astype(bf16)
        for c, grad in ((1, grad_k), (2, grad_v)):
            rows = slice(c * feats + head * HEAD_DIM, c * feats + (head + 1) * HEAD_DIM)
            grads[rows, :] = grad.astype(bf16)
        head_sums[head : head + 1, :] = sum(
            inner_sum[:, k * block : (k + 1) * block] for k in range(WIDE // block)
        )
    ones = jnp.ones((8, 4 * block), bf16)
    bias_sums[...] = dot_nt(ones, grads[...])


def all_sums(sums, u1, u2, u3, ig_mine, p_core, bin_sum, head_sums, bias_sums, vec):
    blocks = sums.shape[1] // 128
    feats = (u2.shape[0] - 16 * blocks) // 2
    total = sums[...] + get_sums(u1, feats, 8, blocks)
    vec[0:8, :] = (total + get_sums(u2, 2 * feats, 8, blocks)) + get_sums(u3, 2 * feats, 8, blocks)
    vec[8:, :] = jnp.zeros((vec.shape[0] - 8, vec.shape[1]), f32)
    pair = p_core[p_core.shape[0] - 16 :, :].astype(f32)
    vec[8:9, :] = ig_mine[0:1, :] + (pair[0:1, :] + pair[8:9, :])
    vec[9:10, :] = bin_sum[0:1, :]
    width = bias_sums.shape[1]
    vec[10:11, :width] = bias_sums[0:1, :]
    vec[11:12, :8] = jnp.sum(jnp.transpose(head_sums[...]), axis=0, keepdims=True)


def pair_value(pair):
    n = pair.shape[0] // 2
    return pair[:n, :].astype(f32) + pair[n:, :].astype(f32)


def qk_weight_grad(
    grads, x_all, sums, u1, u2, u3, ig_mine, p_core, bin_sum, head_sums, bias_sums,
    keep, send, pair, full, vec,
):
    parity = lax.axis_index("rows") & 1
    n = keep.shape[0]
    full[...] = dot_nt(grads[: 2 * n, :], x_all[...])
    all_sums(sums, u1, u2, u3, ig_mine, p_core, bin_sum, head_sums, bias_sums, vec)
    send[:n, :] = full[at(parity ^ 1, n), :].astype(bf16)
    send[n:, :] = high_low(vec[...])
    pair[...] = high_low(vec[...])
    keep[...] = full[at(parity, n), :]


def vo_weight_grad(grads, x_all, wo_mine, wo_core, wo_far, keep, send, full):
    parity = lax.axis_index("rows") & 1
    n = keep.shape[0]
    full[:n, :] = dot_nt(grads[2 * n :, :], x_all[...])
    full[n:, :] = wo_mine[...] + wo_core[:n, :].astype(f32) + wo_far[...].astype(f32)
    send[...] = full[at(parity ^ 1, n), :].astype(bf16)
    keep[...] = full[at(parity, n), :]


def add_low(mine, other, total):
    total[...] = (mine[...].astype(f32) + other[...].astype(f32)).astype(total.dtype)


def add_second(mine, other, total):
    n = mine.shape[0]
    total[...] = (mine[...] + other[n:, :].astype(f32)).astype(total.dtype)


def tokens_step(mine, res_x, recv, send):
    n, toks = mine.shape
    block = res_x.shape[1]
    send[:, :toks] = (mine[...] + recv[n:, :toks].astype(f32)).astype(bf16)
    send[:, toks : toks + block] = res_x[...]
    send[:, toks + block :] = recv[n:, toks:]


def tokens_outputs(mine, res_mine, from_core, from_x, grad, output):
    me = lax.axis_index("hid")
    n, toks = mine.shape
    block = res_mine.shape[1]
    both = from_core[:n, :toks].astype(f32) + from_x[:, :toks].astype(f32)
    grad[...] = (mine[...] + both).astype(bf16)
    output[:, at(me, block)] = res_mine[...]
    output[:, at(me ^ 1, block)] = from_core[:n, toks:]
    output[:, at(me ^ 2, block)] = from_x[:, toks : toks + block]
    output[:, at(me ^ 3, block)] = from_x[:, toks + block :]


def qkv_input_grad(grads, w_qkv, dres, res_send, mine, mine_x, send, full):
    me = lax.axis_index("hid")
    feats = mine.shape[0]
    block = dres.shape[0]
    total = None
    for c in range(3):
        part = dot(jnp.transpose(w_qkv[c]), grads[c * feats : (c + 1) * feats, :])
        total = part if total is None else total + part
    full[...] = total
    full[:, at(me, block)] += jnp.transpose(dres[...])
    toks = full.shape[1]
    send[:feats, :toks] = full[at(me ^ 1, feats), :].astype(bf16)
    send[feats:, :toks] = full[at(me ^ 3, feats), :].astype(bf16)
    send[:, toks:] = res_send[...]
    mine[...] = full[at(me, feats), :]
    mine_x[...] = full[at(me ^ 2, feats), :]


def place_rows(own, core_rows, xa, xb, fa, fb, whole):
    me, parity = lax.axis_index("hid"), lax.axis_index("rows") & 1
    n = own.shape[0]
    half = n // 2
    whole[at(me, n), :] = own[...]
    whole[at(me ^ 1, n), :] = core_rows[...]
    for owner, first, second in ((me ^ 2, xa, xb), (me ^ 3, fa, fb)):
        whole[at(2 * owner + parity, half), :] = first[...]
        whole[at(2 * owner + (parity ^ 1), half), :] = second[...]


def row_norm(values):
    mean = jnp.mean(values, axis=1, keepdims=True)
    centered = values - mean
    spread = jnp.mean(centered * centered, axis=1, keepdims=True)
    inv = lax.rsqrt(spread + norm_eps)
    return centered * inv, inv


def attn_out(
    g0, g1, g2, g3, x_block, vecs, wo, cotangent,
    normed, send, hat, inv_out, pre, gated_rows, heads_all,
):
    me = lax.axis_index("hid")
    feats = g0.shape[0]
    for k, piece in enumerate((g0, g1.at[:feats, :], g2.at[:feats, :], g3.at[feats : 2 * feats, :])):
        heads_all[at(me ^ k, feats), :] = piece[...]
    gated = jnp.transpose(heads_all[...])
    gated_rows[...] = gated
    tokens = jnp.transpose(x_block[...].astype(f32))
    attn = dot_nt(gated, wo[...]) + vecs[0:1, :]
    pre[...] = attn
    n = normed.shape[0]
    resid = tokens + attn * vecs[8:9, :]
    x_hat, inv = row_norm(resid)
    value = x_hat * vecs[1:2, :] + vecs[2:3, :]
    send[:n, :] = value.astype(bf16)
    rows = feats // 3
    for k in range(3):
        piece = cotangent[k * rows : (k + 1) * rows, at(1 - me // 2, 2 * n)]
        send[n:, k * 2 * n : (k + 1) * 2 * n] = piece
    normed[...] = value
    hat[...] = x_hat
    inv_out[...] = jnp.broadcast_to(inv, inv_out.shape)


def high_low(values):
    high = values.astype(bf16).astype(f32)
    return jnp.concatenate([high, values - high], axis=0).astype(bf16)


def put_sums(sums, ref, start):
    pairs = high_low(sums)
    count = pairs.shape[0]
    for t in range(sums.shape[1] // 128):
        ref[start + t * count : start + (t + 1) * count, :] = pairs[:, t * 128 : (t + 1) * 128]


def get_sums(ref, start, count, blocks):
    parts = []
    for t in range(blocks):
        pair = ref[start + 2 * count * t : start + 2 * count * (t + 1), :].astype(f32)
        parts.append(pair[:count, :] + pair[count:, :])
    return jnp.concatenate(parts, axis=1)


def attn_out_back(
    part, recv, dres2, hat, inv, pre, vecs, wo, sums2,
    dres, grad_attn, sums, up_mine, up_core, up_x, ups,
):
    me = lax.axis_index("hid")
    feats = up_mine.shape[0]
    grad = part[...] + recv[...].astype(f32) + dres2[...]
    x_hat = hat[...]
    scaled = grad * vecs[1:2, :]
    mean_plain = jnp.mean(scaled, axis=1, keepdims=True)
    mean_along = jnp.mean(scaled * x_hat, axis=1, keepdims=True)
    grad_resid = inv[:, 0:1] * (scaled - mean_plain - x_hat * mean_along)
    dres[...] = grad_resid
    low = (grad_resid * vecs[8:9, :]).astype(bf16)
    grad_attn[...] = low
    grad_gated = dot(low, wo[...])
    upstream = (grad_gated * vecs[7:8, :]).astype(bf16)
    ups[...] = jnp.transpose(upstream)
    up_mine[...] = ups[at(me, feats), :]
    up_core[:feats, :] = ups[at(me ^ 1, feats), :]
    up_x[:feats, :] = ups[at(me ^ 2, feats), :]
    up_x[feats : 2 * feats, :] = ups[at(me ^ 3, feats), :]
    sums[0:1, :] = jnp.sum(grad * x_hat, axis=0, keepdims=True)
    sums[1:2, :] = jnp.sum(grad, axis=0, keepdims=True)
    sums[2:3, :] = jnp.sum(low.astype(f32), axis=0, keepdims=True)
    sums[3:4, :] = jnp.sum(grad_resid * pre[...], axis=0, keepdims=True)
    sums[4:8, :] = sums2[...]
    for ref, start in ((up_core, feats), (up_x, 2 * feats)):
        put_sums(sums[...], ref, start)


def out_weight_grad(grad_attn, gated_rows, mine, mine_x, send, full):
    me = lax.axis_index("hid")
    feats = mine.shape[0]
    full[...] = dot_tn(grad_attn[...], gated_rows[...])
    send[:feats, :] = full[at(me ^ 1, feats), :].astype(bf16)
    send[feats:, :] = full[at(me ^ 3, feats), :].astype(bf16)
    mine[...] = full[at(me, feats), :]
    mine_x[...] = full[at(me ^ 2, feats), :]


def place_units(wi_own, wi_core, own, core_rows, xa, xb, fa, fb, wi, wb):
    me, core, chip, parity = lax.axis_index("hid"), lax.axis_index("hid") & 1, lax.axis_index("hid") // 2, lax.axis_index("rows") & 1
    n, half = xa.shape
    units = wi_own.shape[1]
    wi[:, at(core, units)] = wi_own[...]
    wi[:, at(core ^ 1, units)] = wi_core[...]
    wb[at(me, n), :] = own[:, at(chip, 2 * half)]
    wb[at(me ^ 1, n), :] = core_rows[:, at(chip, 2 * half)]
    for owner, first, second in ((me ^ 2, xa, xb), (me ^ 3, fa, fb)):
        wb[at(owner, n), at(parity, half)] = first[...]
        wb[at(owner, n), at(parity ^ 1, half)] = second[...]


def ffn_forward(
    rows, unit_rows, wi, wb, core_far, act, slope, inter_mine, part, core_pair, inter
):
    n = part.shape[0]
    core_pair[n:, :] = core_far[...]
    ffn_units(rows[: part.shape[0], :], unit_rows, wi, act, slope, inter_mine, core_pair.at[:n, :], inter)
    part[...] = dot_nt(inter[...], wb[...])


def ffn_forward_far(
    rows, unit_rows, wi, wb, act, slope, inter_mine, inter_core, part, inter
):
    ffn_units(rows[: part.shape[0], :], unit_rows, wi, act, slope, inter_mine, inter_core, inter)
    part[...] = dot_nt(inter[...], wb[...]).astype(part.dtype)


def ffn_units(rows, unit_rows, wi, act, slope, inter_mine, inter_core, inter):
    core = lax.axis_index("hid") & 1
    units = wi.shape[1]
    step = 256
    for j in range(units // step):
        cut = slice(j * step, (j + 1) * step)
        u = dot(rows, wi[:, cut]) + unit_rows[0:1, cut]
        cdf = 0.5 * (1.0 + lax.erf(u * 0.7071067811865476))
        value = u * cdf
        act[:, cut] = value
        slope[:, cut] = cdf + u * (jnp.exp(-0.5 * u * u) * 0.3989422804014327)
        inter[:, cut] = (value * unit_rows[1:2, cut]).astype(bf16)
    inter_mine[...] = inter[:, at(core, units // 2)]
    inter_core[...] = inter[:, at(core ^ 1, units // 2)]


def ffn_backward(
    rows, act, slope, unit_rows, wi, wb, gpre_mine, gpre_core, part, sums, gpre,
):
    ffn_units_back(rows, act, slope, unit_rows, wb, gpre_mine, gpre_core, sums, gpre)
    part[...] = dot_nt(gpre[...], wi[...])


def ffn_backward_far(
    rows, act, slope, unit_rows, wi, wb, core_mine, sums_mine,
    gpre_mine, part, sums, core_pair, gpre, all_sums,
):
    core, n = lax.axis_index("hid") & 1, rows.shape[0]
    units = gpre_mine.shape[1]
    core_pair[:n, :] = core_mine[...]
    ffn_units_back(
        rows, act, slope, unit_rows, wb, gpre_mine, core_pair.at[n : 2 * n, :], all_sums, gpre
    )
    part[...] = dot_nt(gpre[...], wi[...]).astype(part.dtype)
    all_sums[...] += sums_mine[...]
    sums[...] = all_sums[:, at(core, units)]
    core_pair[2 * n :, :] = high_low(all_sums[:, at(core ^ 1, units)])


def ffn_units_back(rows, act, slope, unit_rows, wb, gpre_mine, gpre_core, sums, gpre):
    core = lax.axis_index("hid") & 1
    units = wb.shape[1]
    step = 256
    for j in range(units // step):
        cut = slice(j * step, (j + 1) * step)
        ginter = dot(rows[...], wb[:, cut])
        sums[:, cut] = jnp.broadcast_to(
            jnp.sum(ginter * act[:, cut], axis=0, keepdims=True), (8, step)
        )
        gpre[:, cut] = (ginter * unit_rows[1:2, cut] * slope[:, cut]).astype(bf16)
    gpre_mine[...] = gpre[:, at(core, units // 2)]
    gpre_core[...] = gpre[:, at(core ^ 1, units // 2)]


def ffn_weight_grads(
    n0, n1, n2, n3, e0, e1, e_core, p0, p1, p_core, f0, f1, f2, f3,
    back0_keep, back0_send, back1_keep, back1_send, in0_keep, in0_send, in1_keep, in1_send,
    bias_sums, left, right, full,
):
    parity = lax.axis_index("rows") & 1

    def fill(target, pieces):
        start = 0
        for piece in pieces:
            count = piece.shape[0] // 128 * 128
            target[start : start + count, :] = piece[:count, :]
            start += count

    fill(left, (f0, f1, f2, f3))
    fill(right, (e0, e1, e_core))
    full[...] = dot_tn(left[...], right[...])
    owners, parts = 4, 4
    rows = full.shape[0] // (owners * parts)
    for k, (keep, send) in enumerate(((back0_keep, back0_send), (back1_keep, back1_send))):
        for h in range(owners):
            to = slice(h * rows, (h + 1) * rows)
            send[to, :] = full[at(h * parts + 2 * k + (parity ^ 1), rows), :].astype(bf16)
            keep[to, :] = full[at(h * parts + 2 * k + parity, rows), :]
    fill(left, (n0, n1, n2, n3))
    fill(right, (p0, p1, p_core))
    full[...] = dot_tn(left[...], right[...])
    rows = full.shape[0] // 4
    for k, (keep, send) in enumerate(((in0_keep, in0_send), (in1_keep, in1_send))):
        send[...] = full[at(2 * k + (parity ^ 1), rows), :].astype(bf16)
        keep[...] = full[at(2 * k + parity, rows), :]
    bias_sums[...] = jnp.broadcast_to(
        jnp.sum(right[...].astype(f32), axis=0, keepdims=True), bias_sums.shape
    )


def second_norm(
    part, recv, normed, cot0, cot1, n_x, n_far, vecs,
    grad_low, dres, sums, out_mine, out_x, out_send, cots, outs,
):
    me = lax.axis_index("hid")
    feats = cot0.shape[0]
    block = part.shape[0]
    core = me & 1
    cots[at(me, feats), :] = cot0[:, at(me, block)]
    cots[at(me ^ 1, feats), :] = cot1[:, at(me, block)]
    rows = feats // 3
    for owner, pieces in ((me ^ 2, n_x), (me ^ 3, n_far)):
        for k in range(3):
            to = pl.ds(pl.multiple_of(owner * feats + k * rows, rows), rows)
            cots[to, :] = pieces[block:, at(2 * k + core, block)]
    ffn = part[...] + recv[...].astype(f32) + vecs[4:5, :]
    resid = normed[...] + ffn * vecs[9:10, :]
    x_hat, inv = row_norm(resid)
    grad_out = jnp.transpose(cots[...].astype(f32))
    scaled = grad_out * vecs[5:6, :]
    mean_plain = jnp.mean(scaled, axis=1, keepdims=True)
    mean_along = jnp.mean(scaled * x_hat, axis=1, keepdims=True)
    grad_resid = inv * (scaled - mean_plain - x_hat * mean_along)
    low = (grad_resid * vecs[9:10, :]).astype(bf16)
    grad_low[...] = low
    dres[...] = grad_resid
    value = x_hat * vecs[5:6, :] + vecs[6:7, :]
    outs[...] = jnp.transpose(value).astype(bf16)
    out_mine[...] = outs[at(me, feats), :]
    out_x[...] = outs[at(me ^ 2, feats), :]
    out_send[:feats, :] = outs[at(me ^ 1, feats), :]
    out_send[feats:, :] = outs[at(me ^ 3, feats), :]
    sums[0:1, :] = jnp.sum(grad_out * x_hat, axis=0, keepdims=True)
    sums[1:2, :] = jnp.sum(grad_out, axis=0, keepdims=True)
    sums[2:3, :] = jnp.sum(low.astype(f32), axis=0, keepdims=True)
    sums[3:4, :] = jnp.sum(grad_resid * ffn, axis=0, keepdims=True)


VECTORS = 16


def add_vectors(
    head_gate, branch, b_out, gain, bias, hidden_gate, hidden_mask, b_back, ctx_core, ctx_x,
    send_core, send_x, columns, rows,
):
    feats = b_out.shape[0]

    def row(ref):
        return ref[...].reshape(1, ref.shape[0])

    cols = row(hidden_gate) * row(hidden_mask).astype(f32)
    rows[...] = jnp.zeros_like(rows)
    rows[0:1, :feats] = row(b_out)
    rows[1:2, :feats] = gain[0:1, :]
    rows[2:3, :feats] = bias[0:1, :]
    rows[3:4, :feats] = cols
    rows[4:5, :feats] = row(b_back)
    rows[5:6, :feats] = gain[1:2, :]
    rows[6:7, :feats] = bias[1:2, :]
    rows[7:8, :feats] = jnp.concatenate(
        [jnp.full((1, HEAD_DIM), head_gate[i], f32) for i in range(feats // HEAD_DIM)], axis=1
    )
    rows[8:9, :feats] = branch[0] * cols
    rows[9:10, :feats] = branch[1] * cols
    rest = jnp.transpose(rows[...])[:feats, :]
    columns[...] = jnp.zeros_like(columns)
    for k in range(3):
        low = rest.astype(bf16)
        columns[:, k * VECTORS : (k + 1) * VECTORS] = low
        rest = rest - low.astype(f32)
    for send, ctx in ((send_core, ctx_core), (send_x, ctx_x)):
        n = ctx.shape[0]
        send[:n, :] = ctx[...]
        send[n:, :] = columns[...]


def place_vectors(p0, p1, p2, p3, b_in, gate, b_in_core, gate_core, vecs, unit_rows, cols):
    me, core = lax.axis_index("hid"), lax.axis_index("hid") & 1
    feats = cols.shape[0] // 4
    units = b_in.shape[0]
    for k, piece in enumerate((p0, p1.at[feats:, :], p2.at[2 * feats :, :], p3.at[2 * feats :, :])):
        parts = piece[...].astype(f32)
        cols[at(me ^ k, feats), :] = (
            parts[:, :VECTORS] + parts[:, VECTORS : 2 * VECTORS]
        ) + parts[:, 2 * VECTORS : 3 * VECTORS]
    vecs[...] = jnp.transpose(cols[...])
    for k, (one, two) in enumerate(((b_in, gate), (b_in_core, gate_core))):
        unit_rows[0:1, at(core ^ k, units)] = one[...].reshape(1, units)
        unit_rows[1:2, at(core ^ k, units)] = two[...].reshape(1, units)


def vector_outputs(
    branch, head_gate, vec, vecs, hidden_mask,
    g_qv, g_bout, g_bin, g_bback, g_gain, g_bias, g_head, g_inter, g_branch, g_hidden, cols,
):
    me = lax.axis_index("hid")
    feats = g_bout.shape[0]
    cols[...] = jnp.transpose(vec[0:8, :])
    own = jnp.transpose(cols[at(me, feats), :])
    g_gain[0:1, :] = own[0:1, :]
    g_gain[1:2, :] = own[4:5, :]
    g_bias[0:1, :] = own[1:2, :]
    g_bias[1:2, :] = own[5:6, :]
    g_bout[...] = own[2, :]
    g_bback[...] = own[6, :]
    mask = hidden_mask[...].astype(f32)
    g_hidden[...] = (branch[0] * own[3, :] + branch[1] * own[7, :]) * mask
    g_inter[...] = vec[8, :]
    g_bin[...] = vec[9, :]
    g_qv[0:1, :] = vec[10:11, :feats]
    rolled = vec[10:11, 2 * feats : 3 * feats]
    g_qv[1:2, :] = rolled
    lane = lax.broadcasted_iota(jnp.int32, (1, 128), 1)
    gates = jnp.ones((1, 128), f32)
    for i in range(feats // HEAD_DIM):
        gates = jnp.where(lane == i, head_gate[i], gates)
    g_head[...] = (vec[11:12, :128] / gates)[0, : feats // HEAD_DIM]
    part0 = jnp.sum(vec[3:4, :] * vecs[3:4, :], axis=1, keepdims=True)
    part1 = jnp.sum(vec[7:8, :] * vecs[3:4, :], axis=1, keepdims=True)
    both = jnp.where(lane == 0, part0, part1)
    g_branch[...] = both[0, :2]


def row_place():
    row = lax.axis_index("rows")
    return row & 1, (row >> 1) & 3


def first_add(keep, recv, total, send):
    total[...] = keep[...] + recv[...].astype(f32)
    send[...] = total[...].astype(bf16)


def first_add_pair(keep, pair, recv, total, send):
    n = keep.shape[0]
    total[...] = keep[...] + recv[:n, :].astype(f32)
    send[:n, :] = total[...].astype(bf16)
    send[n:, :] = high_low(pair_value(pair) + pair_value(recv[n:, :]))


def second_add(keep, recv, send):
    send[...] = (keep[...] + recv[...].astype(f32)).astype(bf16)


def second_add_pair(keep, mine, recv, send):
    n = keep.shape[0]
    send[:n, :] = (keep[...] + recv[:n, :].astype(f32)).astype(bf16)
    send[n:, :] = high_low(pair_value(mine[n:, :]) + pair_value(recv[n:, :]))


def third_add(mine, recv, total):
    total[...] = (mine[...].astype(f32) + recv[...].astype(f32)).astype(bf16)


def third_add_pair(mine, recv, total):
    n = mine.shape[0] - 32
    total[:n, :] = (mine[:n, :].astype(f32) + recv[:n, :].astype(f32)).astype(bf16)
    total[n:, :] = high_low(pair_value(mine[n:, :]) + pair_value(recv[n:, :]))


def choose(mine, recv, total):
    z = row_place()[1]
    outer = (z == 0) | (z == 3)
    total[...] = jnp.where(outer, recv[...], mine[...])


def choose_pair(mine, recv, total, vec):
    n = total.shape[0]
    z = row_place()[1]
    outer = (z == 0) | (z == 3)
    total[...] = jnp.where(outer, recv[:n, :], mine[:n, :])
    vec[...] = jnp.where(outer, pair_value(recv[n:, :]), pair_value(mine[n:, :]))


def split_owners(mine, recv, own, own_x, send):
    me = lax.axis_index("hid")
    n = own.shape[0]

    def rows(k):
        total = mine[at(me ^ k, n), :].astype(f32) + recv[at(me ^ k, n), :].astype(f32)
        return total.astype(bf16)

    own[...] = rows(0)
    own_x[...] = rows(2)
    send[:n, :] = rows(1)
    send[n:, :] = rows(3)


def join_owners(mine, from_core, from_x, chunk):
    me, n = lax.axis_index("hid"), mine.shape[0]
    chunk[at(me, n), :] = mine[...]
    chunk[at(me ^ 1, n), :] = from_core[:n, :]
    chunk[at(me ^ 2, n), :] = from_x[:n, :]
    chunk[at(me ^ 3, n), :] = from_x[n:, :]


def in_gradient(mine0, other0, mine1, other1, grad):
    y = row_place()[0]
    n = mine0.shape[0]
    for k, (mine, other) in enumerate(((mine0, other0), (mine1, other1))):
        grad[at(2 * k + y, n), :] = mine[...].astype(f32)
        grad[at(2 * k + (y ^ 1), n), :] = other[...].astype(f32)


def back_gradient(mine0, other0, mine1, other1, grad):
    y = row_place()[0]
    units = mine0.shape[1]
    n = mine0.shape[0] // 4
    for k, (mine, other) in enumerate(((mine0, other0), (mine1, other1))):
        for side, half in ((y, mine), (y ^ 1, other)):
            for owner in range(4):
                block = half[owner * n : (owner + 1) * n, :].astype(f32)
                grad[at(2 * k + side, n), owner * units : (owner + 1) * units] = block


def attn_gradients(qk_mine, qk_other, vo_mine, vo_other, grad_qkv, grad_out):
    y = row_place()[0]
    n = qk_mine.shape[0]
    grad_qkv[at(y, n), :] = qk_mine[...].astype(f32)
    grad_qkv[at(y ^ 1, n), :] = qk_other[...].astype(f32)
    mine, other = vo_mine[...].astype(f32), vo_other[...].astype(f32)
    grad_qkv[2 * n :, :] = jnp.where(y == 0, mine, other)
    grad_out[...] = jnp.where(y == 0, other, mine)


def second_half(mine, recv, both):
    n = mine.shape[0]
    both[:n, :] = mine[...]
    both[n:, :] = recv[n:, :]


EARLY_TURNS = "313"
TURNS = "41q3v2413241v2341q122vg132q4v12q4vg2qegvq"
FIRST = ("in0", "back0")


def along(block, way="y"):
    pairs = []
    for i in range(lax.axis_size("rows")):
        z = (i >> 1) & 3
        step = {
            "y": 1 - 2 * (i & 1),
            "in": {0: 2, 3: -2}.get(z),
            "mid": {1: 2, 2: -2}.get(z),
            "out": {1: -2, 2: 2}.get(z),
        }[way]
        if step is not None:
            pairs.append((i, i + step))
    return lax.ppermute(block, "rows", pairs)


class Turns:
    def __init__(self):
        self.last = ()

    def held(self, block):
        return after(block, *self.last) if self.last else block

    def mark(self, *blocks):
        self.last = blocks


def far_rows_sum(chunk):
    count = lax.axis_size("rows")
    if count == 8:
        return chunk
    groups = [[i + 8 * j for j in range(count // 8)] for i in range(8)]
    return lax.psum(chunk.astype(f32), "rows", axis_index_groups=groups).astype(chunk.dtype)


def shards(
    tokens, w_qkv, b_qv, w_out, b_out, w_in, b_in, w_back, b_back, norm_gain, norm_bias,
    head_gate, inter_gate, branch_gate, hidden_gate, hidden_mask, doc_lengths, cotangent,
):
    feats, toks = tokens.shape
    width = 4 * feats
    units = w_in.shape[1]
    block = toks // 4
    given = jnp.concatenate(
        [
            b_qv,
            jnp.pad(head_gate, (0, feats - head_gate.shape[0]))[None],
            jnp.pad(doc_lengths.astype(f32), ((0, 0), (0, feats - doc_lengths.shape[1]))),
        ],
        0,
    )
    bounds, small, out_half, back_half = local_kernel(
        begin,
        "begin",
        (given, w_out, w_back),
        "VVV",
        [
            sds((8, toks), jnp.int32),
            sds((8, 256), f32),
            sds((feats // 2, width), bf16),
            sds((feats, units), bf16),
        ],
    )
    tokens_x = swap(tokens, "hid", 2)
    tokens_core = swap(tokens, "hid", 1)
    x_own = swap(after(tokens_core, back_half), "hid", 1)
    out_xa = swap(out_half, "hid", 2)
    back_xa = swap(back_half, "hid", 2)
    wi_core = swap(w_in, "hid", 1)
    wo_core = swap(w_out, "hid", 1)
    b_in_core = swap(b_in, "hid", 1)
    gate_core = swap(inter_gate, "hid", 1)
    back_core = swap(w_back, "hid", 1)
    tokens_far = swap(
        after(tokens_x, tokens_core, wi_core, wo_core, back_core, back_half), "hid", 1
    )

    head_block = sds((feats, block), bf16)
    two_blocks = sds((2 * feats, block), bf16)
    x_all, qkv, logsum, g0, g_core, g_x, x_block = local_kernel(
        attn_forward,
        "attn_forward",
        (
            bounds, small, x_own, tokens_core, tokens_x, tokens_far, w_qkv,
        ),
        "V" * 7,
        [
            sds((width, toks), bf16),
            sds((3, feats, toks), bf16),
            sds((8, toks), f32),
            head_block,
            head_block,
            two_blocks,
            sds((width, block), bf16),
        ],
        [pltpu.VMEM((feats, toks), bf16), pltpu.VMEM((toks, toks), f32)],
        micros=5.4,
    )
    cot_core = swap(after(cotangent, x_block), "hid", 1)
    send_core, send_x, columns = local_kernel(
        add_vectors,
        "add_vectors",
        (
            head_gate, branch_gate, after(b_out, x_block), norm_gain, norm_bias, hidden_gate,
            hidden_mask, b_back, g_core, g_x,
        ),
        "SS" + "V" * 8,
        [two_blocks, sds((3 * feats, block), bf16), head_block],
        [pltpu.VMEM((VECTORS, 256), f32)],
    )
    g2 = swap(send_x, "hid", 2)
    g1 = swap(send_core, "hid", 1)
    g3 = swap(after(g2, g1, b_in_core, gate_core), "hid", 1)
    out_xb = swap(after(out_xa, g0), "rows", 1)
    out_fa = swap(after(out_xa, g0), "hid", 1)
    out_fb = swap(out_xb, "hid", 1)
    back_xb = swap(after(back_xa, g1), "rows", 1)
    back_fa = swap(after(back_xa, g1), "hid", 1)
    (wo,) = local_kernel(
        place_rows,
        "place_rows",
        (w_out, wo_core, out_xa, out_xb, out_fa, out_fb),
        "VVVVVV",
        [sds((width, width), bf16)],
    )
    vecs, unit_rows = local_kernel(
        place_vectors,
        "place_vectors",
        (columns, g1, g2, g3, b_in, inter_gate, b_in_core, gate_core),
        "V" * 8,
        [sds((VECTORS, width), f32), sds((2, 2 * units), f32)],
        [pltpu.VMEM((width, VECTORS), f32)],
    )

    normed, n_send, hat, inv, attn_pre, gated_rows = local_kernel(
        attn_out,
        "attn_out",
        (g0, g1, g2, g3, x_block, vecs, wo, cotangent),
        "VVVVVVVV",
        [
            sds((block, width), f32),
            sds((block + feats // 3, width), bf16),
            sds((block, width), f32),
            sds((block, 128), f32),
            sds((block, width), f32),
            sds((block, width), bf16),
        ],
        [pltpu.VMEM((width, block), bf16)],
        micros=1.3,
    )

    n_x = swap(n_send, "hid", 2)
    n_core = swap(n_send, "hid", 1)
    back_fb = swap(after(back_xb, n_x), "hid", 1)
    wi, wb = local_kernel(
        place_units,
        "place_units",
        (w_in, wi_core, w_back, back_core, back_xa, back_xb, back_fa, back_fb),
        "V" * 8,
        [sds((width, 2 * units), bf16), sds((width, 2 * units), bf16)],
        micros=0.85,
    )

    act_block = sds((block, 2 * units), f32)
    half_block = sds((block, units), bf16)
    pair_block = sds((2 * block, units), bf16)
    rows_block = sds((block, width), bf16)
    ffn_scratch = [pltpu.VMEM((block, 2 * units), bf16)]
    act_x, slope_x, e1, inter_core, ffn_send = local_kernel(
        ffn_forward_far,
        "ffn_forward_far",
        (n_x, unit_rows, wi, wb),
        "VVVV",
        [act_block, act_block, half_block, half_block, rows_block],
        ffn_scratch,
        micros=1.85,
    )
    ffn_recv = swap(ffn_send, "hid", 2)
    act, slope, e0, ffn_part, e_pair = local_kernel(
        ffn_forward,
        "ffn_forward",
        (after(n_send, ffn_send), unit_rows, wi, wb, inter_core),
        "VVVVV",
        [act_block, act_block, half_block, sds((block, width), f32), pair_block],
        ffn_scratch,
        micros=1.85,
    )
    n_far = swap(after(n_x, ffn_send), "hid", 1)

    out_block = sds((feats, block), bf16)
    gffn, dres2, sums2, res_mine, res_x, res_send = local_kernel(
        second_norm,
        "second_norm",
        (
            after(ffn_part, n_core), ffn_recv, normed, cotangent, cot_core, n_x, n_far, vecs,
        ),
        "V" * 8,
        [
            sds((block, width), bf16),
            sds((block, width), f32),
            sds((4, width), f32),
            out_block,
            out_block,
            sds((2 * feats, block), bf16),
        ],
        [pltpu.VMEM((width, block), bf16), pltpu.VMEM((width, block), bf16)],
        micros=1.2,
    )

    gffn_x = swap(gffn, "hid", 2)
    e_core = swap(after(e_pair, gffn), "hid", 1)
    f2 = swap(gffn, "hid", 1)
    sums_block = sds((8, 2 * units), f32)
    p0, gpre_core, gn_part, ig_sum = local_kernel(
        ffn_backward,
        "ffn_backward",
        (gffn, act, slope, unit_rows, wi, wb),
        "VVVVVV",
        [half_block, half_block, sds((block, width), f32), sums_block],
        ffn_scratch,
        micros=1.85,
    )
    p1, gn_send, ig_mine, p_pair = local_kernel(
        ffn_backward_far,
        "ffn_backward_far",
        (after(gffn_x, f2, e_core), act_x, slope_x, unit_rows, wi, wb, gpre_core, ig_sum),
        "VVVVVVVV",
        [half_block, rows_block, sds((8, units), f32), sds((2 * block + 16, units), bf16)],
        ffn_scratch + [pltpu.VMEM((8, 2 * units), f32)],
        micros=1.85,
    )
    gn_recv = swap(gn_send, "hid", 2)
    f3 = swap(after(gffn_x, gn_send), "hid", 1)
    p_core = swap(p_pair, "hid", 1)
    *pieces, bin_sum = local_kernel(
        ffn_weight_grads,
        "ffn_weight_grads",
        (
            n_send, n_x, n_core, n_far, e0, e1, e_core,
            p0, p1, p_core, gffn, gffn_x, f2, f3,
        ),
        "V" * 14,
        [
            sds((feats, units), f32),
            sds((feats, units), bf16),
            sds((feats, units), f32),
            sds((feats, units), bf16),
            sds((feats, units), f32),
            sds((feats, units), bf16),
            sds((feats, units), f32),
            sds((feats, units), bf16),
            sds((8, units), f32),
        ],
        [
            pltpu.VMEM((toks, width), bf16),
            pltpu.VMEM((toks, units), bf16),
            pltpu.VMEM((width, units), f32),
        ],
        micros=2.5,
    )

    pieces = dict(zip(("back0", "back1", "in0", "in1"), zip(pieces[0::2], pieces[1::2])))
    early = {name: along(after(pieces[name][1], gn_recv)) for name in FIRST}

    sum_rows = 16 * width // 128
    dres1, gattn, sums1, u0, up_core, up_x = local_kernel(
        attn_out_back,
        "attn_out_back",
        (
            after(gn_part, pieces["in1"][1]), gn_recv, dres2, hat, inv, attn_pre,
            vecs, wo, sums2,
        ),
        "V" * 9,
        [
            sds((block, width), f32),
            sds((block, width), bf16),
            sds((8, width), f32),
            head_block,
            sds((feats + sum_rows, block), bf16),
            sds((2 * feats + sum_rows, block), bf16),
        ],
        [pltpu.VMEM((width, block), bf16)],
        micros=1.3,
    )
    u2 = swap(up_x, "hid", 2)
    u1 = swap(up_core, "hid", 1)
    u3 = swap(u2, "hid", 1)

    weight_block = sds((feats, width), f32)
    low_block = sds((feats, width), bf16)
    wo_mine, wo_keep, wo_send = local_kernel(
        out_weight_grad,
        "out_weight_grad",
        (gattn, gated_rows),
        "VV",
        [weight_block, weight_block, sds((2 * feats, width), bf16)],
        [pltpu.VMEM((width, width), f32)],
        micros=1.2,
    )
    wo_grad_core = swap(after(wo_send, u1), "hid", 1)

    turns = Turns()
    results = {}
    whole_block = sds((feats, width), f32)

    def step(body, args, outs, **more):
        outs = local_kernel(
            body, body.__name__, (turns.held(args[0]),) + args[1:], "V" * len(args), outs, **more
        )
        turns.mark(*outs[-1:])
        return outs

    def sum_chain(name, keep, send, recv=None):
        if recv is None:
            recv = along(turns.held(send))
        yield
        keep, send = step(first_add, (keep, recv), [whole_block, low_block])
        recv = along(send, "in")
        yield
        (mine,) = step(second_add, (keep, recv), [low_block])
        recv = along(mine, "mid")
        yield
        if name.startswith("back"):
            part = sds((feats // 4, units), bf16)
            two = sds((feats // 2, units), bf16)
            mine, mine_x, send = step(split_owners, (mine, recv), [part, part, two])
            from_core = swap(send, "hid", 1)
            yield
            (send,) = step(second_half, (mine_x, from_core), [two])
            from_x = swap(send, "hid", 2)
            yield
            (mine,) = step(join_owners, (mine, from_core, from_x), [low_block])
        else:
            (mine,) = step(third_add, (mine, recv), [low_block])
        recv = along(mine, "out")
        yield
        (mine,) = step(choose, (mine, recv), [low_block])
        yield from last_part(name, mine)

    def last_part(name, mine):
        mine = far_rows_sum(mine)
        other = along(mine)
        yield
        results[name] = (mine, other)
        if name in ("in0", "in1") and "in0" in results and "in1" in results:
            (results["w_in"],) = step(
                in_gradient,
                results["in0"] + results["in1"],
                [sds((width, units), f32)],
                micros=2.1,
            )
        if name in ("back0", "back1") and "back0" in results and "back1" in results:
            (results["w_back"],) = step(
                back_gradient,
                results["back0"] + results["back1"],
                [sds((feats, 4 * units), f32)],
                micros=2.1,
            )
        if name in ("qk", "vo") and "qk" in results and "vo" in results:
            results["w_qkv"], results["w_out"] = step(
                attn_gradients,
                results["qk"] + results["vo"],
                [sds((3 * feats, width), f32), weight_block],
                micros=2.1,
            )

    chains = {
        key: sum_chain(name, *pieces[name], early.get(name))
        for key, name in zip("1234", ("back0", "back1", "in0", "in1"))
    }
    turns.mark(u1)
    for turn in EARLY_TURNS:
        next(chains[turn], None)
    grads, head_sums, bias_sums = local_kernel(
        attn_backward,
        "attn_backward",
        (bounds, turns.held(qkv), logsum, u0, u1, u2, u3),
        "V" * 7,
        [
            sds((3 * feats, toks), bf16),
            sds((8, block), f32),
            sds((8, 3 * feats), f32),
        ],
        [pltpu.VMEM((feats, toks), bf16), pltpu.VMEM((toks, toks), f32)],
        micros=5.0,
    )
    (wo_low,) = local_kernel(add_second, "wo_low", (wo_keep, wo_grad_core), "VV", [low_block])
    wo_far = swap(after(wo_low, u3), "hid", 2)

    gx_block = sds((feats, toks), f32)
    gx_low = sds((feats, toks), bf16)

    def qk_chain():
        with_pair = sds((feats + 32, width), bf16)
        keep, send, pair = local_kernel(
            qk_weight_grad,
            "qk_weight_grad",
            (
                turns.held(grads), x_all, sums1, u1, u2, u3, ig_mine, p_core, bin_sum,
                head_sums, bias_sums,
            ),
            "V" * 11,
            [weight_block, with_pair, sds((32, width), bf16)],
            [pltpu.VMEM((2 * feats, width), f32), pltpu.VMEM((16, width), f32)],
            micros=1.2,
        )
        turns.mark(send)
        recv = along(send)
        yield
        keep, send = step(first_add_pair, (keep, pair, recv), [weight_block, with_pair])
        recv = along(send, "in")
        yield
        (mine,) = step(second_add_pair, (keep, send, recv), [with_pair])
        recv = along(mine, "mid")
        yield
        (mine,) = step(third_add_pair, (mine, recv), [with_pair])
        recv = along(mine, "out")
        yield
        mine, results["sums"] = step(
            choose_pair, (mine, recv), [low_block, sds((16, width), f32)]
        )
        yield from last_part("qk", mine)

    def vo_chain():
        keep, send = local_kernel(
            vo_weight_grad,
            "vo_weight_grad",
            (turns.held(grads), x_all, wo_mine, wo_grad_core, wo_far),
            "VVVVV",
            [weight_block, low_block],
            [pltpu.VMEM((2 * feats, width), f32)],
            micros=1.1,
        )
        turns.mark(send)
        yield from sum_chain("vo", keep, send, along(send))

    def tokens_chain():
        mine, mine_x, send = local_kernel(
            qkv_input_grad,
            "qkv_input_grad",
            (turns.held(grads), w_qkv, dres1, res_send),
            "VVVV",
            [gx_block, gx_block, sds((2 * feats, toks + block), bf16)],
            [pltpu.VMEM((width, toks), f32)],
            micros=1.5,
        )
        turns.mark(send)
        from_core = swap(send, "hid", 1)
        yield
        (send,) = local_kernel(
            tokens_step,
            "tokens_step",
            (turns.held(mine_x), res_x, from_core),
            "VVV",
            [sds((feats, toks + 2 * block), bf16)],
        )
        turns.mark(send)
        from_x = swap(send, "hid", 2)
        yield
        results["tokens"], results["output"] = local_kernel(
            tokens_outputs,
            "tokens_outputs",
            (turns.held(mine), res_mine, from_core, from_x),
            "VVVV",
            [gx_low, gx_low],
            micros=1.2,
        )
        turns.mark(results["tokens"])

    def vector_chain():
        results["vectors"] = local_kernel(
            vector_outputs,
            "vector_outputs",
            (branch_gate, head_gate, far_rows_sum(turns.held(results["sums"])), vecs, hidden_mask),
            "SSVVV",
            [
                sds((2, feats), f32),
                sds((feats,), f32),
                sds((units,), f32),
                sds((feats,), f32),
                sds((2, feats), f32),
                sds((2, feats), f32),
                sds((feats // HEAD_DIM,), f32),
                sds((units,), f32),
                sds((2,), f32),
                sds((feats,), f32),
            ],
            [pltpu.VMEM((width, 8), f32)],
            micros=1.4,
        )
        turns.mark(results["vectors"][0])
        yield

    chains.update(q=qk_chain(), v=vo_chain(), g=tokens_chain(), e=vector_chain())
    turns.mark(grads)
    for turn in TURNS:
        next(chains[turn], None)
    (
        grad_b_qv, grad_b_out, grad_b_in, grad_b_back, grad_norm_gain, grad_norm_bias,
        grad_head_gate, grad_inter_gate, grad_branch_gate, grad_hidden_gate,
    ) = results["vectors"]
    output, grad_tokens = results["output"], results["tokens"]
    grad_w_qkv = results["w_qkv"].reshape(3, feats, width)
    grad_w_out, grad_w_in, grad_w_back = results["w_out"], results["w_in"], results["w_back"]
    return (
        output,
        grad_tokens,
        grad_w_qkv,
        grad_b_qv,
        grad_w_out,
        grad_b_out,
        grad_w_in,
        grad_b_in,
        grad_w_back,
        grad_b_back,
        grad_norm_gain,
        grad_norm_bias,
        grad_head_gate,
        grad_inter_gate,
        grad_branch_gate,
        grad_hidden_gate,
    )


def solution(mesh):
    return jax.shard_map(
        shards,
        mesh=mesh,
        in_specs=(
            P("hid", "rows"),
            P(None, "hid", None),
            P(None, "hid"),
            P("hid", None),
            P("hid"),
            P(None, "hid"),
            P("hid"),
            P("hid", None),
            P("hid"),
            P(None, "hid"),
            P(None, "hid"),
            P("hid"),
            P("hid"),
            P(),
            P("hid"),
            P("hid"),
            P("rows", None),
            P("hid", "rows"),
        ),
        out_specs=(
            P("hid", "rows"),
            P("hid", "rows"),
            P(None, "hid", None),
            P(None, "hid"),
            P("hid", None),
            P("hid"),
            P(None, "hid"),
            P("hid"),
            P("hid", None),
            P("hid"),
            P(None, "hid"),
            P(None, "hid"),
            P("hid"),
            P("hid"),
            P(),
            P("hid"),
        ),
        check_vma=False,
    )
```

```python
import jax
import jax.numpy as jnp
from jax import lax
from jax.experimental import pallas as pl
from jax.experimental.pallas import tpu as pltpu
from jax.sharding import PartitionSpec as P

HEAD_DIM = 64
norm_eps = 1e-06
masked_score = -1e30
bf16 = jnp.bfloat16
f32 = jnp.float32
MIB = 1 << 20
WIDE = 512
HBM_BYTES_PER_MICRO = 3690000

SPECS = {
    "S": pl.BlockSpec(memory_space=pltpu.SMEM),
    "V": pl.BlockSpec(memory_space=pltpu.VMEM),
}


def swap(block, axis, bit):
    return lax.ppermute(block, axis, [(i, i ^ bit) for i in range(lax.axis_size(axis))])


def after(block, *others):
    return lax.optimization_barrier((block, *others))[0]


def sds(shape, dtype):
    return jax.ShapeDtypeStruct(shape, dtype)


def local_kernel(body, name, args, kinds, outs, scratch=(), micros=0.6, vmem=16):
    return pl.pallas_call(
        body,
        name=name,
        out_shape=outs,
        in_specs=[SPECS[k] for k in kinds],
        out_specs=[SPECS["V"]] * len(outs),
        scratch_shapes=list(scratch),
        compiler_params=pltpu.CompilerParams(vmem_limit_bytes=vmem * MIB),
        cost_estimate=pl.CostEstimate(
            flops=1, bytes_accessed=int(micros * HBM_BYTES_PER_MICRO), transcendentals=0
        ),
    )(*args)


def dot(left, right):
    return jnp.dot(left, right, preferred_element_type=f32)


def dot_nt(left, right):
    return lax.dot_general(left, right, (((1,), (1,)), ((), ())), preferred_element_type=f32)


def dot_tn(left, right):
    return lax.dot_general(left, right, (((0,), (0,)), ((), ())), preferred_element_type=f32)


def at(index, size):
    return pl.ds(pl.multiple_of(index * size, size), size)


def begin(given, w_out, w_back, bounds, small, out_half, back_half):
    toks = bounds.shape[1]
    query = lax.broadcasted_iota(jnp.int32, (1, toks), 1).astype(f32)
    start, stop = jnp.zeros_like(query), jnp.zeros_like(query)
    end = jnp.zeros((1, 1), f32)
    for j in range(4):
        first, end = end, end + given[3:4, j : j + 1]
        inside = (query >= first) & (query < end)
        start = jnp.where(inside, first, start)
        stop = jnp.where(inside, end, stop)
    bounds[0:1, :] = start.astype(jnp.int32)
    bounds[1:2, :] = stop.astype(jnp.int32)
    feats = given.shape[1]
    small[...] = jnp.zeros_like(small)
    small[0:2, :feats] = given[0:2, :]
    heads = feats // HEAD_DIM
    small[2:3, :feats] = jnp.concatenate(
        [jnp.broadcast_to(given[2:3, i : i + 1], (1, HEAD_DIM)) for i in range(heads)], axis=1
    )
    other, parity = 1 - lax.axis_index("hid") // 2, lax.axis_index("rows") & 1
    out_half[...] = w_out[at(parity, out_half.shape[0]), :]
    back_half[...] = w_back[:, at(2 * other + parity, back_half.shape[1])]


def fill_mask(bounds, mask):
    toks = mask.shape[0]
    for j in range(toks // WIDE):
        chunk = slice(j * WIDE, (j + 1) * WIDE)
        position = lax.broadcasted_iota(jnp.int32, (toks, WIDE), 0)
        same = (position >= bounds[0:1, chunk]) & (position < bounds[1:2, chunk])
        mask[:, chunk] = jnp.where(same, 0.0, masked_score)


def attn_forward(
    bounds, small, x0, x1, x2, x3, w_qkv,
    x_all, qkv, logsum, mine, send_core, send_x, x_block, gated, mask,
):
    me = lax.axis_index("hid")
    feats, toks = x0.shape
    block = toks // 4
    for k, piece in enumerate((x0, x1, x2, x3)):
        x_all[at(me ^ k, feats), :] = piece[...]
    x_block[...] = x_all[:, at(me, block)]
    cols = jnp.transpose(small[...])
    for c in range(3):
        rows = dot(w_qkv[c], x_all[...])
        if c != 1:
            rows = rows + cols[:feats, c // 2 : c // 2 + 1]
        rows = rows.astype(bf16)
        if c == 0:
            rows = rows * jnp.asarray(HEAD_DIM ** (-0.5), bf16)
        qkv[c] = rows
    fill_mask(bounds, mask)
    heads = feats // HEAD_DIM
    for head in range(heads):
        span = slice(head * HEAD_DIM, (head + 1) * HEAD_DIM)
        keys = jnp.transpose(qkv[1, span, :])
        values = qkv[2, span, :]
        for j in range(4 * block // WIDE):
            chunk = slice(j * WIDE, (j + 1) * WIDE)
            scores = dot(keys, qkv[0, span, chunk])
            scores = scores + mask[:, chunk]
            peak = jnp.max(scores, axis=0, keepdims=True)
            expo = jnp.exp(scores - peak)
            total = jnp.sum(expo, axis=0, keepdims=True)
            probs = (expo * (1.0 / total)).astype(bf16)
            logsum[head : head + 1, chunk] = peak + jnp.log(total)
            gated[span, chunk] = (dot(values, probs) * cols[span, 2:3]).astype(bf16)
    mine[...] = gated[:, at(me, block)]
    send_x[:feats, :] = gated[:, at(me ^ 2, block)]
    send_x[feats:, :] = gated[:, at(me ^ 3, block)]
    send_core[...] = gated[:, at(me ^ 1, block)]


def attn_backward(
    bounds, qkv, logsum, u0, u1, u2, u3, grads, head_sums, bias_sums, up, mask
):
    me = lax.axis_index("hid")
    feats, block = u0.shape
    pieces = (u0, u1.at[:feats, :], u2.at[:feats, :], u3.at[feats : 2 * feats, :])
    for k, piece in enumerate(pieces):
        up[:, at(me ^ k, block)] = piece[...]
    fill_mask(bounds, mask)
    heads = feats // HEAD_DIM
    head_sums[...] = jnp.zeros_like(head_sums)
    for head in range(heads):
        span = slice(head * HEAD_DIM, (head + 1) * HEAD_DIM)
        queries, keys_t, values_t = (qkv[c, span, :] for c in range(3))
        keys = jnp.transpose(keys_t)
        values = jnp.transpose(values_t)
        upstream = up[span, :]
        grad_k = jnp.zeros((HEAD_DIM, 4 * block), f32)
        grad_v = jnp.zeros((HEAD_DIM, 4 * block), f32)
        inner_sum = jnp.zeros((1, WIDE), f32)
        for j in range(4 * block // WIDE):
            chunk = slice(j * WIDE, (j + 1) * WIDE)
            scores = dot(keys, queries[:, chunk])
            scores = scores + mask[:, chunk]
            probs = jnp.exp(scores - logsum[head : head + 1, chunk])
            grad_p = dot(values, upstream[:, chunk])
            weighted = probs * grad_p
            inner = jnp.sum(weighted, axis=0, keepdims=True)
            inner_sum = inner_sum + inner
            grad_s = (weighted - probs * inner).astype(bf16)
            grad_v = grad_v + dot_nt(upstream[:, chunk], probs.astype(bf16))
            grad_k = grad_k + dot_nt(queries[:, chunk], grad_s)
            grads[span, chunk] = (dot(keys_t, grad_s) * HEAD_DIM ** (-0.5)).astype(bf16)
        for c, grad in ((1, grad_k), (2, grad_v)):
            rows = slice(c * feats + head * HEAD_DIM, c * feats + (head + 1) * HEAD_DIM)
            grads[rows, :] = grad.astype(bf16)
        head_sums[head : head + 1, :] = sum(
            inner_sum[:, k * block : (k + 1) * block] for k in range(WIDE // block)
        )
    ones = jnp.ones((8, 4 * block), bf16)
    bias_sums[...] = dot_nt(ones, grads[...])


def all_sums(sums, u1, u2, u3, ig_mine, p_core, bin_sum, head_sums, bias_sums, vec):
    blocks = sums.shape[1] // 128
    feats = (u2.shape[0] - 16 * blocks) // 2
    total = sums[...] + get_sums(u1, feats, 8, blocks)
    vec[0:8, :] = (total + get_sums(u2, 2 * feats, 8, blocks)) + get_sums(u3, 2 * feats, 8, blocks)
    vec[8:, :] = jnp.zeros((vec.shape[0] - 8, vec.shape[1]), f32)
    pair = p_core[p_core.shape[0] - 16 :, :].astype(f32)
    vec[8:9, :] = ig_mine[0:1, :] + (pair[0:1, :] + pair[8:9, :])
    vec[9:10, :] = bin_sum[0:1, :]
    width = bias_sums.shape[1]
    vec[10:11, :width] = bias_sums[0:1, :]
    vec[11:12, :8] = jnp.sum(jnp.transpose(head_sums[...]), axis=0, keepdims=True)


def pair_value(pair):
    n = pair.shape[0] // 2
    return pair[:n, :].astype(f32) + pair[n:, :].astype(f32)


def qk_weight_grad(
    grads, x_all, sums, u1, u2, u3, ig_mine, p_core, bin_sum, head_sums, bias_sums,
    keep, send, pair, full, vec,
):
    parity = lax.axis_index("rows") & 1
    n = keep.shape[0]
    full[...] = dot_nt(grads[: 2 * n, :], x_all[...])
    all_sums(sums, u1, u2, u3, ig_mine, p_core, bin_sum, head_sums, bias_sums, vec)
    send[:n, :] = full[at(parity ^ 1, n), :].astype(bf16)
    send[n:, :] = high_low(vec[...])
    pair[...] = high_low(vec[...])
    keep[...] = full[at(parity, n), :]


def vo_weight_grad(grads, x_all, wo_mine, wo_core, wo_far, keep, send, full):
    parity = lax.axis_index("rows") & 1
    n = keep.shape[0]
    full[:n, :] = dot_nt(grads[2 * n :, :], x_all[...])
    full[n:, :] = wo_mine[...] + wo_core[:n, :].astype(f32) + wo_far[...].astype(f32)
    send[...] = full[at(parity ^ 1, n), :].astype(bf16)
    keep[...] = full[at(parity, n), :]


def add_low(mine, other, total):
    total[...] = (mine[...].astype(f32) + other[...].astype(f32)).astype(total.dtype)


def add_second(mine, other, total):
    n = mine.shape[0]
    total[...] = (mine[...] + other[n:, :].astype(f32)).astype(total.dtype)


def tokens_step(mine, res_x, recv, send):
    n, toks = mine.shape
    block = res_x.shape[1]
    send[:, :toks] = (mine[...] + recv[n:, :toks].astype(f32)).astype(bf16)
    send[:, toks : toks + block] = res_x[...]
    send[:, toks + block :] = recv[n:, toks:]


def tokens_outputs(mine, res_mine, from_core, from_x, grad, output):
    me = lax.axis_index("hid")
    n, toks = mine.shape
    block = res_mine.shape[1]
    both = from_core[:n, :toks].astype(f32) + from_x[:, :toks].astype(f32)
    grad[...] = (mine[...] + both).astype(bf16)
    output[:, at(me, block)] = res_mine[...]
    output[:, at(me ^ 1, block)] = from_core[:n, toks:]
    output[:, at(me ^ 2, block)] = from_x[:, toks : toks + block]
    output[:, at(me ^ 3, block)] = from_x[:, toks + block :]


def qkv_input_grad(grads, w_qkv, dres, res_send, mine, mine_x, send, full):
    me = lax.axis_index("hid")
    feats = mine.shape[0]
    block = dres.shape[0]
    total = None
    for c in range(3):
        part = dot(jnp.transpose(w_qkv[c]), grads[c * feats : (c + 1) * feats, :])
        total = part if total is None else total + part
    full[...] = total
    full[:, at(me, block)] += jnp.transpose(dres[...])
    toks = full.shape[1]
    send[:feats, :toks] = full[at(me ^ 1, feats), :].astype(bf16)
    send[feats:, :toks] = full[at(me ^ 3, feats), :].astype(bf16)
    send[:, toks:] = res_send[...]
    mine[...] = full[at(me, feats), :]
    mine_x[...] = full[at(me ^ 2, feats), :]


def place_rows(own, core_rows, xa, xb, fa, fb, whole):
    me, parity = lax.axis_index("hid"), lax.axis_index("rows") & 1
    n = own.shape[0]
    half = n // 2
    whole[at(me, n), :] = own[...]
    whole[at(me ^ 1, n), :] = core_rows[...]
    for owner, first, second in ((me ^ 2, xa, xb), (me ^ 3, fa, fb)):
        whole[at(2 * owner + parity, half), :] = first[...]
        whole[at(2 * owner + (parity ^ 1), half), :] = second[...]


def row_norm(values):
    mean = jnp.mean(values, axis=1, keepdims=True)
    centered = values - mean
    spread = jnp.mean(centered * centered, axis=1, keepdims=True)
    inv = lax.rsqrt(spread + norm_eps)
    return centered * inv, inv


def attn_out(
    g0, g1, g2, g3, x_block, vecs, wo, cotangent,
    normed, send, hat, inv_out, pre, gated_rows, heads_all,
):
    me = lax.axis_index("hid")
    feats = g0.shape[0]
    for k, piece in enumerate((g0, g1.at[:feats, :], g2.at[:feats, :], g3.at[feats : 2 * feats, :])):
        heads_all[at(me ^ k, feats), :] = piece[...]
    gated = jnp.transpose(heads_all[...])
    gated_rows[...] = gated
    tokens = jnp.transpose(x_block[...].astype(f32))
    attn = dot_nt(gated, wo[...]) + vecs[0:1, :]
    pre[...] = attn
    n = normed.shape[0]
    resid = tokens + attn * vecs[8:9, :]
    x_hat, inv = row_norm(resid)
    value = x_hat * vecs[1:2, :] + vecs[2:3, :]
    send[:n, :] = value.astype(bf16)
    rows = feats // 3
    for k in range(3):
        piece = cotangent[k * rows : (k + 1) * rows, at(1 - me // 2, 2 * n)]
        send[n:, k * 2 * n : (k + 1) * 2 * n] = piece
    normed[...] = value
    hat[...] = x_hat
    inv_out[...] = jnp.broadcast_to(inv, inv_out.shape)


def high_low(values):
    high = values.astype(bf16).astype(f32)
    return jnp.concatenate([high, values - high], axis=0).astype(bf16)


def put_sums(sums, ref, start):
    pairs = high_low(sums)
    count = pairs.shape[0]
    for t in range(sums.shape[1] // 128):
        ref[start + t * count : start + (t + 1) * count, :] = pairs[:, t * 128 : (t + 1) * 128]


def get_sums(ref, start, count, blocks):
    parts = []
    for t in range(blocks):
        pair = ref[start + 2 * count * t : start + 2 * count * (t + 1), :].astype(f32)
        parts.append(pair[:count, :] + pair[count:, :])
    return jnp.concatenate(parts, axis=1)


def attn_out_back(
    part, recv, dres2, hat, inv, pre, vecs, wo, sums2,
    dres, grad_attn, sums, up_mine, up_core, up_x, ups,
):
    me = lax.axis_index("hid")
    feats = up_mine.shape[0]
    grad = part[...] + recv[...].astype(f32) + dres2[...]
    x_hat = hat[...]
    scaled = grad * vecs[1:2, :]
    mean_plain = jnp.mean(scaled, axis=1, keepdims=True)
    mean_along = jnp.mean(scaled * x_hat, axis=1, keepdims=True)
    grad_resid = inv[:, 0:1] * (scaled - mean_plain - x_hat * mean_along)
    dres[...] = grad_resid
    low = (grad_resid * vecs[8:9, :]).astype(bf16)
    grad_attn[...] = low
    grad_gated = dot(low, wo[...])
    upstream = (grad_gated * vecs[7:8, :]).astype(bf16)
    ups[...] = jnp.transpose(upstream)
    up_mine[...] = ups[at(me, feats), :]
    up_core[:feats, :] = ups[at(me ^ 1, feats), :]
    up_x[:feats, :] = ups[at(me ^ 2, feats), :]
    up_x[feats : 2 * feats, :] = ups[at(me ^ 3, feats), :]
    sums[0:1, :] = jnp.sum(grad * x_hat, axis=0, keepdims=True)
    sums[1:2, :] = jnp.sum(grad, axis=0, keepdims=True)
    sums[2:3, :] = jnp.sum(low.astype(f32), axis=0, keepdims=True)
    sums[3:4, :] = jnp.sum(grad_resid * pre[...], axis=0, keepdims=True)
    sums[4:8, :] = sums2[...]
    for ref, start in ((up_core, feats), (up_x, 2 * feats)):
        put_sums(sums[...], ref, start)


def out_weight_grad(grad_attn, gated_rows, mine, mine_x, send, full):
    me = lax.axis_index("hid")
    feats = mine.shape[0]
    full[...] = dot_tn(grad_attn[...], gated_rows[...])
    send[:feats, :] = full[at(me ^ 1, feats), :].astype(bf16)
    send[feats:, :] = full[at(me ^ 3, feats), :].astype(bf16)
    mine[...] = full[at(me, feats), :]
    mine_x[...] = full[at(me ^ 2, feats), :]


def place_units(wi_own, wi_core, own, core_rows, xa, xb, fa, fb, wi, wb):
    me, core, chip, parity = lax.axis_index("hid"), lax.axis_index("hid") & 1, lax.axis_index("hid") // 2, lax.axis_index("rows") & 1
    n, half = xa.shape
    units = wi_own.shape[1]
    wi[:, at(core, units)] = wi_own[...]
    wi[:, at(core ^ 1, units)] = wi_core[...]
    wb[at(me, n), :] = own[:, at(chip, 2 * half)]
    wb[at(me ^ 1, n), :] = core_rows[:, at(chip, 2 * half)]
    for owner, first, second in ((me ^ 2, xa, xb), (me ^ 3, fa, fb)):
        wb[at(owner, n), at(parity, half)] = first[...]
        wb[at(owner, n), at(parity ^ 1, half)] = second[...]


def ffn_forward(
    rows, unit_rows, wi, wb, core_far, act, slope, inter_mine, part, core_pair, inter
):
    n = part.shape[0]
    core_pair[n:, :] = core_far[...]
    ffn_units(rows[: part.shape[0], :], unit_rows, wi, act, slope, inter_mine, core_pair.at[:n, :], inter)
    part[...] = dot_nt(inter[...], wb[...])


def ffn_forward_far(
    rows, unit_rows, wi, wb, act, slope, inter_mine, inter_core, part, inter
):
    ffn_units(rows[: part.shape[0], :], unit_rows, wi, act, slope, inter_mine, inter_core, inter)
    part[...] = dot_nt(inter[...], wb[...]).astype(part.dtype)


def ffn_units(rows, unit_rows, wi, act, slope, inter_mine, inter_core, inter):
    core = lax.axis_index("hid") & 1
    units = wi.shape[1]
    step = 256
    for j in range(units // step):
        cut = slice(j * step, (j + 1) * step)
        u = dot(rows, wi[:, cut]) + unit_rows[0:1, cut]
        cdf = 0.5 * (1.0 + lax.erf(u * 0.7071067811865476))
        value = u * cdf
        act[:, cut] = value
        slope[:, cut] = cdf + u * (jnp.exp(-0.5 * u * u) * 0.3989422804014327)
        inter[:, cut] = (value * unit_rows[1:2, cut]).astype(bf16)
    inter_mine[...] = inter[:, at(core, units // 2)]
    inter_core[...] = inter[:, at(core ^ 1, units // 2)]


def ffn_backward(
    rows, act, slope, unit_rows, wi, wb, gpre_mine, gpre_core, part, sums, gpre,
):
    ffn_units_back(rows, act, slope, unit_rows, wb, gpre_mine, gpre_core, sums, gpre)
    part[...] = dot_nt(gpre[...], wi[...])


def ffn_backward_far(
    rows, act, slope, unit_rows, wi, wb, core_mine, sums_mine,
    gpre_mine, part, sums, core_pair, gpre, all_sums,
):
    core, n = lax.axis_index("hid") & 1, rows.shape[0]
    units = gpre_mine.shape[1]
    core_pair[:n, :] = core_mine[...]
    ffn_units_back(
        rows, act, slope, unit_rows, wb, gpre_mine, core_pair.at[n : 2 * n, :], all_sums, gpre
    )
    part[...] = dot_nt(gpre[...], wi[...]).astype(part.dtype)
    all_sums[...] += sums_mine[...]
    sums[...] = all_sums[:, at(core, units)]
    core_pair[2 * n :, :] = high_low(all_sums[:, at(core ^ 1, units)])


def ffn_units_back(rows, act, slope, unit_rows, wb, gpre_mine, gpre_core, sums, gpre):
    core = lax.axis_index("hid") & 1
    units = wb.shape[1]
    step = 256
    for j in range(units // step):
        cut = slice(j * step, (j + 1) * step)
        ginter = dot(rows[...], wb[:, cut])
        sums[:, cut] = jnp.broadcast_to(
            jnp.sum(ginter * act[:, cut], axis=0, keepdims=True), (8, step)
        )
        gpre[:, cut] = (ginter * unit_rows[1:2, cut] * slope[:, cut]).astype(bf16)
    gpre_mine[...] = gpre[:, at(core, units // 2)]
    gpre_core[...] = gpre[:, at(core ^ 1, units // 2)]


def ffn_weight_grads(
    n0, n1, n2, n3, e0, e1, e_core, p0, p1, p_core, f0, f1, f2, f3,
    back0_keep, back0_send, back1_keep, back1_send, in0_keep, in0_send, in1_keep, in1_send,
    bias_sums, left, right, full,
):
    parity = lax.axis_index("rows") & 1

    def fill(target, pieces):
        start = 0
        for piece in pieces:
            count = piece.shape[0] // 128 * 128
            target[start : start + count, :] = piece[:count, :]
            start += count

    fill(left, (f0, f1, f2, f3))
    fill(right, (e0, e1, e_core))
    full[...] = dot_tn(left[...], right[...])
    owners, parts = 4, 4
    rows = full.shape[0] // (owners * parts)
    for k, (keep, send) in enumerate(((back0_keep, back0_send), (back1_keep, back1_send))):
        for h in range(owners):
            to = slice(h * rows, (h + 1) * rows)
            send[to, :] = full[at(h * parts + 2 * k + (parity ^ 1), rows), :].astype(bf16)
            keep[to, :] = full[at(h * parts + 2 * k + parity, rows), :]
    fill(left, (n0, n1, n2, n3))
    fill(right, (p0, p1, p_core))
    full[...] = dot_tn(left[...], right[...])
    rows = full.shape[0] // 4
    for k, (keep, send) in enumerate(((in0_keep, in0_send), (in1_keep, in1_send))):
        send[...] = full[at(2 * k + (parity ^ 1), rows), :].astype(bf16)
        keep[...] = full[at(2 * k + parity, rows), :]
    bias_sums[...] = jnp.broadcast_to(
        jnp.sum(right[...].astype(f32), axis=0, keepdims=True), bias_sums.shape
    )


def second_norm(
    part, recv, normed, cot0, cot1, n_x, n_far, vecs,
    grad_low, dres, sums, out_mine, out_x, out_send, cots, outs,
):
    me = lax.axis_index("hid")
    feats = cot0.shape[0]
    block = part.shape[0]
    core = me & 1
    cots[at(me, feats), :] = cot0[:, at(me, block)]
    cots[at(me ^ 1, feats), :] = cot1[:, at(me, block)]
    rows = feats // 3
    for owner, pieces in ((me ^ 2, n_x), (me ^ 3, n_far)):
        for k in range(3):
            to = pl.ds(pl.multiple_of(owner * feats + k * rows, rows), rows)
            cots[to, :] = pieces[block:, at(2 * k + core, block)]
    ffn = part[...] + recv[...].astype(f32) + vecs[4:5, :]
    resid = normed[...] + ffn * vecs[9:10, :]
    x_hat, inv = row_norm(resid)
    grad_out = jnp.transpose(cots[...].astype(f32))
    scaled = grad_out * vecs[5:6, :]
    mean_plain = jnp.mean(scaled, axis=1, keepdims=True)
    mean_along = jnp.mean(scaled * x_hat, axis=1, keepdims=True)
    grad_resid = inv * (scaled - mean_plain - x_hat * mean_along)
    low = (grad_resid * vecs[9:10, :]).astype(bf16)
    grad_low[...] = low
    dres[...] = grad_resid
    value = x_hat * vecs[5:6, :] + vecs[6:7, :]
    outs[...] = jnp.transpose(value).astype(bf16)
    out_mine[...] = outs[at(me, feats), :]
    out_x[...] = outs[at(me ^ 2, feats), :]
    out_send[:feats, :] = outs[at(me ^ 1, feats), :]
    out_send[feats:, :] = outs[at(me ^ 3, feats), :]
    sums[0:1, :] = jnp.sum(grad_out * x_hat, axis=0, keepdims=True)
    sums[1:2, :] = jnp.sum(grad_out, axis=0, keepdims=True)
    sums[2:3, :] = jnp.sum(low.astype(f32), axis=0, keepdims=True)
    sums[3:4, :] = jnp.sum(grad_resid * ffn, axis=0, keepdims=True)


VECTORS = 16


def add_vectors(
    head_gate, branch, b_out, gain, bias, hidden_gate, hidden_mask, b_back, ctx_core, ctx_x,
    send_core, send_x, columns, rows,
):
    feats = b_out.shape[0]

    def row(ref):
        return ref[...].reshape(1, ref.shape[0])

    cols = row(hidden_gate) * row(hidden_mask).astype(f32)
    rows[...] = jnp.zeros_like(rows)
    rows[0:1, :feats] = row(b_out)
    rows[1:2, :feats] = gain[0:1, :]
    rows[2:3, :feats] = bias[0:1, :]
    rows[3:4, :feats] = cols
    rows[4:5, :feats] = row(b_back)
    rows[5:6, :feats] = gain[1:2, :]
    rows[6:7, :feats] = bias[1:2, :]
    rows[7:8, :feats] = jnp.concatenate(
        [jnp.full((1, HEAD_DIM), head_gate[i], f32) for i in range(feats // HEAD_DIM)], axis=1
    )
    rows[8:9, :feats] = branch[0] * cols
    rows[9:10, :feats] = branch[1] * cols
    rest = jnp.transpose(rows[...])[:feats, :]
    columns[...] = jnp.zeros_like(columns)
    for k in range(3):
        low = rest.astype(bf16)
        columns[:, k * VECTORS : (k + 1) * VECTORS] = low
        rest = rest - low.astype(f32)
    for send, ctx in ((send_core, ctx_core), (send_x, ctx_x)):
        n = ctx.shape[0]
        send[:n, :] = ctx[...]
        send[n:, :] = columns[...]


def place_vectors(p0, p1, p2, p3, b_in, gate, b_in_core, gate_core, vecs, unit_rows, cols):
    me, core = lax.axis_index("hid"), lax.axis_index("hid") & 1
    feats = cols.shape[0] // 4
    units = b_in.shape[0]
    for k, piece in enumerate((p0, p1.at[feats:, :], p2.at[2 * feats :, :], p3.at[2 * feats :, :])):
        parts = piece[...].astype(f32)
        cols[at(me ^ k, feats), :] = (
            parts[:, :VECTORS] + parts[:, VECTORS : 2 * VECTORS]
        ) + parts[:, 2 * VECTORS : 3 * VECTORS]
    vecs[...] = jnp.transpose(cols[...])
    for k, (one, two) in enumerate(((b_in, gate), (b_in_core, gate_core))):
        unit_rows[0:1, at(core ^ k, units)] = one[...].reshape(1, units)
        unit_rows[1:2, at(core ^ k, units)] = two[...].reshape(1, units)


def vector_outputs(
    branch, head_gate, vec, vecs, hidden_mask,
    g_qv, g_bout, g_bin, g_bback, g_gain, g_bias, g_head, g_inter, g_branch, g_hidden, cols,
):
    me = lax.axis_index("hid")
    feats = g_bout.shape[0]
    cols[...] = jnp.transpose(vec[0:8, :])
    own = jnp.transpose(cols[at(me, feats), :])
    g_gain[0:1, :] = own[0:1, :]
    g_gain[1:2, :] = own[4:5, :]
    g_bias[0:1, :] = own[1:2, :]
    g_bias[1:2, :] = own[5:6, :]
    g_bout[...] = own[2, :]
    g_bback[...] = own[6, :]
    mask = hidden_mask[...].astype(f32)
    g_hidden[...] = (branch[0] * own[3, :] + branch[1] * own[7, :]) * mask
    g_inter[...] = vec[8, :]
    g_bin[...] = vec[9, :]
    g_qv[0:1, :] = vec[10:11, :feats]
    rolled = vec[10:11, 2 * feats : 3 * feats]
    g_qv[1:2, :] = rolled
    lane = lax.broadcasted_iota(jnp.int32, (1, 128), 1)
    gates = jnp.ones((1, 128), f32)
    for i in range(feats // HEAD_DIM):
        gates = jnp.where(lane == i, head_gate[i], gates)
    g_head[...] = (vec[11:12, :128] / gates)[0, : feats // HEAD_DIM]
    part0 = jnp.sum(vec[3:4, :] * vecs[3:4, :], axis=1, keepdims=True)
    part1 = jnp.sum(vec[7:8, :] * vecs[3:4, :], axis=1, keepdims=True)
    both = jnp.where(lane == 0, part0, part1)
    g_branch[...] = both[0, :2]


def row_place():
    row = lax.axis_index("rows")
    return row & 1, (row >> 1) & 3


def first_add(keep, recv, total, send):
    total[...] = keep[...] + recv[...].astype(f32)
    send[...] = total[...].astype(bf16)


def first_add_pair(keep, pair, recv, total, send):
    n = keep.shape[0]
    total[...] = keep[...] + recv[:n, :].astype(f32)
    send[:n, :] = total[...].astype(bf16)
    send[n:, :] = high_low(pair_value(pair) + pair_value(recv[n:, :]))


def second_add(keep, recv, send):
    send[...] = (keep[...] + recv[...].astype(f32)).astype(bf16)


def second_add_pair(keep, mine, recv, send):
    n = keep.shape[0]
    send[:n, :] = (keep[...] + recv[:n, :].astype(f32)).astype(bf16)
    send[n:, :] = high_low(pair_value(mine[n:, :]) + pair_value(recv[n:, :]))


def third_add(mine, recv, total):
    total[...] = (mine[...].astype(f32) + recv[...].astype(f32)).astype(bf16)


def third_add_pair(mine, recv, total):
    n = mine.shape[0] - 32
    total[:n, :] = (mine[:n, :].astype(f32) + recv[:n, :].astype(f32)).astype(bf16)
    total[n:, :] = high_low(pair_value(mine[n:, :]) + pair_value(recv[n:, :]))


def choose(mine, recv, total):
    z = row_place()[1]
    outer = (z == 0) | (z == 3)
    total[...] = jnp.where(outer, recv[...], mine[...])


def choose_pair(mine, recv, total, vec):
    n = total.shape[0]
    z = row_place()[1]
    outer = (z == 0) | (z == 3)
    total[...] = jnp.where(outer, recv[:n, :], mine[:n, :])
    vec[...] = jnp.where(outer, pair_value(recv[n:, :]), pair_value(mine[n:, :]))


def split_owners(mine, recv, own, own_x, send):
    me = lax.axis_index("hid")
    n = own.shape[0]

    def rows(k):
        total = mine[at(me ^ k, n), :].astype(f32) + recv[at(me ^ k, n), :].astype(f32)
        return total.astype(bf16)

    own[...] = rows(0)
    own_x[...] = rows(2)
    send[:n, :] = rows(1)
    send[n:, :] = rows(3)


def join_owners(mine, from_core, from_x, chunk):
    me, n = lax.axis_index("hid"), mine.shape[0]
    chunk[at(me, n), :] = mine[...]
    chunk[at(me ^ 1, n), :] = from_core[:n, :]
    chunk[at(me ^ 2, n), :] = from_x[:n, :]
    chunk[at(me ^ 3, n), :] = from_x[n:, :]


def in_gradient(mine0, other0, mine1, other1, grad):
    y = row_place()[0]
    n = mine0.shape[0]
    for k, (mine, other) in enumerate(((mine0, other0), (mine1, other1))):
        grad[at(2 * k + y, n), :] = mine[...].astype(f32)
        grad[at(2 * k + (y ^ 1), n), :] = other[...].astype(f32)


def back_gradient(mine0, other0, mine1, other1, grad):
    y = row_place()[0]
    units = mine0.shape[1]
    n = mine0.shape[0] // 4
    for k, (mine, other) in enumerate(((mine0, other0), (mine1, other1))):
        for side, half in ((y, mine), (y ^ 1, other)):
            for owner in range(4):
                block = half[owner * n : (owner + 1) * n, :].astype(f32)
                grad[at(2 * k + side, n), owner * units : (owner + 1) * units] = block


def attn_gradients(qk_mine, qk_other, vo_mine, vo_other, grad_qkv, grad_out):
    y = row_place()[0]
    n = qk_mine.shape[0]
    grad_qkv[at(y, n), :] = qk_mine[...].astype(f32)
    grad_qkv[at(y ^ 1, n), :] = qk_other[...].astype(f32)
    mine, other = vo_mine[...].astype(f32), vo_other[...].astype(f32)
    grad_qkv[2 * n :, :] = jnp.where(y == 0, mine, other)
    grad_out[...] = jnp.where(y == 0, other, mine)


def second_half(mine, recv, both):
    n = mine.shape[0]
    both[:n, :] = mine[...]
    both[n:, :] = recv[n:, :]


EARLY_TURNS = "313"
TURNS = "413vq2413241v3241q122vg13q24v12q4vg2qegvq"
FIRST = ("in0", "back0")


def along(block, way="y"):
    pairs = []
    for i in range(lax.axis_size("rows")):
        z = (i >> 1) & 3
        step = {
            "y": 1 - 2 * (i & 1),
            "in": {0: 2, 3: -2}.get(z),
            "mid": {1: 2, 2: -2}.get(z),
            "out": {1: -2, 2: 2}.get(z),
        }[way]
        if step is not None:
            pairs.append((i, i + step))
    return lax.ppermute(block, "rows", pairs)


class Turns:
    def __init__(self):
        self.last = ()

    def held(self, block):
        return after(block, *self.last) if self.last else block

    def mark(self, *blocks):
        self.last = blocks


def far_rows_sum(chunk):
    count = lax.axis_size("rows")
    if count == 8:
        return chunk
    groups = [[i + 8 * j for j in range(count // 8)] for i in range(8)]
    return lax.psum(chunk.astype(f32), "rows", axis_index_groups=groups).astype(chunk.dtype)


def shards(
    tokens, w_qkv, b_qv, w_out, b_out, w_in, b_in, w_back, b_back, norm_gain, norm_bias,
    head_gate, inter_gate, branch_gate, hidden_gate, hidden_mask, doc_lengths, cotangent,
):
    feats, toks = tokens.shape
    width = 4 * feats
    units = w_in.shape[1]
    block = toks // 4
    given = jnp.concatenate(
        [
            b_qv,
            jnp.pad(head_gate, (0, feats - head_gate.shape[0]))[None],
            jnp.pad(doc_lengths.astype(f32), ((0, 0), (0, feats - doc_lengths.shape[1]))),
        ],
        0,
    )
    bounds, small, out_half, back_half = local_kernel(
        begin,
        "begin",
        (given, w_out, w_back),
        "VVV",
        [
            sds((8, toks), jnp.int32),
            sds((8, 256), f32),
            sds((feats // 2, width), bf16),
            sds((feats, units), bf16),
        ],
    )
    tokens_x = swap(tokens, "hid", 2)
    tokens_core = swap(tokens, "hid", 1)
    x_own = swap(after(tokens_core, back_half), "hid", 1)
    out_xa = swap(out_half, "hid", 2)
    back_xa = swap(back_half, "hid", 2)
    wi_core = swap(w_in, "hid", 1)
    wo_core = swap(w_out, "hid", 1)
    b_in_core = swap(b_in, "hid", 1)
    gate_core = swap(inter_gate, "hid", 1)
    back_core = swap(w_back, "hid", 1)
    tokens_far = swap(
        after(tokens_x, tokens_core, wi_core, wo_core, back_core, back_half), "hid", 1
    )

    head_block = sds((feats, block), bf16)
    two_blocks = sds((2 * feats, block), bf16)
    x_all, qkv, logsum, g0, g_core, g_x, x_block = local_kernel(
        attn_forward,
        "attn_forward",
        (
            bounds, small, x_own, tokens_core, tokens_x, tokens_far, w_qkv,
        ),
        "V" * 7,
        [
            sds((width, toks), bf16),
            sds((3, feats, toks), bf16),
            sds((8, toks), f32),
            head_block,
            head_block,
            two_blocks,
            sds((width, block), bf16),
        ],
        [pltpu.VMEM((feats, toks), bf16), pltpu.VMEM((toks, toks), f32)],
        micros=5.4,
    )
    cot_core = swap(after(cotangent, x_block), "hid", 1)
    send_core, send_x, columns = local_kernel(
        add_vectors,
        "add_vectors",
        (
            head_gate, branch_gate, after(b_out, x_block), norm_gain, norm_bias, hidden_gate,
            hidden_mask, b_back, g_core, g_x,
        ),
        "SS" + "V" * 8,
        [two_blocks, sds((3 * feats, block), bf16), head_block],
        [pltpu.VMEM((VECTORS, 256), f32)],
    )
    g2 = swap(send_x, "hid", 2)
    g1 = swap(send_core, "hid", 1)
    g3 = swap(after(g2, g1, b_in_core, gate_core), "hid", 1)
    out_xb = swap(after(out_xa, g0), "rows", 1)
    out_fa = swap(after(out_xa, g0), "hid", 1)
    out_fb = swap(out_xb, "hid", 1)
    back_xb = swap(after(back_xa, g1), "rows", 1)
    back_fa = swap(after(back_xa, g1), "hid", 1)
    (wo,) = local_kernel(
        place_rows,
        "place_rows",
        (w_out, wo_core, out_xa, out_xb, out_fa, out_fb),
        "VVVVVV",
        [sds((width, width), bf16)],
    )
    vecs, unit_rows = local_kernel(
        place_vectors,
        "place_vectors",
        (columns, g1, g2, g3, b_in, inter_gate, b_in_core, gate_core),
        "V" * 8,
        [sds((VECTORS, width), f32), sds((2, 2 * units), f32)],
        [pltpu.VMEM((width, VECTORS), f32)],
    )

    normed, n_send, hat, inv, attn_pre, gated_rows = local_kernel(
        attn_out,
        "attn_out",
        (g0, g1, g2, g3, x_block, vecs, wo, cotangent),
        "VVVVVVVV",
        [
            sds((block, width), f32),
            sds((block + feats // 3, width), bf16),
            sds((block, width), f32),
            sds((block, 128), f32),
            sds((block, width), f32),
            sds((block, width), bf16),
        ],
        [pltpu.VMEM((width, block), bf16)],
        micros=1.3,
    )

    n_x = swap(n_send, "hid", 2)
    n_core = swap(n_send, "hid", 1)
    back_fb = swap(after(back_xb, n_x), "hid", 1)
    wi, wb = local_kernel(
        place_units,
        "place_units",
        (w_in, wi_core, w_back, back_core, back_xa, back_xb, back_fa, back_fb),
        "V" * 8,
        [sds((width, 2 * units), bf16), sds((width, 2 * units), bf16)],
        micros=0.85,
    )

    act_block = sds((block, 2 * units), f32)
    half_block = sds((block, units), bf16)
    pair_block = sds((2 * block, units), bf16)
    rows_block = sds((block, width), bf16)
    ffn_scratch = [pltpu.VMEM((block, 2 * units), bf16)]
    act_x, slope_x, e1, inter_core, ffn_send = local_kernel(
        ffn_forward_far,
        "ffn_forward_far",
        (n_x, unit_rows, wi, wb),
        "VVVV",
        [act_block, act_block, half_block, half_block, rows_block],
        ffn_scratch,
        micros=1.85,
    )
    ffn_recv = swap(ffn_send, "hid", 2)
    act, slope, e0, ffn_part, e_pair = local_kernel(
        ffn_forward,
        "ffn_forward",
        (after(n_send, ffn_send), unit_rows, wi, wb, inter_core),
        "VVVVV",
        [act_block, act_block, half_block, sds((block, width), f32), pair_block],
        ffn_scratch,
        micros=1.85,
    )
    n_far = swap(after(n_x, ffn_send), "hid", 1)

    out_block = sds((feats, block), bf16)
    gffn, dres2, sums2, res_mine, res_x, res_send = local_kernel(
        second_norm,
        "second_norm",
        (
            after(ffn_part, n_core), ffn_recv, normed, cotangent, cot_core, n_x, n_far, vecs,
        ),
        "V" * 8,
        [
            sds((block, width), bf16),
            sds((block, width), f32),
            sds((4, width), f32),
            out_block,
            out_block,
            sds((2 * feats, block), bf16),
        ],
        [pltpu.VMEM((width, block), bf16), pltpu.VMEM((width, block), bf16)],
        micros=1.2,
    )

    gffn_x = swap(gffn, "hid", 2)
    e_core = swap(after(e_pair, gffn), "hid", 1)
    f2 = swap(gffn, "hid", 1)
    sums_block = sds((8, 2 * units), f32)
    p0, gpre_core, gn_part, ig_sum = local_kernel(
        ffn_backward,
        "ffn_backward",
        (gffn, act, slope, unit_rows, wi, wb),
        "VVVVVV",
        [half_block, half_block, sds((block, width), f32), sums_block],
        ffn_scratch,
        micros=1.85,
    )
    p1, gn_send, ig_mine, p_pair = local_kernel(
        ffn_backward_far,
        "ffn_backward_far",
        (after(gffn_x, f2, e_core), act_x, slope_x, unit_rows, wi, wb, gpre_core, ig_sum),
        "VVVVVVVV",
        [half_block, rows_block, sds((8, units), f32), sds((2 * block + 16, units), bf16)],
        ffn_scratch + [pltpu.VMEM((8, 2 * units), f32)],
        micros=1.85,
    )
    gn_recv = swap(gn_send, "hid", 2)
    f3 = swap(after(gffn_x, gn_send), "hid", 1)
    p_core = swap(p_pair, "hid", 1)
    *pieces, bin_sum = local_kernel(
        ffn_weight_grads,
        "ffn_weight_grads",
        (
            n_send, n_x, n_core, n_far, e0, e1, e_core,
            p0, p1, p_core, gffn, gffn_x, f2, f3,
        ),
        "V" * 14,
        [
            sds((feats, units), f32),
            sds((feats, units), bf16),
            sds((feats, units), f32),
            sds((feats, units), bf16),
            sds((feats, units), f32),
            sds((feats, units), bf16),
            sds((feats, units), f32),
            sds((feats, units), bf16),
            sds((8, units), f32),
        ],
        [
            pltpu.VMEM((toks, width), bf16),
            pltpu.VMEM((toks, units), bf16),
            pltpu.VMEM((width, units), f32),
        ],
        micros=2.5,
    )

    pieces = dict(zip(("back0", "back1", "in0", "in1"), zip(pieces[0::2], pieces[1::2])))
    early = {name: along(after(pieces[name][1], gn_recv)) for name in FIRST}

    sum_rows = 16 * width // 128
    dres1, gattn, sums1, u0, up_core, up_x = local_kernel(
        attn_out_back,
        "attn_out_back",
        (
            after(gn_part, pieces["in1"][1]), gn_recv, dres2, hat, inv, attn_pre,
            vecs, wo, sums2,
        ),
        "V" * 9,
        [
            sds((block, width), f32),
            sds((block, width), bf16),
            sds((8, width), f32),
            head_block,
            sds((feats + sum_rows, block), bf16),
            sds((2 * feats + sum_rows, block), bf16),
        ],
        [pltpu.VMEM((width, block), bf16)],
        micros=1.3,
    )
    u2 = swap(up_x, "hid", 2)
    u1 = swap(up_core, "hid", 1)
    u3 = swap(u2, "hid", 1)

    weight_block = sds((feats, width), f32)
    low_block = sds((feats, width), bf16)
    wo_mine, wo_keep, wo_send = local_kernel(
        out_weight_grad,
        "out_weight_grad",
        (gattn, gated_rows),
        "VV",
        [weight_block, weight_block, sds((2 * feats, width), bf16)],
        [pltpu.VMEM((width, width), f32)],
        micros=1.2,
    )
    wo_grad_core = swap(after(wo_send, u1), "hid", 1)

    turns = Turns()
    results = {}
    whole_block = sds((feats, width), f32)

    def step(body, args, outs, **more):
        outs = local_kernel(
            body, body.__name__, (turns.held(args[0]),) + args[1:], "V" * len(args), outs, **more
        )
        turns.mark(*outs[-1:])
        return outs

    def sum_chain(name, keep, send, recv=None):
        if recv is None:
            recv = along(turns.held(send))
        yield
        keep, send = step(first_add, (keep, recv), [whole_block, low_block])
        recv = along(send, "in")
        yield
        (mine,) = step(second_add, (keep, recv), [low_block])
        recv = along(mine, "mid")
        yield
        if name.startswith("back"):
            part = sds((feats // 4, units), bf16)
            two = sds((feats // 2, units), bf16)
            mine, mine_x, send = step(split_owners, (mine, recv), [part, part, two])
            from_core = swap(send, "hid", 1)
            yield
            (send,) = step(second_half, (mine_x, from_core), [two])
            from_x = swap(send, "hid", 2)
            yield
            (mine,) = step(join_owners, (mine, from_core, from_x), [low_block])
        else:
            (mine,) = step(third_add, (mine, recv), [low_block])
        recv = along(mine, "out")
        yield
        (mine,) = step(choose, (mine, recv), [low_block])
        yield from last_part(name, mine)

    def last_part(name, mine):
        mine = far_rows_sum(mine)
        other = along(mine)
        yield
        results[name] = (mine, other)
        if name in ("in0", "in1") and "in0" in results and "in1" in results:
            (results["w_in"],) = step(
                in_gradient,
                results["in0"] + results["in1"],
                [sds((width, units), f32)],
                micros=2.1,
            )
        if name in ("back0", "back1") and "back0" in results and "back1" in results:
            (results["w_back"],) = step(
                back_gradient,
                results["back0"] + results["back1"],
                [sds((feats, 4 * units), f32)],
                micros=2.1,
            )
        if name in ("qk", "vo") and "qk" in results and "vo" in results:
            results["w_qkv"], results["w_out"] = step(
                attn_gradients,
                results["qk"] + results["vo"],
                [sds((3 * feats, width), f32), weight_block],
                micros=2.1,
            )

    chains = {
        key: sum_chain(name, *pieces[name], early.get(name))
        for key, name in zip("1234", ("back0", "back1", "in0", "in1"))
    }
    turns.mark(u1)
    for turn in EARLY_TURNS:
        next(chains[turn], None)
    grads, head_sums, bias_sums = local_kernel(
        attn_backward,
        "attn_backward",
        (bounds, turns.held(qkv), logsum, u0, u1, u2, u3),
        "V" * 7,
        [
            sds((3 * feats, toks), bf16),
            sds((8, block), f32),
            sds((8, 3 * feats), f32),
        ],
        [pltpu.VMEM((feats, toks), bf16), pltpu.VMEM((toks, toks), f32)],
        micros=5.0,
    )
    (wo_low,) = local_kernel(add_second, "wo_low", (wo_keep, wo_grad_core), "VV", [low_block])
    wo_far = swap(after(wo_low, u3), "hid", 2)

    gx_block = sds((feats, toks), f32)
    gx_low = sds((feats, toks), bf16)

    def qk_chain():
        with_pair = sds((feats + 32, width), bf16)
        keep, send, pair = local_kernel(
            qk_weight_grad,
            "qk_weight_grad",
            (
                turns.held(grads), x_all, sums1, u1, u2, u3, ig_mine, p_core, bin_sum,
                head_sums, bias_sums,
            ),
            "V" * 11,
            [weight_block, with_pair, sds((32, width), bf16)],
            [pltpu.VMEM((2 * feats, width), f32), pltpu.VMEM((16, width), f32)],
            micros=1.2,
        )
        turns.mark(send)
        recv = along(send)
        yield
        keep, send = step(first_add_pair, (keep, pair, recv), [weight_block, with_pair])
        recv = along(send, "in")
        yield
        (mine,) = step(second_add_pair, (keep, send, recv), [with_pair])
        recv = along(mine, "mid")
        yield
        (mine,) = step(third_add_pair, (mine, recv), [with_pair])
        recv = along(mine, "out")
        yield
        mine, results["sums"] = step(
            choose_pair, (mine, recv), [low_block, sds((16, width), f32)]
        )
        yield from last_part("qk", mine)

    def vo_chain():
        keep, send = local_kernel(
            vo_weight_grad,
            "vo_weight_grad",
            (turns.held(grads), x_all, wo_mine, wo_grad_core, wo_far),
            "VVVVV",
            [weight_block, low_block],
            [pltpu.VMEM((2 * feats, width), f32)],
            micros=1.1,
        )
        turns.mark(send)
        yield from sum_chain("vo", keep, send, along(send))

    def tokens_chain():
        mine, mine_x, send = local_kernel(
            qkv_input_grad,
            "qkv_input_grad",
            (turns.held(grads), w_qkv, dres1, res_send),
            "VVVV",
            [gx_block, gx_block, sds((2 * feats, toks + block), bf16)],
            [pltpu.VMEM((width, toks), f32)],
            micros=1.5,
        )
        turns.mark(send)
        from_core = swap(send, "hid", 1)
        yield
        (send,) = local_kernel(
            tokens_step,
            "tokens_step",
            (turns.held(mine_x), res_x, from_core),
            "VVV",
            [sds((feats, toks + 2 * block), bf16)],
        )
        turns.mark(send)
        from_x = swap(send, "hid", 2)
        yield
        results["tokens"], results["output"] = local_kernel(
            tokens_outputs,
            "tokens_outputs",
            (turns.held(mine), res_mine, from_core, from_x),
            "VVVV",
            [gx_low, gx_low],
            micros=1.2,
        )
        turns.mark(results["tokens"])

    def vector_chain():
        results["vectors"] = local_kernel(
            vector_outputs,
            "vector_outputs",
            (branch_gate, head_gate, far_rows_sum(turns.held(results["sums"])), vecs, hidden_mask),
            "SSVVV",
            [
                sds((2, feats), f32),
                sds((feats,), f32),
                sds((units,), f32),
                sds((feats,), f32),
                sds((2, feats), f32),
                sds((2, feats), f32),
                sds((feats // HEAD_DIM,), f32),
                sds((units,), f32),
                sds((2,), f32),
                sds((feats,), f32),
            ],
            [pltpu.VMEM((width, 8), f32)],
            micros=1.4,
        )
        turns.mark(results["vectors"][0])
        yield

    chains.update(q=qk_chain(), v=vo_chain(), g=tokens_chain(), e=vector_chain())
    turns.mark(grads)
    for turn in TURNS:
        next(chains[turn], None)
    (
        grad_b_qv, grad_b_out, grad_b_in, grad_b_back, grad_norm_gain, grad_norm_bias,
        grad_head_gate, grad_inter_gate, grad_branch_gate, grad_hidden_gate,
    ) = results["vectors"]
    output, grad_tokens = results["output"], results["tokens"]
    grad_w_qkv = results["w_qkv"].reshape(3, feats, width)
    grad_w_out, grad_w_in, grad_w_back = results["w_out"], results["w_in"], results["w_back"]
    return (
        output,
        grad_tokens,
        grad_w_qkv,
        grad_b_qv,
        grad_w_out,
        grad_b_out,
        grad_w_in,
        grad_b_in,
        grad_w_back,
        grad_b_back,
        grad_norm_gain,
        grad_norm_bias,
        grad_head_gate,
        grad_inter_gate,
        grad_branch_gate,
        grad_hidden_gate,
    )


def solution(mesh):
    return jax.shard_map(
        shards,
        mesh=mesh,
        in_specs=(
            P("hid", "rows"),
            P(None, "hid", None),
            P(None, "hid"),
            P("hid", None),
            P("hid"),
            P(None, "hid"),
            P("hid"),
            P("hid", None),
            P("hid"),
            P(None, "hid"),
            P(None, "hid"),
            P("hid"),
            P("hid"),
            P(),
            P("hid"),
            P("hid"),
            P("rows", None),
            P("hid", "rows"),
        ),
        out_specs=(
            P("hid", "rows"),
            P("hid", "rows"),
            P(None, "hid", None),
            P(None, "hid"),
            P("hid", None),
            P("hid"),
            P(None, "hid"),
            P("hid"),
            P("hid", None),
            P("hid"),
            P(None, "hid"),
            P(None, "hid"),
            P("hid"),
            P("hid"),
            P(),
            P("hid"),
        ),
        check_vma=False,
    )
```

```python
import jax
import jax.numpy as jnp
from jax import lax
from jax.experimental import pallas as pl
from jax.experimental.pallas import tpu as pltpu
from jax.sharding import PartitionSpec as P

HEAD_DIM = 64
norm_eps = 1e-06
masked_score = -1e30
bf16 = jnp.bfloat16
f32 = jnp.float32
MIB = 1 << 20
WIDE = 512
HBM_BYTES_PER_MICRO = 3690000

SPECS = {
    "S": pl.BlockSpec(memory_space=pltpu.SMEM),
    "V": pl.BlockSpec(memory_space=pltpu.VMEM),
}


def swap(block, axis, bit):
    return lax.ppermute(block, axis, [(i, i ^ bit) for i in range(lax.axis_size(axis))])


def after(block, *others):
    return lax.optimization_barrier((block, *others))[0]


def sds(shape, dtype):
    return jax.ShapeDtypeStruct(shape, dtype)


def local_kernel(body, name, args, kinds, outs, scratch=(), micros=0.6, vmem=16):
    return pl.pallas_call(
        body,
        name=name,
        out_shape=outs,
        in_specs=[SPECS[k] for k in kinds],
        out_specs=[SPECS["V"]] * len(outs),
        scratch_shapes=list(scratch),
        compiler_params=pltpu.CompilerParams(vmem_limit_bytes=vmem * MIB),
        cost_estimate=pl.CostEstimate(
            flops=1, bytes_accessed=int(micros * HBM_BYTES_PER_MICRO), transcendentals=0
        ),
    )(*args)


def dot(left, right):
    return jnp.dot(left, right, preferred_element_type=f32)


def dot_nt(left, right):
    return lax.dot_general(left, right, (((1,), (1,)), ((), ())), preferred_element_type=f32)


def dot_tn(left, right):
    return lax.dot_general(left, right, (((0,), (0,)), ((), ())), preferred_element_type=f32)


def at(index, size):
    return pl.ds(pl.multiple_of(index * size, size), size)


def begin(given, w_out, w_back, bounds, small, out_half, back_half):
    toks = bounds.shape[1]
    query = lax.broadcasted_iota(jnp.int32, (1, toks), 1).astype(f32)
    start, stop = jnp.zeros_like(query), jnp.zeros_like(query)
    end = jnp.zeros((1, 1), f32)
    for j in range(4):
        first, end = end, end + given[3:4, j : j + 1]
        inside = (query >= first) & (query < end)
        start = jnp.where(inside, first, start)
        stop = jnp.where(inside, end, stop)
    bounds[0:1, :] = start.astype(jnp.int32)
    bounds[1:2, :] = stop.astype(jnp.int32)
    feats = given.shape[1]
    small[...] = jnp.zeros_like(small)
    small[0:2, :feats] = given[0:2, :]
    heads = feats // HEAD_DIM
    small[2:3, :feats] = jnp.concatenate(
        [jnp.broadcast_to(given[2:3, i : i + 1], (1, HEAD_DIM)) for i in range(heads)], axis=1
    )
    other, parity = 1 - lax.axis_index("hid") // 2, lax.axis_index("rows") & 1
    out_half[...] = w_out[at(parity, out_half.shape[0]), :]
    back_half[...] = w_back[:, at(2 * other + parity, back_half.shape[1])]


def fill_mask(bounds, mask):
    toks = mask.shape[0]
    for j in range(toks // WIDE):
        chunk = slice(j * WIDE, (j + 1) * WIDE)
        position = lax.broadcasted_iota(jnp.int32, (toks, WIDE), 0)
        same = (position >= bounds[0:1, chunk]) & (position < bounds[1:2, chunk])
        mask[:, chunk] = jnp.where(same, 0.0, masked_score)


def attn_forward(
    bounds, small, x0, x1, x2, x3, w_qkv,
    x_all, qkv, logsum, mine, send_core, send_x, x_block, gated, mask,
):
    me = lax.axis_index("hid")
    feats, toks = x0.shape
    block = toks // 4
    for k, piece in enumerate((x0, x1, x2, x3)):
        x_all[at(me ^ k, feats), :] = piece[...]
    x_block[...] = x_all[:, at(me, block)]
    cols = jnp.transpose(small[...])
    for c in range(3):
        rows = dot(w_qkv[c], x_all[...])
        if c != 1:
            rows = rows + cols[:feats, c // 2 : c // 2 + 1]
        rows = rows.astype(bf16)
        if c == 0:
            rows = rows * jnp.asarray(HEAD_DIM ** (-0.5), bf16)
        qkv[c] = rows
    fill_mask(bounds, mask)
    heads = feats // HEAD_DIM
    for head in range(heads):
        span = slice(head * HEAD_DIM, (head + 1) * HEAD_DIM)
        keys = jnp.transpose(qkv[1, span, :])
        values = qkv[2, span, :]
        for j in range(4 * block // WIDE):
            chunk = slice(j * WIDE, (j + 1) * WIDE)
            scores = dot(keys, qkv[0, span, chunk])
            scores = scores + mask[:, chunk]
            peak = jnp.max(scores, axis=0, keepdims=True)
            expo = jnp.exp(scores - peak)
            total = jnp.sum(expo, axis=0, keepdims=True)
            probs = (expo * (1.0 / total)).astype(bf16)
            logsum[head : head + 1, chunk] = peak + jnp.log(total)
            gated[span, chunk] = (dot(values, probs) * cols[span, 2:3]).astype(bf16)
    mine[...] = gated[:, at(me, block)]
    send_x[:feats, :] = gated[:, at(me ^ 2, block)]
    send_x[feats:, :] = gated[:, at(me ^ 3, block)]
    send_core[...] = gated[:, at(me ^ 1, block)]


def attn_backward(
    bounds, qkv, logsum, u0, u1, u2, u3, grads, head_sums, bias_sums, up, mask
):
    me = lax.axis_index("hid")
    feats, block = u0.shape
    pieces = (u0, u1.at[:feats, :], u2.at[:feats, :], u3.at[feats : 2 * feats, :])
    for k, piece in enumerate(pieces):
        up[:, at(me ^ k, block)] = piece[...]
    fill_mask(bounds, mask)
    heads = feats // HEAD_DIM
    head_sums[...] = jnp.zeros_like(head_sums)
    for head in range(heads):
        span = slice(head * HEAD_DIM, (head + 1) * HEAD_DIM)
        queries, keys_t, values_t = (qkv[c, span, :] for c in range(3))
        keys = jnp.transpose(keys_t)
        values = jnp.transpose(values_t)
        upstream = up[span, :]
        grad_k = jnp.zeros((HEAD_DIM, 4 * block), f32)
        grad_v = jnp.zeros((HEAD_DIM, 4 * block), f32)
        inner_sum = jnp.zeros((1, WIDE), f32)
        for j in range(4 * block // WIDE):
            chunk = slice(j * WIDE, (j + 1) * WIDE)
            scores = dot(keys, queries[:, chunk])
            scores = scores + mask[:, chunk]
            probs = jnp.exp(scores - logsum[head : head + 1, chunk])
            grad_p = dot(values, upstream[:, chunk])
            weighted = probs * grad_p
            inner = jnp.sum(weighted, axis=0, keepdims=True)
            inner_sum = inner_sum + inner
            grad_s = (weighted - probs * inner).astype(bf16)
            grad_v = grad_v + dot_nt(upstream[:, chunk], probs.astype(bf16))
            grad_k = grad_k + dot_nt(queries[:, chunk], grad_s)
            grads[span, chunk] = (dot(keys_t, grad_s) * HEAD_DIM ** (-0.5)).astype(bf16)
        for c, grad in ((1, grad_k), (2, grad_v)):
            rows = slice(c * feats + head * HEAD_DIM, c * feats + (head + 1) * HEAD_DIM)
            grads[rows, :] = grad.astype(bf16)
        head_sums[head : head + 1, :] = sum(
            inner_sum[:, k * block : (k + 1) * block] for k in range(WIDE // block)
        )
    ones = jnp.ones((8, 4 * block), bf16)
    bias_sums[...] = dot_nt(ones, grads[...])


def all_sums(sums, u1, u2, u3, ig_mine, p_core, bin_sum, head_sums, bias_sums, vec):
    blocks = sums.shape[1] // 128
    feats = (u2.shape[0] - 16 * blocks) // 2
    total = sums[...] + get_sums(u1, feats, 8, blocks)
    vec[0:8, :] = (total + get_sums(u2, 2 * feats, 8, blocks)) + get_sums(u3, 2 * feats, 8, blocks)
    vec[8:, :] = jnp.zeros((vec.shape[0] - 8, vec.shape[1]), f32)
    pair = p_core[p_core.shape[0] - 16 :, :].astype(f32)
    vec[8:9, :] = ig_mine[0:1, :] + (pair[0:1, :] + pair[8:9, :])
    vec[9:10, :] = bin_sum[0:1, :]
    width = bias_sums.shape[1]
    vec[10:11, :width] = bias_sums[0:1, :]
    vec[11:12, :8] = jnp.sum(jnp.transpose(head_sums[...]), axis=0, keepdims=True)


def pair_value(pair):
    n = pair.shape[0] // 2
    return pair[:n, :].astype(f32) + pair[n:, :].astype(f32)


def qk_weight_grad(
    grads, x_all, sums, u1, u2, u3, ig_mine, p_core, bin_sum, head_sums, bias_sums,
    keep, send, pair, full, vec,
):
    parity = lax.axis_index("rows") & 1
    n = keep.shape[0]
    full[...] = dot_nt(grads[: 2 * n, :], x_all[...])
    all_sums(sums, u1, u2, u3, ig_mine, p_core, bin_sum, head_sums, bias_sums, vec)
    send[:n, :] = full[at(parity ^ 1, n), :].astype(bf16)
    send[n:, :] = high_low(vec[...])
    pair[...] = high_low(vec[...])
    keep[...] = full[at(parity, n), :]


def vo_weight_grad(grads, x_all, wo_mine, wo_core, wo_far, keep, send, full):
    parity = lax.axis_index("rows") & 1
    n = keep.shape[0]
    full[:n, :] = dot_nt(grads[2 * n :, :], x_all[...])
    full[n:, :] = wo_mine[...] + wo_core[:n, :].astype(f32) + wo_far[...].astype(f32)
    send[...] = full[at(parity ^ 1, n), :].astype(bf16)
    keep[...] = full[at(parity, n), :]


def add_low(mine, other, total):
    total[...] = (mine[...].astype(f32) + other[...].astype(f32)).astype(total.dtype)


def add_second(mine, other, total):
    n = mine.shape[0]
    total[...] = (mine[...] + other[n:, :].astype(f32)).astype(total.dtype)


def tokens_step(mine, res_x, recv, send):
    n, toks = mine.shape
    block = res_x.shape[1]
    send[:, :toks] = (mine[...] + recv[n:, :toks].astype(f32)).astype(bf16)
    send[:, toks : toks + block] = res_x[...]
    send[:, toks + block :] = recv[n:, toks:]


def tokens_outputs(mine, res_mine, from_core, from_x, grad, output):
    me = lax.axis_index("hid")
    n, toks = mine.shape
    block = res_mine.shape[1]
    both = from_core[:n, :toks].astype(f32) + from_x[:, :toks].astype(f32)
    grad[...] = (mine[...] + both).astype(bf16)
    output[:, at(me, block)] = res_mine[...]
    output[:, at(me ^ 1, block)] = from_core[:n, toks:]
    output[:, at(me ^ 2, block)] = from_x[:, toks : toks + block]
    output[:, at(me ^ 3, block)] = from_x[:, toks + block :]


def qkv_input_grad(grads, w_qkv, dres, res_send, mine, mine_x, send, full):
    me = lax.axis_index("hid")
    feats = mine.shape[0]
    block = dres.shape[0]
    total = None
    for c in range(3):
        part = dot(jnp.transpose(w_qkv[c]), grads[c * feats : (c + 1) * feats, :])
        total = part if total is None else total + part
    full[...] = total
    full[:, at(me, block)] += jnp.transpose(dres[...])
    toks = full.shape[1]
    send[:feats, :toks] = full[at(me ^ 1, feats), :].astype(bf16)
    send[feats:, :toks] = full[at(me ^ 3, feats), :].astype(bf16)
    send[:, toks:] = res_send[...]
    mine[...] = full[at(me, feats), :]
    mine_x[...] = full[at(me ^ 2, feats), :]


def place_rows(own, core_rows, xa, xb, fa, fb, whole):
    me, parity = lax.axis_index("hid"), lax.axis_index("rows") & 1
    n = own.shape[0]
    half = n // 2
    whole[at(me, n), :] = own[...]
    whole[at(me ^ 1, n), :] = core_rows[...]
    for owner, first, second in ((me ^ 2, xa, xb), (me ^ 3, fa, fb)):
        whole[at(2 * owner + parity, half), :] = first[...]
        whole[at(2 * owner + (parity ^ 1), half), :] = second[...]


def row_norm(values):
    mean = jnp.mean(values, axis=1, keepdims=True)
    centered = values - mean
    spread = jnp.mean(centered * centered, axis=1, keepdims=True)
    inv = lax.rsqrt(spread + norm_eps)
    return centered * inv, inv


def attn_out(
    g0, g1, g2, g3, x_block, vecs, wo, cotangent,
    normed, send, hat, inv_out, pre, gated_rows, heads_all,
):
    me = lax.axis_index("hid")
    feats = g0.shape[0]
    for k, piece in enumerate((g0, g1.at[:feats, :], g2.at[:feats, :], g3.at[feats : 2 * feats, :])):
        heads_all[at(me ^ k, feats), :] = piece[...]
    gated = jnp.transpose(heads_all[...])
    gated_rows[...] = gated
    tokens = jnp.transpose(x_block[...].astype(f32))
    attn = dot_nt(gated, wo[...]) + vecs[0:1, :]
    pre[...] = attn
    n = normed.shape[0]
    resid = tokens + attn * vecs[8:9, :]
    x_hat, inv = row_norm(resid)
    value = x_hat * vecs[1:2, :] + vecs[2:3, :]
    send[:n, :] = value.astype(bf16)
    rows = feats // 3
    for k in range(3):
        piece = cotangent[k * rows : (k + 1) * rows, at(1 - me // 2, 2 * n)]
        send[n:, k * 2 * n : (k + 1) * 2 * n] = piece
    normed[...] = value
    hat[...] = x_hat
    inv_out[...] = jnp.broadcast_to(inv, inv_out.shape)


def high_low(values):
    high = values.astype(bf16).astype(f32)
    return jnp.concatenate([high, values - high], axis=0).astype(bf16)


def put_sums(sums, ref, start):
    pairs = high_low(sums)
    count = pairs.shape[0]
    for t in range(sums.shape[1] // 128):
        ref[start + t * count : start + (t + 1) * count, :] = pairs[:, t * 128 : (t + 1) * 128]


def get_sums(ref, start, count, blocks):
    parts = []
    for t in range(blocks):
        pair = ref[start + 2 * count * t : start + 2 * count * (t + 1), :].astype(f32)
        parts.append(pair[:count, :] + pair[count:, :])
    return jnp.concatenate(parts, axis=1)


def attn_out_back(
    part, recv, dres2, hat, inv, pre, vecs, wo, sums2,
    dres, grad_attn, sums, up_mine, up_core, up_x, ups,
):
    me = lax.axis_index("hid")
    feats = up_mine.shape[0]
    grad = part[...] + recv[...].astype(f32) + dres2[...]
    x_hat = hat[...]
    scaled = grad * vecs[1:2, :]
    mean_plain = jnp.mean(scaled, axis=1, keepdims=True)
    mean_along = jnp.mean(scaled * x_hat, axis=1, keepdims=True)
    grad_resid = inv[:, 0:1] * (scaled - mean_plain - x_hat * mean_along)
    dres[...] = grad_resid
    low = (grad_resid * vecs[8:9, :]).astype(bf16)
    grad_attn[...] = low
    grad_gated = dot(low, wo[...])
    upstream = (grad_gated * vecs[7:8, :]).astype(bf16)
    ups[...] = jnp.transpose(upstream)
    up_mine[...] = ups[at(me, feats), :]
    up_core[:feats, :] = ups[at(me ^ 1, feats), :]
    up_x[:feats, :] = ups[at(me ^ 2, feats), :]
    up_x[feats : 2 * feats, :] = ups[at(me ^ 3, feats), :]
    sums[0:1, :] = jnp.sum(grad * x_hat, axis=0, keepdims=True)
    sums[1:2, :] = jnp.sum(grad, axis=0, keepdims=True)
    sums[2:3, :] = jnp.sum(low.astype(f32), axis=0, keepdims=True)
    sums[3:4, :] = jnp.sum(grad_resid * pre[...], axis=0, keepdims=True)
    sums[4:8, :] = sums2[...]
    for ref, start in ((up_core, feats), (up_x, 2 * feats)):
        put_sums(sums[...], ref, start)


def out_weight_grad(grad_attn, gated_rows, mine, mine_x, send, full):
    me = lax.axis_index("hid")
    feats = mine.shape[0]
    full[...] = dot_tn(grad_attn[...], gated_rows[...])
    send[:feats, :] = full[at(me ^ 1, feats), :].astype(bf16)
    send[feats:, :] = full[at(me ^ 3, feats), :].astype(bf16)
    mine[...] = full[at(me, feats), :]
    mine_x[...] = full[at(me ^ 2, feats), :]


def place_units(wi_own, wi_core, own, core_rows, xa, xb, fa, fb, wi, wb):
    me, core, chip, parity = lax.axis_index("hid"), lax.axis_index("hid") & 1, lax.axis_index("hid") // 2, lax.axis_index("rows") & 1
    n, half = xa.shape
    units = wi_own.shape[1]
    wi[:, at(core, units)] = wi_own[...]
    wi[:, at(core ^ 1, units)] = wi_core[...]
    wb[at(me, n), :] = own[:, at(chip, 2 * half)]
    wb[at(me ^ 1, n), :] = core_rows[:, at(chip, 2 * half)]
    for owner, first, second in ((me ^ 2, xa, xb), (me ^ 3, fa, fb)):
        wb[at(owner, n), at(parity, half)] = first[...]
        wb[at(owner, n), at(parity ^ 1, half)] = second[...]


def ffn_forward(
    rows, unit_rows, wi, wb, core_far, act, slope, inter_mine, part, core_pair, inter
):
    n = part.shape[0]
    core_pair[n:, :] = core_far[...]
    ffn_units(rows[: part.shape[0], :], unit_rows, wi, act, slope, inter_mine, core_pair.at[:n, :], inter)
    part[...] = dot_nt(inter[...], wb[...])


def ffn_forward_far(
    rows, unit_rows, wi, wb, act, slope, inter_mine, inter_core, part, inter
):
    ffn_units(rows[: part.shape[0], :], unit_rows, wi, act, slope, inter_mine, inter_core, inter)
    part[...] = dot_nt(inter[...], wb[...]).astype(part.dtype)


def ffn_units(rows, unit_rows, wi, act, slope, inter_mine, inter_core, inter):
    core = lax.axis_index("hid") & 1
    units = wi.shape[1]
    step = 256
    for j in range(units // step):
        cut = slice(j * step, (j + 1) * step)
        u = dot(rows, wi[:, cut]) + unit_rows[0:1, cut]
        cdf = 0.5 * (1.0 + lax.erf(u * 0.7071067811865476))
        value = u * cdf
        act[:, cut] = value
        slope[:, cut] = cdf + u * (jnp.exp(-0.5 * u * u) * 0.3989422804014327)
        inter[:, cut] = (value * unit_rows[1:2, cut]).astype(bf16)
    inter_mine[...] = inter[:, at(core, units // 2)]
    inter_core[...] = inter[:, at(core ^ 1, units // 2)]


def ffn_backward(
    rows, act, slope, unit_rows, wi, wb, gpre_mine, gpre_core, part, sums, gpre,
):
    ffn_units_back(rows, act, slope, unit_rows, wb, gpre_mine, gpre_core, sums, gpre)
    part[...] = dot_nt(gpre[...], wi[...])


def ffn_backward_far(
    rows, act, slope, unit_rows, wi, wb, core_mine, sums_mine,
    gpre_mine, part, sums, core_pair, gpre, all_sums,
):
    core, n = lax.axis_index("hid") & 1, rows.shape[0]
    units = gpre_mine.shape[1]
    core_pair[:n, :] = core_mine[...]
    ffn_units_back(
        rows, act, slope, unit_rows, wb, gpre_mine, core_pair.at[n : 2 * n, :], all_sums, gpre
    )
    part[...] = dot_nt(gpre[...], wi[...]).astype(part.dtype)
    all_sums[...] += sums_mine[...]
    sums[...] = all_sums[:, at(core, units)]
    core_pair[2 * n :, :] = high_low(all_sums[:, at(core ^ 1, units)])


def ffn_units_back(rows, act, slope, unit_rows, wb, gpre_mine, gpre_core, sums, gpre):
    core = lax.axis_index("hid") & 1
    units = wb.shape[1]
    step = 256
    for j in range(units // step):
        cut = slice(j * step, (j + 1) * step)
        ginter = dot(rows[...], wb[:, cut])
        sums[:, cut] = jnp.broadcast_to(
            jnp.sum(ginter * act[:, cut], axis=0, keepdims=True), (8, step)
        )
        gpre[:, cut] = (ginter * unit_rows[1:2, cut] * slope[:, cut]).astype(bf16)
    gpre_mine[...] = gpre[:, at(core, units // 2)]
    gpre_core[...] = gpre[:, at(core ^ 1, units // 2)]


def ffn_weight_grads(
    n0, n1, n2, n3, e0, e1, e_core, p0, p1, p_core, f0, f1, f2, f3,
    back0_keep, back0_send, back1_keep, back1_send, in0_keep, in0_send, in1_keep, in1_send,
    bias_sums, left, right, full,
):
    parity = lax.axis_index("rows") & 1

    def fill(target, pieces):
        start = 0
        for piece in pieces:
            count = piece.shape[0] // 128 * 128
            target[start : start + count, :] = piece[:count, :]
            start += count

    fill(left, (f0, f1, f2, f3))
    fill(right, (e0, e1, e_core))
    full[...] = dot_tn(left[...], right[...])
    owners, parts = 4, 4
    rows = full.shape[0] // (owners * parts)
    for k, (keep, send) in enumerate(((back0_keep, back0_send), (back1_keep, back1_send))):
        for h in range(owners):
            to = slice(h * rows, (h + 1) * rows)
            send[to, :] = full[at(h * parts + 2 * k + (parity ^ 1), rows), :].astype(bf16)
            keep[to, :] = full[at(h * parts + 2 * k + parity, rows), :]
    fill(left, (n0, n1, n2, n3))
    fill(right, (p0, p1, p_core))
    full[...] = dot_tn(left[...], right[...])
    rows = full.shape[0] // 4
    for k, (keep, send) in enumerate(((in0_keep, in0_send), (in1_keep, in1_send))):
        send[...] = full[at(2 * k + (parity ^ 1), rows), :].astype(bf16)
        keep[...] = full[at(2 * k + parity, rows), :]
    bias_sums[...] = jnp.broadcast_to(
        jnp.sum(right[...].astype(f32), axis=0, keepdims=True), bias_sums.shape
    )


def second_norm(
    part, recv, normed, cot0, cot1, n_x, n_far, vecs,
    grad_low, dres, sums, out_mine, out_x, out_send, cots, outs,
):
    me = lax.axis_index("hid")
    feats = cot0.shape[0]
    block = part.shape[0]
    core = me & 1
    cots[at(me, feats), :] = cot0[:, at(me, block)]
    cots[at(me ^ 1, feats), :] = cot1[:, at(me, block)]
    rows = feats // 3
    for owner, pieces in ((me ^ 2, n_x), (me ^ 3, n_far)):
        for k in range(3):
            to = pl.ds(pl.multiple_of(owner * feats + k * rows, rows), rows)
            cots[to, :] = pieces[block:, at(2 * k + core, block)]
    ffn = part[...] + recv[...].astype(f32) + vecs[4:5, :]
    resid = normed[...] + ffn * vecs[9:10, :]
    x_hat, inv = row_norm(resid)
    grad_out = jnp.transpose(cots[...].astype(f32))
    scaled = grad_out * vecs[5:6, :]
    mean_plain = jnp.mean(scaled, axis=1, keepdims=True)
    mean_along = jnp.mean(scaled * x_hat, axis=1, keepdims=True)
    grad_resid = inv * (scaled - mean_plain - x_hat * mean_along)
    low = (grad_resid * vecs[9:10, :]).astype(bf16)
    grad_low[...] = low
    dres[...] = grad_resid
    value = x_hat * vecs[5:6, :] + vecs[6:7, :]
    outs[...] = jnp.transpose(value).astype(bf16)
    out_mine[...] = outs[at(me, feats), :]
    out_x[...] = outs[at(me ^ 2, feats), :]
    out_send[:feats, :] = outs[at(me ^ 1, feats), :]
    out_send[feats:, :] = outs[at(me ^ 3, feats), :]
    sums[0:1, :] = jnp.sum(grad_out * x_hat, axis=0, keepdims=True)
    sums[1:2, :] = jnp.sum(grad_out, axis=0, keepdims=True)
    sums[2:3, :] = jnp.sum(low.astype(f32), axis=0, keepdims=True)
    sums[3:4, :] = jnp.sum(grad_resid * ffn, axis=0, keepdims=True)


VECTORS = 16


def add_vectors(
    head_gate, branch, b_out, gain, bias, hidden_gate, hidden_mask, b_back, ctx_core, ctx_x,
    send_core, send_x, columns, rows,
):
    feats = b_out.shape[0]

    def row(ref):
        return ref[...].reshape(1, ref.shape[0])

    cols = row(hidden_gate) * row(hidden_mask).astype(f32)
    rows[...] = jnp.zeros_like(rows)
    rows[0:1, :feats] = row(b_out)
    rows[1:2, :feats] = gain[0:1, :]
    rows[2:3, :feats] = bias[0:1, :]
    rows[3:4, :feats] = cols
    rows[4:5, :feats] = row(b_back)
    rows[5:6, :feats] = gain[1:2, :]
    rows[6:7, :feats] = bias[1:2, :]
    rows[7:8, :feats] = jnp.concatenate(
        [jnp.full((1, HEAD_DIM), head_gate[i], f32) for i in range(feats // HEAD_DIM)], axis=1
    )
    rows[8:9, :feats] = branch[0] * cols
    rows[9:10, :feats] = branch[1] * cols
    rest = jnp.transpose(rows[...])[:feats, :]
    columns[...] = jnp.zeros_like(columns)
    for k in range(3):
        low = rest.astype(bf16)
        columns[:, k * VECTORS : (k + 1) * VECTORS] = low
        rest = rest - low.astype(f32)
    for send, ctx in ((send_core, ctx_core), (send_x, ctx_x)):
        n = ctx.shape[0]
        send[:n, :] = ctx[...]
        send[n:, :] = columns[...]


def place_vectors(p0, p1, p2, p3, b_in, gate, b_in_core, gate_core, vecs, unit_rows, cols):
    me, core = lax.axis_index("hid"), lax.axis_index("hid") & 1
    feats = cols.shape[0] // 4
    units = b_in.shape[0]
    for k, piece in enumerate((p0, p1.at[feats:, :], p2.at[2 * feats :, :], p3.at[2 * feats :, :])):
        parts = piece[...].astype(f32)
        cols[at(me ^ k, feats), :] = (
            parts[:, :VECTORS] + parts[:, VECTORS : 2 * VECTORS]
        ) + parts[:, 2 * VECTORS : 3 * VECTORS]
    vecs[...] = jnp.transpose(cols[...])
    for k, (one, two) in enumerate(((b_in, gate), (b_in_core, gate_core))):
        unit_rows[0:1, at(core ^ k, units)] = one[...].reshape(1, units)
        unit_rows[1:2, at(core ^ k, units)] = two[...].reshape(1, units)


def vector_outputs(
    branch, head_gate, vec, vecs, hidden_mask,
    g_qv, g_bout, g_bin, g_bback, g_gain, g_bias, g_head, g_inter, g_branch, g_hidden, cols,
):
    me = lax.axis_index("hid")
    feats = g_bout.shape[0]
    cols[...] = jnp.transpose(vec[0:8, :])
    own = jnp.transpose(cols[at(me, feats), :])
    g_gain[0:1, :] = own[0:1, :]
    g_gain[1:2, :] = own[4:5, :]
    g_bias[0:1, :] = own[1:2, :]
    g_bias[1:2, :] = own[5:6, :]
    g_bout[...] = own[2, :]
    g_bback[...] = own[6, :]
    mask = hidden_mask[...].astype(f32)
    g_hidden[...] = (branch[0] * own[3, :] + branch[1] * own[7, :]) * mask
    g_inter[...] = vec[8, :]
    g_bin[...] = vec[9, :]
    g_qv[0:1, :] = vec[10:11, :feats]
    rolled = vec[10:11, 2 * feats : 3 * feats]
    g_qv[1:2, :] = rolled
    lane = lax.broadcasted_iota(jnp.int32, (1, 128), 1)
    gates = jnp.ones((1, 128), f32)
    for i in range(feats // HEAD_DIM):
        gates = jnp.where(lane == i, head_gate[i], gates)
    g_head[...] = (vec[11:12, :128] / gates)[0, : feats // HEAD_DIM]
    part0 = jnp.sum(vec[3:4, :] * vecs[3:4, :], axis=1, keepdims=True)
    part1 = jnp.sum(vec[7:8, :] * vecs[3:4, :], axis=1, keepdims=True)
    both = jnp.where(lane == 0, part0, part1)
    g_branch[...] = both[0, :2]


def row_place():
    row = lax.axis_index("rows")
    return row & 1, (row >> 1) & 3


def first_add(keep, recv, total, send):
    total[...] = keep[...] + recv[...].astype(f32)
    send[...] = total[...].astype(bf16)


def first_add_pair(keep, pair, recv, total, send):
    n = keep.shape[0]
    total[...] = keep[...] + recv[:n, :].astype(f32)
    send[:n, :] = total[...].astype(bf16)
    send[n:, :] = high_low(pair_value(pair) + pair_value(recv[n:, :]))


def second_add(keep, recv, send):
    send[...] = (keep[...] + recv[...].astype(f32)).astype(bf16)


def second_add_pair(keep, mine, recv, send):
    n = keep.shape[0]
    send[:n, :] = (keep[...] + recv[:n, :].astype(f32)).astype(bf16)
    send[n:, :] = high_low(pair_value(mine[n:, :]) + pair_value(recv[n:, :]))


def third_add(mine, recv, total):
    total[...] = (mine[...].astype(f32) + recv[...].astype(f32)).astype(bf16)


def third_add_pair(mine, recv, total):
    n = mine.shape[0] - 32
    total[:n, :] = (mine[:n, :].astype(f32) + recv[:n, :].astype(f32)).astype(bf16)
    total[n:, :] = high_low(pair_value(mine[n:, :]) + pair_value(recv[n:, :]))


def choose(mine, recv, total):
    z = row_place()[1]
    outer = (z == 0) | (z == 3)
    total[...] = jnp.where(outer, recv[...], mine[...])


def choose_pair(mine, recv, total, vec):
    n = total.shape[0]
    z = row_place()[1]
    outer = (z == 0) | (z == 3)
    total[...] = jnp.where(outer, recv[:n, :], mine[:n, :])
    vec[...] = jnp.where(outer, pair_value(recv[n:, :]), pair_value(mine[n:, :]))


def split_owners(mine, recv, own, own_x, send):
    me = lax.axis_index("hid")
    n = own.shape[0]

    def rows(k):
        total = mine[at(me ^ k, n), :].astype(f32) + recv[at(me ^ k, n), :].astype(f32)
        return total.astype(bf16)

    own[...] = rows(0)
    own_x[...] = rows(2)
    send[:n, :] = rows(1)
    send[n:, :] = rows(3)


def join_owners(mine, from_core, from_x, chunk):
    me, n = lax.axis_index("hid"), mine.shape[0]
    chunk[at(me, n), :] = mine[...]
    chunk[at(me ^ 1, n), :] = from_core[:n, :]
    chunk[at(me ^ 2, n), :] = from_x[:n, :]
    chunk[at(me ^ 3, n), :] = from_x[n:, :]


def in_gradient(mine0, other0, mine1, other1, grad):
    y = row_place()[0]
    n = mine0.shape[0]
    for k, (mine, other) in enumerate(((mine0, other0), (mine1, other1))):
        grad[at(2 * k + y, n), :] = mine[...].astype(f32)
        grad[at(2 * k + (y ^ 1), n), :] = other[...].astype(f32)


def back_gradient(mine0, other0, mine1, other1, grad):
    y = row_place()[0]
    units = mine0.shape[1]
    n = mine0.shape[0] // 4
    for k, (mine, other) in enumerate(((mine0, other0), (mine1, other1))):
        for side, half in ((y, mine), (y ^ 1, other)):
            for owner in range(4):
                block = half[owner * n : (owner + 1) * n, :].astype(f32)
                grad[at(2 * k + side, n), owner * units : (owner + 1) * units] = block


def attn_gradients(qk_mine, qk_other, vo_mine, vo_other, grad_qkv, grad_out):
    y = row_place()[0]
    n = qk_mine.shape[0]
    grad_qkv[at(y, n), :] = qk_mine[...].astype(f32)
    grad_qkv[at(y ^ 1, n), :] = qk_other[...].astype(f32)
    mine, other = vo_mine[...].astype(f32), vo_other[...].astype(f32)
    grad_qkv[2 * n :, :] = jnp.where(y == 0, mine, other)
    grad_out[...] = jnp.where(y == 0, other, mine)


def second_half(mine, recv, both):
    n = mine.shape[0]
    both[:n, :] = mine[...]
    both[n:, :] = recv[n:, :]


EARLY_TURNS = "313"
TURNS = "413vq2413241v3241q122v13gq24vq124vg2qegvq"
FIRST = ("in0", "back0")


def along(block, way="y"):
    pairs = []
    for i in range(lax.axis_size("rows")):
        z = (i >> 1) & 3
        step = {
            "y": 1 - 2 * (i & 1),
            "in": {0: 2, 3: -2}.get(z),
            "mid": {1: 2, 2: -2}.get(z),
            "out": {1: -2, 2: 2}.get(z),
        }[way]
        if step is not None:
            pairs.append((i, i + step))
    return lax.ppermute(block, "rows", pairs)


class Turns:
    def __init__(self):
        self.last = ()

    def held(self, block):
        return after(block, *self.last) if self.last else block

    def mark(self, *blocks):
        self.last = blocks


def far_rows_sum(chunk):
    count = lax.axis_size("rows")
    if count == 8:
        return chunk
    groups = [[i + 8 * j for j in range(count // 8)] for i in range(8)]
    return lax.psum(chunk.astype(f32), "rows", axis_index_groups=groups).astype(chunk.dtype)


def shards(
    tokens, w_qkv, b_qv, w_out, b_out, w_in, b_in, w_back, b_back, norm_gain, norm_bias,
    head_gate, inter_gate, branch_gate, hidden_gate, hidden_mask, doc_lengths, cotangent,
):
    feats, toks = tokens.shape
    width = 4 * feats
    units = w_in.shape[1]
    block = toks // 4
    given = jnp.concatenate(
        [
            b_qv,
            jnp.pad(head_gate, (0, feats - head_gate.shape[0]))[None],
            jnp.pad(doc_lengths.astype(f32), ((0, 0), (0, feats - doc_lengths.shape[1]))),
        ],
        0,
    )
    bounds, small, out_half, back_half = local_kernel(
        begin,
        "begin",
        (given, w_out, w_back),
        "VVV",
        [
            sds((8, toks), jnp.int32),
            sds((8, 256), f32),
            sds((feats // 2, width), bf16),
            sds((feats, units), bf16),
        ],
    )
    tokens_x = swap(tokens, "hid", 2)
    tokens_core = swap(tokens, "hid", 1)
    x_own = swap(after(tokens_core, back_half), "hid", 1)
    out_xa = swap(out_half, "hid", 2)
    back_xa = swap(back_half, "hid", 2)
    wi_core = swap(w_in, "hid", 1)
    wo_core = swap(w_out, "hid", 1)
    b_in_core = swap(b_in, "hid", 1)
    gate_core = swap(inter_gate, "hid", 1)
    back_core = swap(w_back, "hid", 1)
    tokens_far = swap(
        after(tokens_x, tokens_core, wi_core, wo_core, back_core, back_half), "hid", 1
    )

    head_block = sds((feats, block), bf16)
    two_blocks = sds((2 * feats, block), bf16)
    x_all, qkv, logsum, g0, g_core, g_x, x_block = local_kernel(
        attn_forward,
        "attn_forward",
        (
            bounds, small, x_own, tokens_core, tokens_x, tokens_far, w_qkv,
        ),
        "V" * 7,
        [
            sds((width, toks), bf16),
            sds((3, feats, toks), bf16),
            sds((8, toks), f32),
            head_block,
            head_block,
            two_blocks,
            sds((width, block), bf16),
        ],
        [pltpu.VMEM((feats, toks), bf16), pltpu.VMEM((toks, toks), f32)],
        micros=5.4,
    )
    cot_core = swap(after(cotangent, x_block), "hid", 1)
    send_core, send_x, columns = local_kernel(
        add_vectors,
        "add_vectors",
        (
            head_gate, branch_gate, after(b_out, x_block), norm_gain, norm_bias, hidden_gate,
            hidden_mask, b_back, g_core, g_x,
        ),
        "SS" + "V" * 8,
        [two_blocks, sds((3 * feats, block), bf16), head_block],
        [pltpu.VMEM((VECTORS, 256), f32)],
    )
    g2 = swap(send_x, "hid", 2)
    g1 = swap(send_core, "hid", 1)
    g3 = swap(after(g2, g1, b_in_core, gate_core), "hid", 1)
    out_xb = swap(after(out_xa, g0), "rows", 1)
    out_fa = swap(after(out_xa, g0), "hid", 1)
    out_fb = swap(out_xb, "hid", 1)
    back_xb = swap(after(back_xa, g1), "rows", 1)
    back_fa = swap(after(back_xa, g1), "hid", 1)
    (wo,) = local_kernel(
        place_rows,
        "place_rows",
        (w_out, wo_core, out_xa, out_xb, out_fa, out_fb),
        "VVVVVV",
        [sds((width, width), bf16)],
    )
    vecs, unit_rows = local_kernel(
        place_vectors,
        "place_vectors",
        (columns, g1, g2, g3, b_in, inter_gate, b_in_core, gate_core),
        "V" * 8,
        [sds((VECTORS, width), f32), sds((2, 2 * units), f32)],
        [pltpu.VMEM((width, VECTORS), f32)],
    )

    normed, n_send, hat, inv, attn_pre, gated_rows = local_kernel(
        attn_out,
        "attn_out",
        (g0, g1, g2, g3, x_block, vecs, wo, cotangent),
        "VVVVVVVV",
        [
            sds((block, width), f32),
            sds((block + feats // 3, width), bf16),
            sds((block, width), f32),
            sds((block, 128), f32),
            sds((block, width), f32),
            sds((block, width), bf16),
        ],
        [pltpu.VMEM((width, block), bf16)],
        micros=1.3,
    )

    n_x = swap(n_send, "hid", 2)
    n_core = swap(n_send, "hid", 1)
    back_fb = swap(after(back_xb, n_x), "hid", 1)
    wi, wb = local_kernel(
        place_units,
        "place_units",
        (w_in, wi_core, w_back, back_core, back_xa, back_xb, back_fa, back_fb),
        "V" * 8,
        [sds((width, 2 * units), bf16), sds((width, 2 * units), bf16)],
        micros=0.85,
    )

    act_block = sds((block, 2 * units), f32)
    half_block = sds((block, units), bf16)
    pair_block = sds((2 * block, units), bf16)
    rows_block = sds((block, width), bf16)
    ffn_scratch = [pltpu.VMEM((block, 2 * units), bf16)]
    act_x, slope_x, e1, inter_core, ffn_send = local_kernel(
        ffn_forward_far,
        "ffn_forward_far",
        (n_x, unit_rows, wi, wb),
        "VVVV",
        [act_block, act_block, half_block, half_block, rows_block],
        ffn_scratch,
        micros=1.85,
    )
    ffn_recv = swap(ffn_send, "hid", 2)
    act, slope, e0, ffn_part, e_pair = local_kernel(
        ffn_forward,
        "ffn_forward",
        (after(n_send, ffn_send), unit_rows, wi, wb, inter_core),
        "VVVVV",
        [act_block, act_block, half_block, sds((block, width), f32), pair_block],
        ffn_scratch,
        micros=1.85,
    )
    n_far = swap(after(n_x, ffn_send), "hid", 1)

    out_block = sds((feats, block), bf16)
    gffn, dres2, sums2, res_mine, res_x, res_send = local_kernel(
        second_norm,
        "second_norm",
        (
            after(ffn_part, n_core), ffn_recv, normed, cotangent, cot_core, n_x, n_far, vecs,
        ),
        "V" * 8,
        [
            sds((block, width), bf16),
            sds((block, width), f32),
            sds((4, width), f32),
            out_block,
            out_block,
            sds((2 * feats, block), bf16),
        ],
        [pltpu.VMEM((width, block), bf16), pltpu.VMEM((width, block), bf16)],
        micros=1.2,
    )

    gffn_x = swap(gffn, "hid", 2)
    e_core = swap(after(e_pair, gffn), "hid", 1)
    f2 = swap(gffn, "hid", 1)
    sums_block = sds((8, 2 * units), f32)
    p0, gpre_core, gn_part, ig_sum = local_kernel(
        ffn_backward,
        "ffn_backward",
        (gffn, act, slope, unit_rows, wi, wb),
        "VVVVVV",
        [half_block, half_block, sds((block, width), f32), sums_block],
        ffn_scratch,
        micros=1.85,
    )
    p1, gn_send, ig_mine, p_pair = local_kernel(
        ffn_backward_far,
        "ffn_backward_far",
        (after(gffn_x, f2, e_core), act_x, slope_x, unit_rows, wi, wb, gpre_core, ig_sum),
        "VVVVVVVV",
        [half_block, rows_block, sds((8, units), f32), sds((2 * block + 16, units), bf16)],
        ffn_scratch + [pltpu.VMEM((8, 2 * units), f32)],
        micros=1.85,
    )
    gn_recv = swap(gn_send, "hid", 2)
    f3 = swap(after(gffn_x, gn_send), "hid", 1)
    p_core = swap(p_pair, "hid", 1)
    *pieces, bin_sum = local_kernel(
        ffn_weight_grads,
        "ffn_weight_grads",
        (
            n_send, n_x, n_core, n_far, e0, e1, e_core,
            p0, p1, p_core, gffn, gffn_x, f2, f3,
        ),
        "V" * 14,
        [
            sds((feats, units), f32),
            sds((feats, units), bf16),
            sds((feats, units), f32),
            sds((feats, units), bf16),
            sds((feats, units), f32),
            sds((feats, units), bf16),
            sds((feats, units), f32),
            sds((feats, units), bf16),
            sds((8, units), f32),
        ],
        [
            pltpu.VMEM((toks, width), bf16),
            pltpu.VMEM((toks, units), bf16),
            pltpu.VMEM((width, units), f32),
        ],
        micros=2.5,
    )

    pieces = dict(zip(("back0", "back1", "in0", "in1"), zip(pieces[0::2], pieces[1::2])))
    early = {name: along(after(pieces[name][1], gn_recv)) for name in FIRST}

    sum_rows = 16 * width // 128
    dres1, gattn, sums1, u0, up_core, up_x = local_kernel(
        attn_out_back,
        "attn_out_back",
        (
            after(gn_part, pieces["in1"][1]), gn_recv, dres2, hat, inv, attn_pre,
            vecs, wo, sums2,
        ),
        "V" * 9,
        [
            sds((block, width), f32),
            sds((block, width), bf16),
            sds((8, width), f32),
            head_block,
            sds((feats + sum_rows, block), bf16),
            sds((2 * feats + sum_rows, block), bf16),
        ],
        [pltpu.VMEM((width, block), bf16)],
        micros=1.3,
    )
    u2 = swap(up_x, "hid", 2)
    u1 = swap(up_core, "hid", 1)
    u3 = swap(u2, "hid", 1)

    weight_block = sds((feats, width), f32)
    low_block = sds((feats, width), bf16)
    wo_mine, wo_keep, wo_send = local_kernel(
        out_weight_grad,
        "out_weight_grad",
        (gattn, gated_rows),
        "VV",
        [weight_block, weight_block, sds((2 * feats, width), bf16)],
        [pltpu.VMEM((width, width), f32)],
        micros=1.2,
    )
    wo_grad_core = swap(after(wo_send, u1), "hid", 1)

    turns = Turns()
    results = {}
    whole_block = sds((feats, width), f32)

    def step(body, args, outs, **more):
        outs = local_kernel(
            body, body.__name__, (turns.held(args[0]),) + args[1:], "V" * len(args), outs, **more
        )
        turns.mark(*outs[-1:])
        return outs

    def sum_chain(name, keep, send, recv=None):
        if recv is None:
            recv = along(turns.held(send))
        yield
        keep, send = step(first_add, (keep, recv), [whole_block, low_block])
        recv = along(send, "in")
        yield
        (mine,) = step(second_add, (keep, recv), [low_block])
        recv = along(mine, "mid")
        yield
        if name.startswith("back"):
            part = sds((feats // 4, units), bf16)
            two = sds((feats // 2, units), bf16)
            mine, mine_x, send = step(split_owners, (mine, recv), [part, part, two])
            from_core = swap(send, "hid", 1)
            yield
            (send,) = step(second_half, (mine_x, from_core), [two])
            from_x = swap(send, "hid", 2)
            yield
            (mine,) = step(join_owners, (mine, from_core, from_x), [low_block])
        else:
            (mine,) = step(third_add, (mine, recv), [low_block])
        recv = along(mine, "out")
        yield
        (mine,) = step(choose, (mine, recv), [low_block])
        yield from last_part(name, mine)

    def last_part(name, mine):
        mine = far_rows_sum(mine)
        other = along(mine)
        yield
        results[name] = (mine, other)
        if name in ("in0", "in1") and "in0" in results and "in1" in results:
            (results["w_in"],) = step(
                in_gradient,
                results["in0"] + results["in1"],
                [sds((width, units), f32)],
                micros=2.1,
            )
        if name in ("back0", "back1") and "back0" in results and "back1" in results:
            (results["w_back"],) = step(
                back_gradient,
                results["back0"] + results["back1"],
                [sds((feats, 4 * units), f32)],
                micros=2.1,
            )
        if name in ("qk", "vo") and "qk" in results and "vo" in results:
            results["w_qkv"], results["w_out"] = step(
                attn_gradients,
                results["qk"] + results["vo"],
                [sds((3 * feats, width), f32), weight_block],
                micros=2.1,
            )

    chains = {
        key: sum_chain(name, *pieces[name], early.get(name))
        for key, name in zip("1234", ("back0", "back1", "in0", "in1"))
    }
    turns.mark(u1)
    for turn in EARLY_TURNS:
        next(chains[turn], None)
    grads, head_sums, bias_sums = local_kernel(
        attn_backward,
        "attn_backward",
        (bounds, turns.held(qkv), logsum, u0, u1, u2, u3),
        "V" * 7,
        [
            sds((3 * feats, toks), bf16),
            sds((8, block), f32),
            sds((8, 3 * feats), f32),
        ],
        [pltpu.VMEM((feats, toks), bf16), pltpu.VMEM((toks, toks), f32)],
        micros=5.0,
    )
    (wo_low,) = local_kernel(add_second, "wo_low", (wo_keep, wo_grad_core), "VV", [low_block])
    wo_far = swap(after(wo_low, u3), "hid", 2)

    gx_block = sds((feats, toks), f32)
    gx_low = sds((feats, toks), bf16)

    def qk_chain():
        with_pair = sds((feats + 32, width), bf16)
        keep, send, pair = local_kernel(
            qk_weight_grad,
            "qk_weight_grad",
            (
                turns.held(grads), x_all, sums1, u1, u2, u3, ig_mine, p_core, bin_sum,
                head_sums, bias_sums,
            ),
            "V" * 11,
            [weight_block, with_pair, sds((32, width), bf16)],
            [pltpu.VMEM((2 * feats, width), f32), pltpu.VMEM((16, width), f32)],
            micros=1.2,
        )
        turns.mark(send)
        recv = along(send)
        yield
        keep, send = step(first_add_pair, (keep, pair, recv), [weight_block, with_pair])
        recv = along(send, "in")
        yield
        (mine,) = step(second_add_pair, (keep, send, recv), [with_pair])
        recv = along(mine, "mid")
        yield
        (mine,) = step(third_add_pair, (mine, recv), [with_pair])
        recv = along(mine, "out")
        yield
        mine, results["sums"] = step(
            choose_pair, (mine, recv), [low_block, sds((16, width), f32)]
        )
        yield from last_part("qk", mine)

    def vo_chain():
        keep, send = local_kernel(
            vo_weight_grad,
            "vo_weight_grad",
            (turns.held(grads), x_all, wo_mine, wo_grad_core, wo_far),
            "VVVVV",
            [weight_block, low_block],
            [pltpu.VMEM((2 * feats, width), f32)],
            micros=1.1,
        )
        turns.mark(send)
        yield from sum_chain("vo", keep, send, along(send))

    def tokens_chain():
        mine, mine_x, send = local_kernel(
            qkv_input_grad,
            "qkv_input_grad",
            (turns.held(grads), w_qkv, dres1, res_send),
            "VVVV",
            [gx_block, gx_block, sds((2 * feats, toks + block), bf16)],
            [pltpu.VMEM((width, toks), f32)],
            micros=1.5,
        )
        turns.mark(send)
        from_core = swap(send, "hid", 1)
        yield
        (send,) = local_kernel(
            tokens_step,
            "tokens_step",
            (turns.held(mine_x), res_x, from_core),
            "VVV",
            [sds((feats, toks + 2 * block), bf16)],
        )
        turns.mark(send)
        from_x = swap(send, "hid", 2)
        yield
        results["tokens"], results["output"] = local_kernel(
            tokens_outputs,
            "tokens_outputs",
            (turns.held(mine), res_mine, from_core, from_x),
            "VVVV",
            [gx_low, gx_low],
            micros=1.2,
        )
        turns.mark(results["tokens"])

    def vector_chain():
        results["vectors"] = local_kernel(
            vector_outputs,
            "vector_outputs",
            (branch_gate, head_gate, far_rows_sum(turns.held(results["sums"])), vecs, hidden_mask),
            "SSVVV",
            [
                sds((2, feats), f32),
                sds((feats,), f32),
                sds((units,), f32),
                sds((feats,), f32),
                sds((2, feats), f32),
                sds((2, feats), f32),
                sds((feats // HEAD_DIM,), f32),
                sds((units,), f32),
                sds((2,), f32),
                sds((feats,), f32),
            ],
            [pltpu.VMEM((width, 8), f32)],
            micros=1.4,
        )
        turns.mark(results["vectors"][0])
        yield

    chains.update(q=qk_chain(), v=vo_chain(), g=tokens_chain(), e=vector_chain())
    turns.mark(grads)
    for turn in TURNS:
        next(chains[turn], None)
    (
        grad_b_qv, grad_b_out, grad_b_in, grad_b_back, grad_norm_gain, grad_norm_bias,
        grad_head_gate, grad_inter_gate, grad_branch_gate, grad_hidden_gate,
    ) = results["vectors"]
    output, grad_tokens = results["output"], results["tokens"]
    grad_w_qkv = results["w_qkv"].reshape(3, feats, width)
    grad_w_out, grad_w_in, grad_w_back = results["w_out"], results["w_in"], results["w_back"]
    return (
        output,
        grad_tokens,
        grad_w_qkv,
        grad_b_qv,
        grad_w_out,
        grad_b_out,
        grad_w_in,
        grad_b_in,
        grad_w_back,
        grad_b_back,
        grad_norm_gain,
        grad_norm_bias,
        grad_head_gate,
        grad_inter_gate,
        grad_branch_gate,
        grad_hidden_gate,
    )


def solution(mesh):
    return jax.shard_map(
        shards,
        mesh=mesh,
        in_specs=(
            P("hid", "rows"),
            P(None, "hid", None),
            P(None, "hid"),
            P("hid", None),
            P("hid"),
            P(None, "hid"),
            P("hid"),
            P("hid", None),
            P("hid"),
            P(None, "hid"),
            P(None, "hid"),
            P("hid"),
            P("hid"),
            P(),
            P("hid"),
            P("hid"),
            P("rows", None),
            P("hid", "rows"),
        ),
        out_specs=(
            P("hid", "rows"),
            P("hid", "rows"),
            P(None, "hid", None),
            P(None, "hid"),
            P("hid", None),
            P("hid"),
            P(None, "hid"),
            P("hid"),
            P("hid", None),
            P("hid"),
            P(None, "hid"),
            P(None, "hid"),
            P("hid"),
            P("hid"),
            P(),
            P("hid"),
        ),
        check_vma=False,
    )
```
